32 devices in a mesh: ctx: 4 (over y, x), fsdp: 8 (over z, core).
Axes of the slice: x: 2, y: 2, z: 4, core: 2. Of those that a mesh axis runs over, the one named last changes fastest.
Arguments:
- tokens: bfloat16 [8192, 2048], P(('ctx', 'fsdp')), may hold values from -6 to 6
- routes: int32 [8192, 4], P(('ctx', 'fsdp')), may hold values from 0 to 7, all different within a row; in each aligned block of 256 rows (0 to 255, 256 to 511, ...) at most 176 rows name the same one
- block_ids: int32 [8], replicated, may hold values from 0 to 7, as said below
- attn_gain: bfloat16 [2048], P('fsdp'), may hold values from 0.099609375 to 1.8984375
- w_attn_in: bfloat16 [2048, 6144], P('fsdp'), may hold values from -0.125 to 0.125
- b_qkv: bfloat16 [6144], P('fsdp'), may hold values from -2 to 2
- w_attn_out: bfloat16 [2048, 2048], P('fsdp'), may hold values from -1 to 1
- ffn_gain: bfloat16 [2048], P('fsdp'), may hold values from 0.099609375 to 1.8984375
- router: bfloat16 [2048, 8], P('fsdp'), may hold values from -0.0625 to 0.0625
- shared_gate: bfloat16 [2048], P('fsdp'), may hold values from -0.125 to 0.125
- w_sh_in: bfloat16 [2048, 11264], P('fsdp'), may hold values from -0.125 to 0.125
- w_sh_out: bfloat16 [2048, 5632], P('fsdp'), may hold values from -0.21875 to 0.21875
- w_exp_in: bfloat16 [8, 2048, 2816], P(None, 'fsdp'), may hold values from -0.125 to 0.125
- w_exp_out: bfloat16 [8, 2048, 1408], P(None, 'fsdp'), may hold values from -0.625 to 0.625
- cotangent: bfloat16 [8192, 2048], P(('ctx', 'fsdp')), may hold values from -6 to 6
Outputs:
- block_out: bfloat16 [8192, 2048], P(('ctx', 'fsdp'))
- d_tokens: float32 [8192, 2048], P(('ctx', 'fsdp'))
- d_attn_gain: float32 [2048], P('fsdp')
- d_w_attn_in: float32 [2048, 6144], P('fsdp')
- d_b_qkv: float32 [6144], P('fsdp')
- d_w_attn_out: float32 [2048, 2048], P('fsdp')
- d_ffn_gain: float32 [2048], P('fsdp')
- d_router: float32 [2048, 8], P('fsdp')
- d_shared_gate: float32 [2048], P('fsdp')
- d_w_sh_in: float32 [2048, 11264], P('fsdp')
- d_w_sh_out: float32 [2048, 5632], P('fsdp')
- d_w_exp_in: float32 [8, 2048, 2816], P(None, 'fsdp')
- d_w_exp_out: float32 [8, 2048, 1408], P(None, 'fsdp')
The draws below stay inside these ranges and needn't reach their ends.
Inputs may be any that keep to these rules, and one draw needn't show every extreme that they name: `routes`: each row names 4 different experts. Within the rows of one device no expert is named by more than 176 rows, and in every draw some expert is named by exactly 176 rows of some device. `block_ids`: entries 2c and 2c + 1 are the blocks of positions, of 128 tokens each, whose rows ctx index c holds, in that order; the two numbers add up to 7, and every number appears once.
All inputs are finite; a program needn't handle non-finite values.
Results may differ from the reference program's by a relative error of at most 0.035.
Values may be sent and summed in bfloat16 or wider, within the bound.
No kernel may reach another device: no remote copies, remote signals or barrier semaphores. Data moves between devices by JAX's collectives and lax.ppermute only.
A program may use at most 704 MiB of HBM per device.

```python
import math
import jax
import jax.numpy as jnp
import numpy as np
from jax import lax

D = 2048
HEADS = 16
HEAD_DIM = 128
FS = 5632
FE = 1408
TOP = 4
EXPERTS = 8
SEQ = 1024
TOK_DEV = 256
BLK = 128
BLOCKS = 8
CAP = 176
TOKENS = 8192
N_CTX = 4
N_FSDP = 8


def draw_block_ids(key, part):
    key = jax.random.fold_in(key, 17)
    perm_key, flip_key = jax.random.split(key)
    lower_blocks = jax.random.permutation(perm_key, BLOCKS // 2).astype(jnp.int32)
    flip_bits = jax.random.randint(flip_key, (BLOCKS // 2,), 0, 2)
    first_block = jnp.where(flip_bits == 1, lower_blocks, BLOCKS - 1 - lower_blocks)
    return jnp.stack([first_block, BLOCKS - 1 - first_block], axis=1).reshape(BLOCKS).astype(jnp.int32)


def shard_levels(own_key, extent, shards, smallest, largest):
    loudness, own = 1.0, jax.random.fold_in(own_key, 6)
    for position, shards_of in shards:
        steps = jnp.exp(jax.random.uniform(jax.random.fold_in(own, position), (shards_of,), jnp.float32, smallest / len(shards), largest / len(shards)))
        loudness = loudness * jnp.repeat(steps, extent[position] // shards_of).reshape([-1 if axis == position else 1 for axis in range(len(extent))])
    return loudness


def deal_out(own_key, own, number, rows, count, top, reach, slope):
    ranking = jax.random.permutation(own_key, count)
    crowded, ordinary = shares(count, rows * top, reach, slope, True), shares(count, rows * top, reach, slope, False)
    places = jnp.arange(count)

    def named(tallies, rotation):
        used = int((tallies > 0).sum())
        fixed = max(1, used // 4)
        passed = fixed + (places - fixed + rotation * (used - fixed)) % max(1, count - fixed)
        return jnp.zeros((count,), jnp.int32).at[ranking[jnp.where(places < fixed, places, passed)]].set(jnp.asarray(tallies, jnp.int32))

    tallies = jnp.where(number % 4 == 0, named(crowded, number // 4), named(ordinary, number - number // 4 - 1))
    mixed = jax.random.permutation(jax.random.fold_in(own, 3), count)
    source_of, taker = mixed[0:count // 2 * 2:2], mixed[1:count // 2 * 2:2]
    slack = jnp.minimum(tallies[source_of] - 1, reach - tallies[taker]) // 2
    slack = jnp.where((source_of == ranking[0]) | (taker == ranking[0]) | (tallies[taker] == 0), 0, jnp.maximum(slack, 0))
    passed = jax.random.randint(jax.random.fold_in(own, 4), (count // 2,), 0, 1 << 20) % (slack + 1)
    tallies = tallies.at[source_of].add(-passed).at[taker].add(passed)
    labels = jnp.searchsorted(jnp.cumsum(tallies), jnp.arange(rows * top), side="right").astype(jnp.int32)
    table = labels.reshape(top, rows).T
    table = table[jax.random.permutation(jax.random.fold_in(own, 1), rows)]
    rotation = jax.random.randint(jax.random.fold_in(own, 2), (rows, 1), 0, top)
    return jnp.take_along_axis(table, (jnp.arange(top)[None, :] + rotation) % top, axis=1)


def shares(amount, total, limit, lean, full):
    portions = [(1 << 20) // math.isqrt(rank ** lean) + 1 for rank in range(1, amount + 1)]
    largest = limit if full else min(limit, max(-(-total // amount), total * portions[0] // sum(portions)))
    least = 1 if total - largest >= amount - 1 else 0
    counts, surplus = [largest] + [least] * (amount - 1), total - largest - least * (amount - 1)
    while surplus > 0:
        free = [i for i in range(1, amount) if counts[i] < largest] or [i for i in range(1, amount) if counts[i] < limit]
        whole, remaining = sum([portions[i] for i in free]), surplus
        for i in free:
            extra = min(limit - counts[i], max(1, remaining * portions[i] // whole), surplus)
            counts[i] = counts[i] + extra
            surplus = surplus - extra
    return np.array(counts)


def gaussian(key, extent, deviation, limit, cuts=(), held_as=jnp.bfloat16):
    array = deviation * jax.random.normal(key, extent, jnp.float32)
    if cuts:
        array = array * shard_levels(key, extent, cuts, -0.22, 0.18)
    return jnp.clip(array, -limit, limit).astype(held_as)


def setup_inputs(seed: int = 0) -> dict:
    arg_keys = jax.random.split(jax.random.key(seed), 16)
    tokens = gaussian(arg_keys[0], (TOKENS, D), 1.0, 6.0, ((0, 32),))
    routes_keys = jax.random.split(jax.random.fold_in(arg_keys[1], 1), TOKENS // TOK_DEV)
    routes_turns = jax.random.permutation(jax.random.fold_in(arg_keys[1], 3), TOKENS // TOK_DEV)
    routes = jax.vmap(lambda own, number: deal_out(jax.random.fold_in(arg_keys[1], 2), own, number, TOK_DEV, EXPERTS, TOP, CAP, 1))(routes_keys, routes_turns).reshape((TOKENS, TOP))
    block_ids = draw_block_ids(jax.random.fold_in(arg_keys[15], 71), 0)
    attn_gain = jnp.clip(1.0 + 0.18 * jax.random.normal(arg_keys[3], (D,), jnp.float32), 0.099609375, 1.8984375).astype(jnp.bfloat16)
    w_attn_in = gaussian(arg_keys[4], (D, 3 * D), D ** -0.5, 0.125, ((0, 8),))
    b_qkv = gaussian(arg_keys[5], (3 * D,), 0.3, 2.0, ((0, 8),))
    w_attn_out = gaussian(arg_keys[6], (D, D), (D // 64) ** -0.5, 1.0, ((0, 8),))
    ffn_gain = jnp.clip(1.0 + 0.18 * jax.random.normal(arg_keys[7], (D,), jnp.float32), 0.099609375, 1.8984375).astype(jnp.bfloat16)
    router = gaussian(arg_keys[8], (D, EXPERTS), (4 * D) ** -0.5, 0.0625, ((0, 8),))
    shared_gate = gaussian(arg_keys[9], (D,), D ** -0.5, 0.125, ((0, 8),))
    w_sh_in = gaussian(arg_keys[10], (D, 2 * FS), D ** -0.5, 0.125, ((0, 8),))
    w_sh_out = gaussian(arg_keys[11], (D, FS), (FS // 8) ** -0.5, 0.21875, ((0, 8),))
    w_exp_in = gaussian(arg_keys[12], (EXPERTS, D, 2 * FE), D ** -0.5, 0.125, ((1, 8),))
    w_exp_out = gaussian(arg_keys[13], (EXPERTS, D, FE), (FE // 16) ** -0.5, 0.625, ((1, 8),))
    cotangent = gaussian(arg_keys[14], (TOKENS, D), 1.0, 6.0, ((0, 32),))
    return {"tokens": tokens, "routes": routes, "block_ids": block_ids, "attn_gain": attn_gain, "w_attn_in": w_attn_in, "b_qkv": b_qkv, "w_attn_out": w_attn_out, "ffn_gain": ffn_gain, "router": router, "shared_gate": shared_gate, "w_sh_in": w_sh_in, "w_sh_out": w_sh_out, "w_exp_in": w_exp_in, "w_exp_out": w_exp_out, "cotangent": cotangent}


@jax.custom_vjp
def low(v):
    return lax.optimization_barrier(v.astype(jnp.bfloat16)).astype(jnp.float32)

@jax.custom_vjp
def low_back(v):
    return v

def low_keep(v):
    return (low(v), None)

def low_pass(kept, grad):
    return (grad,)

def back_keep(v):
    return (v, None)

def back_low(kept, grad):
    return (low(grad),)
low.defvjp(low_keep, low_pass)
low_back.defvjp(back_keep, back_low)
norm_eps = 1e-06
rope_base = 1000000.0
highest = lax.Precision.HIGHEST

def matmul(left_op, right_op):
    return jnp.dot(left_op, right_op, precision=highest, preferred_element_type=jnp.float32)

def rms_scale(values):
    return lax.rsqrt(lax.optimization_barrier(jnp.mean(values * values, axis=-1, keepdims=True)) + norm_eps)

def block_places(block_list, block_len):
    offsets = jnp.arange(block_len, dtype=jnp.int32)
    return (block_list.astype(jnp.int32)[:, None] * block_len + offsets[None, :]).reshape(-1)

def rotary_tables(positions):
    half_dim = HEAD_DIM // 2
    inverse = rope_base ** (-2.0 * jnp.arange(half_dim, dtype=jnp.float32) / HEAD_DIM)
    angles = positions.astype(jnp.float32)[:, None] * inverse[None, :]
    cos_table = jnp.cos(angles)
    sin_table = jnp.sin(angles)
    return (jnp.concatenate([cos_table, cos_table], axis=1), jnp.concatenate([sin_table, sin_table], axis=1))

def rotate(values, cos_table, sin_table):
    half_dim = HEAD_DIM // 2
    turned = jnp.concatenate([-values[..., half_dim:], values[..., :half_dim]], axis=-1)
    return values * cos_table[:, None, :] + turned * sin_table[:, None, :]

def swiglu(activation, breadth):
    return jax.nn.silu(activation[:, :breadth]) * activation[:, breadth:]

def forward(inputs, attn_gain, w_attn_in, b_qkv, w_attn_out, ffn_gain, router, shared_gate, w_sh_in, w_sh_out, w_exp_in, w_exp_out, routes, places):
    score_scale = HEAD_DIM ** (-0.5)
    normed = low(inputs * rms_scale(inputs) * attn_gain)
    mixed = low_back(matmul(normed, w_attn_in) + b_qkv)
    cos_table, sin_table = rotary_tables(places)
    by_seq = mixed.reshape(N_CTX, N_FSDP, TOK_DEV, 3, HEADS, HEAD_DIM).transpose(1, 0, 2, 3, 4, 5)
    by_seq = by_seq.reshape(N_FSDP, SEQ, 3, HEADS, HEAD_DIM)
    queries = low(rotate(by_seq[:, :, 0], cos_table, sin_table))
    keys_all = low(rotate(by_seq[:, :, 1], cos_table, sin_table))
    values_all = low(by_seq[:, :, 2])
    visible = places[None, :] <= places[:, None]

    def heads_first(values):
        return values.transpose(0, 2, 1, 3).reshape(N_FSDP * HEADS, SEQ, HEAD_DIM)

    def attend(triple):
        query_one, key_one, value_one = triple
        raw_scores = low_back(matmul(query_one, key_one.T))
        scores = jnp.where(visible, raw_scores * score_scale, -jnp.inf)
        top_score = lax.optimization_barrier(jnp.max(scores, axis=1, keepdims=True))
        exponent = jnp.exp(scores - top_score)
        attn_prob = exponent / lax.optimization_barrier(jnp.sum(exponent, axis=1, keepdims=True))
        return matmul(low(attn_prob), value_one)
    attended = lax.map(jax.checkpoint(attend), (heads_first(queries), heads_first(keys_all), heads_first(values_all)))
    attended = attended.reshape(N_FSDP, HEADS, SEQ, HEAD_DIM).transpose(0, 2, 1, 3)
    attended = attended.reshape(N_FSDP, N_CTX, TOK_DEV, D).transpose(1, 0, 2, 3).reshape(TOKENS, D)
    attn_vec = low_back(low(attended))
    residual = inputs + low_back(matmul(attn_vec, w_attn_out))
    hidden_in = low(residual * rms_scale(residual) * ffn_gain)
    route_probs = jax.nn.softmax(matmul(hidden_in, router), axis=1)
    shared_prob = jax.nn.sigmoid(jnp.dot(hidden_in, shared_gate, precision=highest))
    shared_act = low_back(matmul(hidden_in, w_sh_in))
    shared_hidden = low(swiglu(shared_act, FS))
    shared_out = low_back(matmul(shared_hidden, w_sh_out.T))
    chosen = lax.optimization_barrier(jnp.sum((routes[:, :, None] == jnp.arange(EXPERTS, dtype=jnp.int32)[None, None, :]).astype(jnp.float32), axis=1))
    mixing = (route_probs * chosen).T

    def one_expert(moe_sum, stacked):
        in_weight, out_weight, column = stacked
        expert_act = low_back(matmul(hidden_in, in_weight))
        expert_hidden = low(swiglu(expert_act, FE))
        expert_out = low_back(matmul(expert_hidden, out_weight.T))
        return (moe_sum + column[:, None] * expert_out, None)
    moe_total, unused = lax.scan(jax.checkpoint(one_expert), jnp.zeros_like(inputs), (w_exp_in, w_exp_out, mixing))
    return residual + moe_total + shared_prob[:, None] * shared_out

def reference(tokens, routes, block_ids, attn_gain, w_attn_in, b_qkv, w_attn_out, ffn_gain, router, shared_gate, w_sh_in, w_sh_out, w_exp_in, w_exp_out, cotangent):
    places = block_places(block_ids, BLK)
    floats = tuple((array_in.astype(jnp.float32) for array_in in (tokens, attn_gain, w_attn_in, b_qkv, w_attn_out, ffn_gain, router, shared_gate, w_sh_in, w_sh_out, w_exp_in, w_exp_out)))

    def wrapped(*values):
        return forward(*values, routes, places)
    result, pullback = jax.vjp(wrapped, *floats)
    grads = pullback(cotangent.astype(jnp.float32))
    return (result.astype(jnp.bfloat16), grads[0], grads[1], grads[2], grads[3], grads[4], grads[5], grads[6], grads[7], grads[8], grads[9], grads[10], grads[11])
```

```python
import jax
import jax.numpy as jnp
from jax import lax
from jax.sharding import PartitionSpec as P

D = 2048
HEADS = 16
HEAD_DIM = 128
FS = 5632
FE = 1408
EXPERTS = 8


norm_eps = 1e-06
rope_base = 1000000.0
highest = lax.Precision.HIGHEST


def rms_scale(values):
    return lax.rsqrt(jnp.mean(values * values, axis=1, keepdims=True) + norm_eps)


def rms_back(grad_rows, unit_rows, row_scale, gain_row):
    scaled = grad_rows * gain_row
    return row_scale * (scaled - unit_rows * jnp.mean(scaled * unit_rows, axis=1, keepdims=True))


def block_places(block_list, block_len):
    offsets = jnp.arange(block_len, dtype=jnp.int32)
    return (block_list[:, None] * block_len + offsets[None, :]).reshape(-1)


def rotary_tables(positions):
    half_dim = HEAD_DIM // 2
    inverse = rope_base ** (-2.0 * jnp.arange(half_dim, dtype=jnp.float32) / HEAD_DIM)
    angles = positions.astype(jnp.float32)[:, None] * inverse[None, :]
    cos_table = jnp.cos(angles)
    sin_table = jnp.sin(angles)
    return (
        jnp.concatenate([cos_table, cos_table], axis=1),
        jnp.concatenate([sin_table, sin_table], axis=1),
    )


def rotate(values, cos_table, sin_table):
    half_dim = HEAD_DIM // 2
    turned = jnp.concatenate([-values[..., half_dim:], values[..., :half_dim]], axis=-1)
    return values * cos_table[:, None, :] + turned * sin_table[:, None, :]


def unrotate(values, cos_table, sin_table):
    half_dim = HEAD_DIM // 2
    scaled = values * sin_table[:, None, :]
    turned = jnp.concatenate([scaled[..., half_dim:], -scaled[..., :half_dim]], axis=-1)
    return values * cos_table[:, None, :] + turned


def swiglu(activation, breadth):
    return jax.nn.silu(activation[:, :breadth]) * activation[:, breadth:]


def swiglu_back(grad_hidden, activation, breadth):
    gate_part = activation[:, :breadth]
    up_part = activation[:, breadth:]
    sig_gate = jax.nn.sigmoid(gate_part)
    d_gate = grad_hidden * up_part * sig_gate * (1.0 + gate_part * (1.0 - sig_gate))
    d_up = grad_hidden * gate_part * sig_gate
    return jnp.concatenate([d_gate, d_up], axis=1)


def outer_rows(left_ops, right_ops):
    pieces = []
    for left_op, right_op in zip(left_ops, right_ops):
        pieces.append(
            lax.dot_general(
                left_op, right_op, (((0,), (0,)), ((), ())), preferred_element_type=jnp.float32
            )
        )
    return jnp.concatenate(pieces, axis=1)


def right_product(left_op, right_op):
    return lax.dot_general(
        left_op, right_op, (((1,), (1,)), ((), ())), preferred_element_type=jnp.float32
    )


def per_device(
    tokens,
    routes,
    block_ids,
    attn_gain,
    w_attn_in,
    b_qkv,
    w_attn_out,
    ffn_gain,
    router,
    shared_gate,
    w_sh_in,
    w_sh_out,
    w_exp_in,
    w_exp_out,
    cotangent,
):
    ctx_size = lax.axis_size("ctx")
    fsdp_size = lax.axis_size("fsdp")
    ctx_rank = lax.axis_index("ctx")
    fsdp_rank = lax.axis_index("fsdp")
    tok_rows = tokens.shape[0]
    block_len = tok_rows // 2
    seq_len = tok_rows * ctx_size
    heads_own = HEADS // ctx_size
    att_cols = heads_own * HEAD_DIM
    sh_cols = FS // ctx_size
    experts_own = EXPERTS // ctx_size
    score_scale = HEAD_DIM ** (-0.5)

    def own_cols(array, start, breadth):
        return lax.dynamic_slice_in_dim(array, start + ctx_rank * breadth, breadth, axis=1)

    def gather_fsdp(array):
        return lax.all_gather(array, "fsdp", axis=0, tiled=True)

    def gather_ctx(array):
        return lax.all_gather(array, "ctx", axis=0, tiled=True)

    def scatter_ctx(array):
        return lax.psum_scatter(
            array.astype(jnp.bfloat16), "ctx", scatter_dimension=0, tiled=True
        ).astype(jnp.float32)

    def scatter_fsdp(array):
        return lax.psum_scatter(
            array.astype(jnp.bfloat16), "fsdp", scatter_dimension=0, tiled=True
        )

    tokens_all = gather_ctx(tokens)
    smalls = jnp.concatenate(
        [attn_gain, ffn_gain, shared_gate, b_qkv, router.reshape(-1)]
    )
    smalls_all = lax.all_gather(smalls, "fsdp", axis=0, tiled=False)
    rows = attn_gain.shape[0]
    bias_rows = b_qkv.shape[0]
    gain_one = smalls_all[:, :rows].reshape(D).astype(jnp.float32)
    gain_two = smalls_all[:, rows : 2 * rows].reshape(D).astype(jnp.float32)
    gate_vec = smalls_all[:, 2 * rows : 3 * rows].reshape(D).astype(jnp.float32)
    bias_full = smalls_all[:, 3 * rows : 3 * rows + bias_rows].reshape(3 * D)
    router_wide = smalls_all[:, 3 * rows + bias_rows :].reshape(D, EXPERTS).astype(jnp.float32)
    bias_own = own_cols(bias_full.reshape(3, D), 0, att_cols).reshape(3 * att_cols)
    w_in_own = gather_fsdp(
        jnp.concatenate([own_cols(w_attn_in, part * D, att_cols) for part in range(3)], axis=1)
    )
    w_out_full = gather_fsdp(w_attn_out)
    routes_all = gather_ctx(routes)
    cot_all = gather_ctx(cotangent)

    ins = [
        jnp.concatenate([own_cols(w_sh_in, part * FS, sh_cols) for part in range(2)], axis=1)
    ]
    outs = [own_cols(w_sh_out, 0, sh_cols)]
    for own in range(experts_own):
        ins.append(w_exp_in[ctx_rank * experts_own + own])
        outs.append(w_exp_out[ctx_rank * experts_own + own])
    units = [sh_cols] + [FE] * experts_own

    wide_all = tokens_all.astype(jnp.float32)
    normed_all = (wide_all * rms_scale(wide_all) * gain_one).astype(jnp.bfloat16)
    inputs = tokens.astype(jnp.float32)
    scale_one = rms_scale(inputs)
    unit_one = inputs * scale_one
    mixed = jnp.dot(normed_all, w_in_own, preferred_element_type=jnp.float32) + bias_own.astype(
        jnp.float32
    )
    places = block_places(block_ids, block_len)
    cos_table, sin_table = rotary_tables(places)
    split_heads = mixed.reshape(seq_len, 3, heads_own, HEAD_DIM)
    queries = rotate(split_heads[:, 0], cos_table, sin_table).astype(jnp.bfloat16)
    key_heads = rotate(split_heads[:, 1], cos_table, sin_table).astype(jnp.bfloat16)
    value_heads = split_heads[:, 2].astype(jnp.bfloat16)
    visible = (places[None, :] <= places[:, None])[None]
    raw_scores = jnp.einsum("qhd,khd->hqk", queries, key_heads, preferred_element_type=jnp.float32)
    scores = jnp.where(visible, raw_scores * score_scale, -jnp.inf)
    top_score = jnp.max(scores, axis=2, keepdims=True)
    exponent = jnp.exp(scores - top_score)
    row_total = jnp.sum(exponent, axis=2, keepdims=True)
    attn_prob = exponent / row_total
    log_total = top_score + jnp.log(row_total)
    attended = jnp.einsum(
        "hqk,khd->qhd",
        attn_prob.astype(jnp.bfloat16),
        value_heads,
        preferred_element_type=jnp.float32,
    )
    attn_vec = lax.all_to_all(
        attended.reshape(seq_len, att_cols).astype(jnp.bfloat16), "ctx", 0, 1, tiled=True
    )
    residual = inputs + jnp.dot(attn_vec, w_out_full, preferred_element_type=jnp.float32)

    scale_two = rms_scale(residual)
    unit_two = residual * scale_two
    hidden_in = (unit_two * gain_two).astype(jnp.bfloat16)
    hidden_all = gather_ctx(hidden_in)
    hidden_wide = hidden_all.astype(jnp.float32)
    route_probs = jax.nn.softmax(
        jnp.dot(hidden_wide, router_wide, precision=highest, preferred_element_type=jnp.float32),
        axis=1,
    )
    shared_prob = jax.nn.sigmoid(
        jnp.dot(hidden_wide, gate_vec, precision=highest, preferred_element_type=jnp.float32)
    )
    expert_ids = jnp.arange(EXPERTS, dtype=jnp.int32)
    chosen = jnp.any(routes_all[:, :, None] == expert_ids[None, None, :], axis=1).astype(
        jnp.float32
    )
    mixing = route_probs * chosen

    block_sum = jnp.zeros((seq_len, D), jnp.float32)
    d_hidden_sum = jnp.zeros((seq_len, D), jnp.float32)
    d_probs = jnp.zeros((seq_len, EXPERTS), jnp.float32)
    d_shared_prob = None
    grad_ins, grad_outs = [], []
    for index, (in_shard, out_shard, breadth) in enumerate(zip(ins, outs, units)):
        in_full = gather_fsdp(in_shard)
        out_full = gather_fsdp(out_shard)
        if index == 0:
            factor = shared_prob[:, None]
        else:
            picked = expert_ids == ctx_rank * experts_own + (index - 1)
            factor = jnp.sum(jnp.where(picked[None, :], mixing, 0.0), axis=1, keepdims=True)
        act = jnp.dot(hidden_all, in_full, preferred_element_type=jnp.float32)
        d_unit = jnp.dot(cot_all, out_full, preferred_element_type=jnp.float32)
        unit_out = swiglu(act, breadth)
        d_factor = jnp.sum(d_unit * unit_out, axis=1)
        scaled_out = (factor * unit_out).astype(jnp.bfloat16)
        d_act = swiglu_back(factor * d_unit, act, breadth).astype(jnp.bfloat16)
        block_sum = block_sum + right_product(scaled_out, out_full)
        d_hidden_sum = d_hidden_sum + right_product(d_act, in_full)
        if index == 0:
            d_shared_prob = d_factor
        else:
            d_probs = d_probs + jnp.where(picked[None, :], chosen * d_factor[:, None], 0.0)
        grad_ins.append(scatter_fsdp(outer_rows((hidden_all,), (d_act,))))
        grad_outs.append(scatter_fsdp(outer_rows((cot_all,), (scaled_out,))))

    d_gate_logit = d_shared_prob * shared_prob * (1.0 - shared_prob)
    d_logits = route_probs * (d_probs - jnp.sum(route_probs * d_probs, axis=1, keepdims=True))
    d_route = jnp.concatenate([d_logits, d_gate_logit[:, None]], axis=1)
    route_mat = jnp.concatenate([router_wide, gate_vec[:, None]], axis=1)
    d_hidden_sum = d_hidden_sum + lax.dot_general(
        d_route,
        route_mat,
        (((1,), (1,)), ((), ())),
        precision=highest,
        preferred_element_type=jnp.float32,
    )
    d_route_mat = lax.dot_general(
        d_route,
        hidden_wide,
        (((0,), (0,)), ((), ())),
        precision=highest,
        preferred_element_type=jnp.float32,
    )
    block_out = (residual + scatter_ctx(block_sum)).astype(jnp.bfloat16)
    d_hidden = scatter_ctx(d_hidden_sum)
    grad_out = cotangent.astype(jnp.float32)
    d_gain_two = jnp.sum(d_hidden * unit_two, axis=0)
    d_resid = grad_out + rms_back(d_hidden, unit_two, scale_two, gain_two)
    d_attn = d_resid.astype(jnp.bfloat16)
    grad_w_out = scatter_fsdp(outer_rows((attn_vec,), (d_attn,)))
    d_vec = lax.all_to_all(
        right_product(d_attn, w_out_full).astype(jnp.bfloat16), "ctx", 1, 0, tiled=True
    )
    d_vec_heads = d_vec.reshape(seq_len, heads_own, HEAD_DIM)
    raw_again = jnp.einsum("qhd,khd->hqk", queries, key_heads, preferred_element_type=jnp.float32)
    prob_again = jnp.where(visible, jnp.exp(raw_again * score_scale - log_total), 0.0)
    d_value = jnp.einsum(
        "hqk,qhd->khd",
        prob_again.astype(jnp.bfloat16),
        d_vec_heads,
        preferred_element_type=jnp.float32,
    )
    d_prob = jnp.einsum(
        "qhd,khd->hqk", d_vec_heads, value_heads, preferred_element_type=jnp.float32
    )
    row_inner = jnp.sum(prob_again * d_prob, axis=2, keepdims=True)
    d_score = (prob_again * (d_prob - row_inner) * score_scale).astype(jnp.bfloat16)
    d_query = jnp.einsum("hqk,khd->qhd", d_score, key_heads, preferred_element_type=jnp.float32)
    d_key = jnp.einsum("hqk,qhd->khd", d_score, queries, preferred_element_type=jnp.float32)
    d_mixed = jnp.stack(
        [
            unrotate(d_query, cos_table, sin_table),
            unrotate(d_key, cos_table, sin_table),
            d_value,
        ],
        axis=1,
    )
    d_mixed = d_mixed.reshape(seq_len, 3 * att_cols).astype(jnp.bfloat16)
    d_bias = jnp.sum(d_mixed.astype(jnp.float32), axis=0)
    d_normed = scatter_ctx(right_product(d_mixed, w_in_own))
    grad_w_in = scatter_fsdp(outer_rows((normed_all,), (d_mixed,)))
    d_gain_one = jnp.sum(d_normed * unit_one, axis=0)
    d_tokens = d_resid + rms_back(d_normed, unit_one, scale_one, gain_one)

    def spread_cols(shard, parts):
        breadth = shard.shape[1] // parts
        spread = lax.all_gather(shard, "ctx", axis=0, tiled=False)
        spread = spread.reshape(ctx_size, shard.shape[0], parts, breadth)
        spread = jnp.transpose(spread, (1, 2, 0, 3))
        return spread.reshape(shard.shape[0], parts * ctx_size * breadth).astype(jnp.float32)

    def spread_experts(shards):
        spread = lax.all_gather(jnp.stack(shards), "ctx", axis=0, tiled=True)
        return spread.astype(jnp.float32)

    small_grads = lax.psum(
        jnp.concatenate([d_route_mat.reshape(-1), d_gain_two, d_gain_one]), ("ctx", "fsdp")
    )
    bias_grads = lax.psum(d_bias, "fsdp")
    bias_grads = lax.all_gather(bias_grads.reshape(3, att_cols), "ctx", axis=1, tiled=True)
    bias_grads = bias_grads.reshape(3 * D)

    def own_part(vector):
        size = vector.shape[0] // fsdp_size
        return lax.dynamic_slice_in_dim(vector, fsdp_rank * size, size)

    route_total = small_grads[: (EXPERTS + 1) * D].reshape(EXPERTS + 1, D)
    route_part = lax.dynamic_slice_in_dim(route_total, fsdp_rank * rows, rows, axis=1)
    return (
        block_out,
        d_tokens,
        own_part(small_grads[(EXPERTS + 2) * D :]),
        spread_cols(grad_w_in, 3),
        own_part(bias_grads),
        lax.psum(grad_w_out, "ctx").astype(jnp.float32),
        own_part(small_grads[(EXPERTS + 1) * D : (EXPERTS + 2) * D]),
        route_part[:EXPERTS].T,
        route_part[EXPERTS],
        spread_cols(grad_ins[0], 2),
        spread_cols(grad_outs[0], 1),
        spread_experts(grad_ins[1:]),
        spread_experts(grad_outs[1:]),
    )


def solution(mesh):
    return jax.shard_map(
        per_device,
        mesh=mesh,
        in_specs=(
            P(("ctx", "fsdp"), None),
            P(("ctx", "fsdp"), None),
            P(),
            P("fsdp"),
            P("fsdp", None),
            P("fsdp"),
            P("fsdp", None),
            P("fsdp"),
            P("fsdp", None),
            P("fsdp"),
            P("fsdp", None),
            P("fsdp", None),
            P(None, "fsdp", None),
            P(None, "fsdp", None),
            P(("ctx", "fsdp"), None),
        ),
        out_specs=(
            P(("ctx", "fsdp"), None),
            P(("ctx", "fsdp"), None),
            P("fsdp"),
            P("fsdp", None),
            P("fsdp"),
            P("fsdp", None),
            P("fsdp"),
            P("fsdp", None),
            P("fsdp"),
            P("fsdp", None),
            P("fsdp", None),
            P(None, "fsdp", None),
            P(None, "fsdp", None),
        ),
        check_vma=False,
    )
```

```python
import functools

import jax
import jax.numpy as jnp
from jax import lax
from jax.experimental import pallas as pl
from jax.experimental.pallas import tpu as pltpu
from jax.sharding import PartitionSpec as P

D = 2048
HEADS = 16
HEAD_DIM = 128
FS = 5632
FE = 1408
EXPERTS = 8


norm_eps = 1e-06
rope_base = 1000000.0
highest = lax.Precision.HIGHEST


def rms_scale(values):
    return lax.rsqrt(jnp.mean(values * values, axis=1, keepdims=True) + norm_eps)


def rms_back(grad_rows, unit_rows, row_scale, gain_row):
    scaled = grad_rows * gain_row
    return row_scale * (scaled - unit_rows * jnp.mean(scaled * unit_rows, axis=1, keepdims=True))


def block_places(block_list, block_len):
    offsets = jnp.arange(block_len, dtype=jnp.int32)
    return (block_list[:, None] * block_len + offsets[None, :]).reshape(-1)


def rotary_tables(positions):
    half_dim = HEAD_DIM // 2
    inverse = rope_base ** (-2.0 * jnp.arange(half_dim, dtype=jnp.float32) / HEAD_DIM)
    angles = positions.astype(jnp.float32)[:, None] * inverse[None, :]
    cos_table = jnp.cos(angles)
    sin_table = jnp.sin(angles)
    return (
        jnp.concatenate([cos_table, cos_table], axis=1),
        jnp.concatenate([sin_table, sin_table], axis=1),
    )


def rotate(values, cos_table, sin_table):
    half_dim = HEAD_DIM // 2
    turned = jnp.concatenate([-values[..., half_dim:], values[..., :half_dim]], axis=-1)
    return values * cos_table[:, None, :] + turned * sin_table[:, None, :]


def unrotate(values, cos_table, sin_table):
    half_dim = HEAD_DIM // 2
    scaled = values * sin_table[:, None, :]
    turned = jnp.concatenate([scaled[..., half_dim:], -scaled[..., :half_dim]], axis=-1)
    return values * cos_table[:, None, :] + turned


def swiglu(activation, breadth):
    return jax.nn.silu(activation[:, :breadth]) * activation[:, breadth:]


def swiglu_back(grad_hidden, activation, breadth):
    gate_part = activation[:, :breadth]
    up_part = activation[:, breadth:]
    sig_gate = jax.nn.sigmoid(gate_part)
    d_gate = grad_hidden * up_part * sig_gate * (1.0 + gate_part * (1.0 - sig_gate))
    d_up = grad_hidden * gate_part * sig_gate
    return jnp.concatenate([d_gate, d_up], axis=1)


def outer_rows(left_ops, right_ops):
    pieces = []
    for left_op, right_op in zip(left_ops, right_ops):
        pieces.append(
            lax.dot_general(
                left_op, right_op, (((0,), (0,)), ((), ())), preferred_element_type=jnp.float32
            )
        )
    return jnp.concatenate(pieces, axis=1)


def right_product(left_op, right_op):
    return lax.dot_general(
        left_op, right_op, (((1,), (1,)), ((), ())), preferred_element_type=jnp.float32
    )


def to_peer(array, bits):
    size = lax.axis_size("ctx")
    return lax.ppermute(array, "ctx", [(rank, rank ^ bits) for rank in range(size)])


def peer_gather(array):
    size = lax.axis_size("ctx")
    if size != 4:
        return [array] + [to_peer(array, bits) for bits in range(1, size)]
    half = array.shape[0] // 2
    one, two = to_peer(array, 1), to_peer(array, 2)
    three = jnp.concatenate([to_peer(one[:half], 2), to_peer(two[half:], 1)], axis=0)
    return [array, one, two, three]


def wide(array):
    return array.astype(jnp.float32)


def low(array):
    return array.astype(jnp.bfloat16)


def peer_scatter(pieces):
    size = lax.axis_size("ctx")
    pieces = [low(piece) for piece in pieces]
    if size != 4:
        total = wide(pieces[0])
        for bits in range(1, size):
            total = total + wide(to_peer(pieces[bits], bits))
        return total
    half = pieces[0].shape[0] // 2
    first = to_peer(jnp.concatenate([pieces[1][:half], pieces[3][:half]], axis=0), 1)
    second = to_peer(jnp.concatenate([pieces[2][half:], pieces[3][half:]], axis=0), 2)
    upper = to_peer(low(wide(pieces[2][:half]) + wide(first[half:])), 2)
    lower = to_peer(low(wide(pieces[1][half:]) + wide(second[half:])), 1)
    return wide(pieces[0]) + jnp.concatenate(
        [wide(first[:half]) + wide(upper), wide(second[:half]) + wide(lower)], axis=0
    )


def peer_sum(array):
    size, bits = lax.axis_size("ctx"), 1
    while bits < size:
        array = low(array)
        array = wide(array) + wide(to_peer(array, bits))
        bits *= 2
    return array


def by_rank(pieces):
    rank, bits = lax.axis_index("ctx"), 1
    while bits < len(pieces):
        odd = (rank & bits) != 0
        pieces = [jnp.where(odd, pieces[k ^ bits], pieces[k]) for k in range(len(pieces))]
        bits *= 2
    return pieces


def to_mate(array, bits):
    size = lax.axis_size("fsdp")
    return lax.ppermute(array, "fsdp", [(rank, rank ^ bits) for rank in range(size)])


def total_sum(array):
    bits = 1
    while bits < lax.axis_size("fsdp"):
        array = array + to_mate(array, bits)
        bits *= 2
    bits = 1
    while bits < lax.axis_size("ctx"):
        array = array + to_peer(array, bits)
        bits *= 2
    return array


VMEM_BYTES = 56 * 1024 * 1024


def own_call(kernel, name, grid, ins, in_specs, outs, out_specs, flops, waits=(), order=None, aliases=None):
    lead = 0 if order is None else 1
    count = len(ins)

    def body(*refs):
        kernel(*refs[lead : lead + count], *refs[lead + count + len(waits) :])

    moved = sum(array.size * array.dtype.itemsize for array in [*ins, *outs])
    return pl.pallas_call(
        body,
        out_shape=list(outs),
        grid_spec=pltpu.PrefetchScalarGridSpec(
            num_scalar_prefetch=lead,
            grid=grid,
            in_specs=list(in_specs) + [pl.BlockSpec(memory_space=pl.ANY)] * len(waits),
            out_specs=list(out_specs),
        ),
        compiler_params=pltpu.CompilerParams(vmem_limit_bytes=VMEM_BYTES),
        cost_estimate=pl.CostEstimate(flops=flops, transcendentals=0, bytes_accessed=moved),
        input_output_aliases=aliases or {},
        name=name,
    )(*([] if order is None else [order]), *ins, *waits)


def unit_backward(rows_in, rows_grad, weight, factor, waits=()):
    rows, depth = rows_in.shape
    breadth = weight.shape[1] // 3
    if breadth % 128:
        act = jnp.dot(rows_in, weight[:, : 2 * breadth], preferred_element_type=jnp.float32)
        d_unit = jnp.dot(rows_grad, weight[:, 2 * breadth :], preferred_element_type=jnp.float32)
        units = swiglu(act, breadth)
        return (
            low(factor * units),
            low(swiglu_back(factor * d_unit, act, breadth)),
            jnp.sum(d_unit * units, axis=1, keepdims=True),
        )
    tall = min(rows, 256)

    def kernel(rows_ref, grad_ref, weight_ref, factor_ref, out_ref, d_act_ref, d_factor_ref):
        scale = factor_ref[...]
        total = jnp.zeros((tall, 1), jnp.float32)
        for start in range(0, breadth, 256):
            gate = slice(start, min(start + 256, breadth))
            up = slice(breadth + gate.start, breadth + gate.stop)
            down = slice(2 * breadth + gate.start, 2 * breadth + gate.stop)
            gate_part = jnp.dot(
                rows_ref[...], weight_ref[:, gate], preferred_element_type=jnp.float32
            )
            up_part = jnp.dot(rows_ref[...], weight_ref[:, up], preferred_element_type=jnp.float32)
            d_unit = jnp.dot(grad_ref[...], weight_ref[:, down], preferred_element_type=jnp.float32)
            sig_gate = jax.nn.sigmoid(gate_part)
            silu = gate_part * sig_gate
            units = silu * up_part
            total = total + jnp.sum(d_unit * units, axis=1, keepdims=True)
            out_ref[:, gate] = low(scale * units)
            scaled = scale * d_unit
            d_act_ref[:, gate] = low(scaled * up_part * (sig_gate + silu * (1.0 - sig_gate)))
            d_act_ref[:, up] = low(scaled * silu)
        d_factor_ref[...] = total

    return own_call(
        kernel,
        "unit_backward",
        (rows // tall,),
        [rows_in, rows_grad, weight, factor],
        [
            pl.BlockSpec((tall, depth), lambda i: (i, 0)),
            pl.BlockSpec((tall, depth), lambda i: (i, 0)),
            pl.BlockSpec((depth, 3 * breadth), lambda i: (0, 0)),
            pl.BlockSpec((tall, 1), lambda i: (i, 0)),
        ],
        [
            jax.ShapeDtypeStruct((rows, breadth), jnp.bfloat16),
            jax.ShapeDtypeStruct((rows, 2 * breadth), jnp.bfloat16),
            jax.ShapeDtypeStruct((rows, 1), jnp.float32),
        ],
        [
            pl.BlockSpec((tall, breadth), lambda i: (i, 0)),
            pl.BlockSpec((tall, 2 * breadth), lambda i: (i, 0)),
            pl.BlockSpec((tall, 1), lambda i: (i, 0)),
        ],
        6 * rows * depth * breadth,
        waits,
    )


def back_matmul(jobs, waits=()):
    rows, breadth = jobs[0][0][0][0].shape[0], jobs[0][0][0][1].shape[0]
    tile = 256
    ins, specs, flops = [], [], 0
    for products, total, dtype in jobs:
        for rows_in, weight, column in products:
            depth = rows_in.shape[1]
            if depth % 128 and weight.shape[1] != depth:
                weight = weight[:, column * depth : (column + 1) * depth]
                column = 0
            ins += [rows_in, weight]
            specs += [
                pl.BlockSpec((rows, depth), lambda j: (0, 0)),
                pl.BlockSpec((tile, depth), lambda j, column=column: (j, column)),
            ]
            flops += 2 * rows * depth * breadth
        if total is not None:
            ins.append(total)
            specs.append(pl.BlockSpec((rows, tile), lambda j: (0, j)))

    def kernel(*refs):
        used = 0
        for out, (products, total, dtype) in enumerate(jobs):
            value = None
            for _ in products:
                part = right_product(refs[used][...], refs[used + 1][...])
                value = part if value is None else value + part
                used += 2
            if total is not None:
                value = value + wide(refs[used][...])
                used += 1
            refs[len(ins) + out][...] = value.astype(dtype)

    return own_call(
        kernel,
        "back_matmul",
        (breadth // tile,),
        ins,
        specs,
        [jax.ShapeDtypeStruct((rows, breadth), dtype) for products, total, dtype in jobs],
        [pl.BlockSpec((rows, tile), lambda j: (0, j))] * len(jobs),
        flops,
        waits,
    )


def route_product(d_route, route_mat):
    coarse = low(d_route)
    fine = low(d_route - wide(coarse))
    both = low(jnp.concatenate([route_mat, route_mat], axis=1))
    return (jnp.concatenate([coarse, fine], axis=1), both, 0)


def grad_matmul(pairs, order, adds=(), waits=()):
    rows = pairs[0][1].shape[0]
    widths = [right.shape[1] for left, right in pairs]
    total = sum(widths)
    count = order.shape[0]
    block = pairs[0][0].shape[1] // lax.axis_size("fsdp")
    lefts = []
    for left, right in pairs:
        if not any(left is other for other in lefts):
            lefts.append(left)
    which = [[left is other for other in lefts].index(True) for left, right in pairs]

    def kernel(*refs):
        left_refs, right_refs = refs[: len(lefts)], refs[len(lefts) : len(lefts) + len(pairs)]
        add_refs, out_ref = refs[len(lefts) + len(pairs) : -1], refs[-1]
        start = 0
        for spot, right_ref, width in zip(which, right_refs, widths):
            here = slice(start, start + width)
            value = lax.dot_general(
                left_refs[spot][...],
                right_ref[...],
                (((0,), (0,)), ((), ())),
                preferred_element_type=jnp.float32,
            )
            for ref in add_refs:
                value = value + wide(ref[:, here])
            out_ref[:, here] = low(value)
            start += width

    place = pl.BlockSpec((block, total), lambda j, order_ref: (j, 0))
    return own_call(
        kernel,
        "grad_matmul",
        (count,),
        [*lefts, *[right for left, right in pairs], *adds],
        [pl.BlockSpec((rows, block), lambda j, order_ref: (0, order_ref[j]))] * len(lefts)
        + [pl.BlockSpec((rows, width), lambda j, order_ref: (0, 0)) for width in widths]
        + [place] * len(adds),
        [jax.ShapeDtypeStruct((count * block, total), jnp.bfloat16)],
        [place],
        2 * rows * block * count * total,
        waits,
        order,
    )[0]


def pick_blocks(stack, picks, totals, waits=()):
    count = len(totals)
    rows, breadth = stack.shape[0] // (lax.axis_size("fsdp") // 2), stack.shape[1]
    tall = rows // 4
    flat = [array for arrays in totals for array in arrays]

    def kernel(*refs):
        used = count
        for out, arrays in enumerate(totals):
            value = refs[out][...]
            if arrays:
                value = wide(value)
                for ref in refs[used : used + len(arrays)]:
                    value = value + wide(ref[...])
                used += len(arrays)
            refs[count + len(flat) + out][...] = low(value)

    def from_stack(out):
        return pl.BlockSpec((tall, breadth), lambda i, pick_ref: (pick_ref[out] * 4 + i, 0))

    plain = pl.BlockSpec((tall, breadth), lambda i, pick_ref: (i, 0))
    return own_call(
        kernel,
        "pick_blocks",
        (4,),
        [stack] * count + flat,
        [from_stack(out) for out in range(count)] + [plain] * len(flat),
        [jax.ShapeDtypeStruct((rows, breadth), jnp.bfloat16)] * count,
        [plain] * count,
        0,
        waits,
        picks,
    )


class LineScatter:
    def __init__(self, pairs):
        size = lax.axis_size("fsdp")
        self.pairs, self.line = pairs, size // 2
        self.spot, self.core = lax.axis_index("fsdp") // 2, lax.axis_index("fsdp") % 2
        self.step_count, self.running = 0, [[], []]

    def blocks_of(self, core):
        return 2 * jnp.arange(self.line, dtype=jnp.int32) + core

    def give(self, waits=()):
        self.mark = grad_matmul(self.pairs, self.blocks_of(1 - self.core), (), waits)
        self.got = to_mate(self.mark, 1)

    def keep(self, waits=()):
        self.mark = self.stack = grad_matmul(
            self.pairs, self.blocks_of(self.core), [self.got], waits
        )

    def step(self, waits=()):
        self.step_count += 1
        left_over = self.line - self.step_count
        picks = jnp.clip(
            jnp.stack([left_over + self.spot, self.spot - left_over]), 0, self.line - 1
        )
        ups, downs = pick_blocks(self.stack, picks, self.running, waits)
        self.mark = downs
        up_pairs = [
            (2 * spot + core, 2 * spot + 2 + core)
            for spot in range(min(self.step_count, self.line - 1))
            for core in range(2)
        ]
        last = 2 * self.line - 1
        down_pairs = [(last - start, last - end) for start, end in up_pairs]
        self.running = [
            [lax.ppermute(ups, "fsdp", up_pairs)],
            [lax.ppermute(downs, "fsdp", down_pairs)],
        ]

    def finish(self, waits=()):
        while self.step_count < self.line - 1:
            self.step(waits)
        picks = self.spot.reshape(1)
        self.mark = pick_blocks(self.stack, picks, [self.running[0] + self.running[1]], waits)[0]
        return self.mark


def split_matmul(rows_in, gain, weight, bias, cos_table, sin_table, waits=()):
    rows, depth = rows_in.shape
    breadth = bias.shape[0]
    tile = 256
    turned = breadth * 2 // 3 // tile
    tall = min(rows, 256)

    def kernel(rows_ref, gain_ref, weight_ref, bias_ref, cos_ref, sin_ref, normed_ref, out_ref):
        @pl.when(pl.program_id(0) == 0)
        def _():
            for start in range(0, rows, tall):
                some = slice(start, start + tall)
                values = wide(rows_ref[some, :])
                normed_ref[some, :] = low(values * rms_scale(values) * gain_ref[...])

        value = jnp.dot(normed_ref[...], weight_ref[...], preferred_element_type=jnp.float32)
        value = value + bias_ref[...]

        @pl.when(pl.program_id(0) < turned)
        def _():
            for start in range(0, tile, HEAD_DIM):
                head = value[:, start : start + HEAD_DIM]
                head = head * cos_ref[...] + pltpu.roll(head, HEAD_DIM // 2, 1) * sin_ref[...]
                out_ref[:, start : start + HEAD_DIM] = low(head)

        @pl.when(pl.program_id(0) >= turned)
        def _():
            out_ref[...] = low(value)

    whole = pl.BlockSpec((rows, depth), lambda j: (0, 0))
    table = pl.BlockSpec((rows, HEAD_DIM), lambda j: (0, 0))
    return own_call(
        kernel,
        "split_matmul",
        (breadth // tile,),
        [rows_in, gain.reshape(1, depth), weight, bias.reshape(1, breadth), cos_table, sin_table],
        [
            whole,
            pl.BlockSpec((1, depth), lambda j: (0, 0)),
            pl.BlockSpec((depth, tile), lambda j: (0, j)),
            pl.BlockSpec((1, tile), lambda j: (0, j)),
            table,
            table,
        ],
        [
            jax.ShapeDtypeStruct((rows, depth), jnp.bfloat16),
            jax.ShapeDtypeStruct((rows, breadth), jnp.bfloat16),
        ],
        [whole, pl.BlockSpec((rows, tile), lambda j: (0, j))],
        2 * rows * depth * breadth,
        waits,
    )


def head_specs(rows, heads):
    return [
        pl.BlockSpec((rows, HEAD_DIM), lambda h, part=part: (0, part * heads + h))
        for part in range(3)
    ]


def attend(split, places, heads, waits=()):
    rows = split.shape[0]
    tall = min(rows, 256)
    scale = HEAD_DIM ** (-0.5)

    def kernel(query_ref, key_ref, value_ref, down_ref, across_ref, out_ref, log_ref):
        for start in range(0, rows, tall):
            some = slice(start, start + tall)
            scores = right_product(query_ref[some, :], key_ref[...]) * scale
            scores = jnp.where(across_ref[...] <= down_ref[some, :], scores, -1e30)
            top = jnp.max(scores, axis=1, keepdims=True)
            exponent = jnp.exp(scores - top)
            total = jnp.sum(exponent, axis=1, keepdims=True)
            prob = low(exponent * (1.0 / total))
            out_ref[some, :] = low(
                jnp.dot(prob, value_ref[...], preferred_element_type=jnp.float32)
            )
            log_ref[some, :] = top + jnp.log(total)

    return own_call(
        kernel,
        "attend",
        (heads,),
        [split, split, split, places.reshape(rows, 1), places.reshape(1, rows)],
        head_specs(rows, heads)
        + [
            pl.BlockSpec((rows, 1), lambda h: (0, 0)),
            pl.BlockSpec((1, rows), lambda h: (0, 0)),
        ],
        [
            jax.ShapeDtypeStruct((rows, heads * HEAD_DIM), jnp.bfloat16),
            jax.ShapeDtypeStruct((heads, rows, 1), jnp.float32),
        ],
        [
            pl.BlockSpec((rows, HEAD_DIM), lambda h: (0, h)),
            pl.BlockSpec((None, rows, 1), lambda h: (h, 0, 0)),
        ],
        4 * rows * rows * heads * HEAD_DIM,
        waits,
    )


def attend_back(split, places, log_total, d_vec, cos_table, sin_table, heads, waits=()):
    rows = split.shape[0]
    tall = min(rows, 256)
    scale = HEAD_DIM ** (-0.5)

    def kernel(query_ref, key_ref, value_ref, down_ref, across_ref, log_ref, grad_ref, cos_ref, sin_ref, out_ref):
        first = pl.multiple_of(pl.program_id(0) * HEAD_DIM, HEAD_DIM)
        d_key = jnp.zeros((rows, HEAD_DIM), jnp.float32)
        d_value = jnp.zeros((rows, HEAD_DIM), jnp.float32)

        def unturned(grad, some):
            return low(
                grad * cos_ref[some, :]
                - pltpu.roll(grad, HEAD_DIM // 2, 1) * sin_ref[some, :]
            )

        def columns(part):
            return pl.ds(first + part * heads * HEAD_DIM, HEAD_DIM)

        for start in range(0, rows, tall):
            some = slice(start, start + tall)
            query, grad = query_ref[some, :], grad_ref[some, :]
            scores = right_product(query, key_ref[...]) * scale
            prob = jnp.where(
                across_ref[...] <= down_ref[some, :], jnp.exp(scores - log_ref[some, :]), 0.0
            )
            d_prob = right_product(grad, value_ref[...])
            inner = jnp.sum(prob * d_prob, axis=1, keepdims=True)
            d_score = low(prob * (d_prob - inner) * scale)
            across = (((0,), (0,)), ((), ()))
            d_value = d_value + lax.dot_general(
                low(prob), grad, across, preferred_element_type=jnp.float32
            )
            d_key = d_key + lax.dot_general(
                d_score, query, across, preferred_element_type=jnp.float32
            )
            d_query = jnp.dot(d_score, key_ref[...], preferred_element_type=jnp.float32)
            out_ref[some, columns(0)] = unturned(d_query, some)
        out_ref[:, columns(1)] = unturned(d_key, slice(0, rows))
        out_ref[:, columns(2)] = low(d_value)

    table = pl.BlockSpec((rows, HEAD_DIM), lambda h: (0, 0))
    return own_call(
        kernel,
        "attend_back",
        (heads,),
        [split, split, split, places.reshape(rows, 1), places.reshape(1, rows), log_total, d_vec]
        + [cos_table, sin_table],
        head_specs(rows, heads)
        + [
            pl.BlockSpec((rows, 1), lambda h: (0, 0)),
            pl.BlockSpec((1, rows), lambda h: (0, 0)),
            pl.BlockSpec((None, rows, 1), lambda h: (h, 0, 0)),
            pl.BlockSpec((rows, HEAD_DIM), lambda h: (0, h)),
            table,
            table,
        ],
        [jax.ShapeDtypeStruct((rows, 3 * heads * HEAD_DIM), jnp.bfloat16)],
        [pl.BlockSpec((rows, 3 * heads * HEAD_DIM), lambda h: (0, 0))],
        10 * rows * rows * heads * HEAD_DIM,
        waits,
    )[0]


def place_grads(spread, slot, slots, totals, waits=()):
    size, rows = len(spread[0][0]), spread[0][0][0].shape[0]
    units = sum([sum(parts) for pieces, parts in spread])
    if units % 128:
        ordered = by_rank(spread[0][0])
        sides = [
            jnp.stack([piece[:, k * units : (k + 1) * units] for piece in ordered], axis=1)
            for k in range(3)
        ]
        into = jnp.stack(sides[:2], axis=1).reshape(rows, 2 * size * units)
        return wide(into), wide(sides[2].reshape(rows, size * units))
    tall = min(rows, 64)
    columns = 2 if slot is None else 1
    pieces = [held[k] for k in range(size) for held, parts in spread]
    onto = [] if totals is None else list(totals)
    rest = list(waits) + onto
    steps = rows // tall

    def kernel(*refs):
        in_ref, out_ref = refs[-2:]
        for k in range(size):

            @pl.when(pl.program_id(0) == k)
            def _():
                used = refs[k * len(spread) : (k + 1) * len(spread)]
                place = 0
                for (held, parts), ref in zip(spread, used):
                    start = 0
                    for part in parts:
                        gate = ref[:, start : start + part]
                        up = ref[:, start + part : start + 2 * part]
                        if slot is None:
                            here = pl.program_id(2) == 0
                            in_ref[:, place : place + part] = wide(jnp.where(here, gate, up))
                        else:
                            in_ref[:, place : place + part] = wide(gate)
                            in_ref[:, units + place : units + place + part] = wide(up)
                        out_ref[:, place : place + part] = wide(
                            ref[:, start + 2 * part : start + 3 * part]
                        )
                        place += part
                        start += 3 * part

    def piece_spec(k, parts):
        def piece_map(step, row, column, rank_ref):
            return (jnp.where(step == k, row, jnp.where(step < k, 0, steps - 1)), 0)

        return pl.BlockSpec((tall, 3 * sum(parts)), piece_map)

    if slot is None:
        shapes = [(rows, 2 * size * units), (rows, size * units)]
        out_specs = [
            pl.BlockSpec(
                (tall, units),
                lambda k, row, column, rank_ref: (row, column * size + (rank_ref[0] ^ k)),
            ),
            pl.BlockSpec((tall, units), lambda k, row, column, rank_ref: (row, rank_ref[0] ^ k)),
        ]
    else:
        shapes = [(size * slots, rows, 2 * units), (size * slots, rows, units)]
        out_specs = [
            pl.BlockSpec(
                (None, tall, shape[2]),
                lambda k, row, column, rank_ref: ((rank_ref[0] ^ k) * slots + slot, row, 0),
            )
            for shape in shapes
        ]
    first = 1 + len(pieces) + len(waits)
    return own_call(
        kernel,
        "place_grads",
        (size, steps, columns),
        pieces,
        [piece_spec(k, parts) for k in range(size) for held, parts in spread],
        [jax.ShapeDtypeStruct(shape, jnp.float32) for shape in shapes],
        out_specs,
        0,
        rest,
        lax.axis_index("ctx").reshape(1),
        {first: 0, first + 1: 1} if onto else {},
    )


def place_cols(pieces, parts, waits=()):
    size, rows = len(pieces), pieces[0].shape[0]
    breadth = pieces[0].shape[1] // parts
    if breadth % 128:
        ordered = [piece.reshape(rows, parts, breadth) for piece in by_rank(pieces)]
        return wide(jnp.stack(ordered, axis=2).reshape(rows, parts * size * breadth))

    def kernel(*refs):
        for k, ref in enumerate(refs[:-1]):

            @pl.when(pl.program_id(0) == k)
            def _():
                refs[-1][...] = wide(ref[...])

    def piece_spec(own):
        def piece_map(k, part, rank_ref):
            return (0, jnp.where(k == own, part, jnp.where(k < own, 0, parts - 1)))

        return pl.BlockSpec((rows, breadth), piece_map)

    return own_call(
        kernel,
        "place_cols",
        (size, parts),
        pieces,
        [piece_spec(own) for own in range(size)],
        [jax.ShapeDtypeStruct((rows, parts * size * breadth), jnp.float32)],
        [
            pl.BlockSpec(
                (rows, breadth), lambda k, part, rank_ref: (0, part * size + (rank_ref[0] ^ k))
            )
        ],
        0,
        waits,
        lax.axis_index("ctx").reshape(1),
    )[0]

def per_device(
    tokens,
    routes,
    block_ids,
    attn_gain,
    w_attn_in,
    b_qkv,
    w_attn_out,
    ffn_gain,
    router,
    shared_gate,
    w_sh_in,
    w_sh_out,
    w_exp_in,
    w_exp_out,
    cotangent,
):
    ctx_size = lax.axis_size("ctx")
    fsdp_size = lax.axis_size("fsdp")
    ctx_rank = lax.axis_index("ctx")
    fsdp_rank = lax.axis_index("fsdp")
    tok_rows = tokens.shape[0]
    block_len = tok_rows // 2
    seq_len = tok_rows * ctx_size
    heads_own = HEADS // ctx_size
    att_cols = heads_own * HEAD_DIM
    sh_cols = FS // ctx_size
    experts_own = EXPERTS // ctx_size

    def own_cols(array, start, breadth):
        return lax.dynamic_slice_in_dim(array, start + ctx_rank * breadth, breadth, axis=1)

    def gather_fsdp(array):
        return lax.all_gather(array, "fsdp", axis=0, tiled=True)

    def scatter_fsdp(array):
        return lax.psum_scatter(
            array.astype(jnp.bfloat16), "fsdp", scatter_dimension=0, tiled=True
        )

    def token_pieces(array):
        return [array[k * tok_rows : (k + 1) * tok_rows] for k in range(ctx_size)]

    tokens_all = jnp.concatenate(peer_gather(tokens), axis=0)
    rows = attn_gain.shape[0]
    smalls = jnp.concatenate(
        [jnp.stack([attn_gain, ffn_gain, shared_gate], axis=1), router, b_qkv.reshape(3, rows).T],
        axis=1,
    )
    smalls = jnp.pad(smalls, ((0, 0), (0, 128 - smalls.shape[1])))
    w_in_own = gather_fsdp(
        jnp.concatenate(
            [own_cols(w_attn_in, part * D, att_cols) for part in range(3)] + [smalls], axis=1
        )
    )
    smalls_all = w_in_own[:, 3 * att_cols :]
    gain_one, gain_two, gate_vec = [wide(smalls_all[:, k]) for k in range(3)]
    router_wide = wide(smalls_all[:, 3 : 3 + EXPERTS])
    bias_full = smalls_all[:, 3 + EXPERTS : 6 + EXPERTS].reshape(fsdp_size, rows, 3)
    bias_full = jnp.transpose(bias_full, (0, 2, 1)).reshape(3, D)
    bias_own = wide(own_cols(bias_full, 0, att_cols)).reshape(3 * att_cols)
    w_out_full = gather_fsdp(w_attn_out)

    slabs = []
    for own in range(-1, experts_own):
        if own < 0:
            units = sh_cols
            into = [own_cols(w_sh_in, part * FS, sh_cols) for part in range(2)]
            into.append(own_cols(w_sh_out, 0, sh_cols))
        else:
            units = FE
            expert = ctx_rank * experts_own + own
            into = [w_exp_in[expert, :, :FE], w_exp_in[expert, :, FE:], w_exp_out[expert]]
        middle = units if units % 128 else (units // 128 + 1) // 2 * 128
        slabs.append(
            [
                jnp.concatenate([side[:, start:stop] for side in into], axis=1)
                for start, stop in ((0, middle), (middle, units))
                if start < stop
            ]
        )

    plain = jnp.arange(fsdp_size, dtype=jnp.int32)

    inputs = wide(tokens)
    scale_one = rms_scale(inputs)
    unit_one = inputs * scale_one
    ranks = ctx_rank ^ jnp.arange(ctx_size, dtype=jnp.int32)
    places = block_places(block_ids.reshape(ctx_size, 2)[ranks].reshape(-1), block_len)
    cos_table, sin_table = rotary_tables(places)
    half = HEAD_DIM // 2
    sin_table = jnp.concatenate([-sin_table[:, :half], sin_table[:, half:]], axis=1)
    normed_all, split = split_matmul(
        tokens_all, gain_one, w_in_own, bias_own, cos_table, sin_table
    )
    attended, log_total = attend(split, places, heads_own)
    head_pieces = token_pieces(attended)
    head_pieces = head_pieces[:1] + [
        to_peer(head_pieces[bits], bits) for bits in range(1, ctx_size)
    ]
    attn_vec = jnp.concatenate(by_rank(head_pieces), axis=1)
    residual = inputs + jnp.dot(attn_vec, w_out_full, preferred_element_type=jnp.float32)

    scale_two = rms_scale(residual)
    unit_two = residual * scale_two
    hidden_in = low(unit_two * gain_two)
    hidden_all = jnp.concatenate(peer_gather(hidden_in), axis=0)
    cot_all = jnp.concatenate(peer_gather(cotangent), axis=0)
    routes_all = jnp.concatenate(
        [routes] + [to_peer(routes, bits) for bits in range(1, ctx_size)], axis=0
    )
    hidden_wide = wide(hidden_all)
    route_probs = jax.nn.softmax(
        jnp.dot(hidden_wide, router_wide, precision=highest, preferred_element_type=jnp.float32),
        axis=1,
    )
    shared_prob = jax.nn.sigmoid(
        jnp.dot(hidden_wide, gate_vec, precision=highest, preferred_element_type=jnp.float32)
    )
    expert_ids = jnp.arange(EXPERTS, dtype=jnp.int32)
    chosen = wide(jnp.any(routes_all[:, :, None] == expert_ids[None, None, :], axis=1))
    mixing = route_probs * chosen

    block_sum = d_hidden_sum = None
    d_probs = jnp.zeros((seq_len, EXPERTS), jnp.float32)
    d_gate_logit = jnp.zeros((seq_len, 1), jnp.float32)
    waits, line, spread = [], None, []
    for own, own_slabs in zip(range(-1, experts_own), slabs):
        if own < 0:
            factor = shared_prob[:, None]
        else:
            picked = expert_ids == ctx_rank * experts_own + own
            factor = jnp.sum(jnp.where(picked[None, :], mixing, 0.0), axis=1, keepdims=True)
        inward, outward, pairs, parts, last_shards = [], [], [], [], []
        for index, slab in enumerate(own_slabs):
            weight = gather_fsdp(slab)
            scaled_out, d_act, d_factor = unit_backward(
                hidden_all, cot_all, weight, factor, waits
            )
            waits = [scaled_out]
            inward.append((d_act, weight, 0))
            outward.append((scaled_out, weight, 2))
            pairs.append([(hidden_all, d_act), (cot_all, scaled_out)])
            parts.append(slab.shape[1] // 3)
            if own < 0:
                d_gate_logit = (
                    d_gate_logit + d_factor * (shared_prob * (1.0 - shared_prob))[:, None]
                )
            else:
                d_probs = d_probs + jnp.where(picked[None, :], chosen * d_factor, 0.0)
            if own == experts_own - 1:
                if index == len(own_slabs) - 1:
                    d_logits = route_probs * (
                        d_probs - jnp.sum(route_probs * d_probs, axis=1, keepdims=True)
                    )
                    d_route = jnp.concatenate([d_logits, d_gate_logit], axis=1)
                    route_mat = jnp.concatenate([router_wide, gate_vec[:, None]], axis=1)
                    inward.append(route_product(d_route, route_mat))
                    d_hidden_sum = back_matmul([(inward, d_hidden_sum, jnp.bfloat16)])[0]
                    waits = [d_hidden_sum]
                last_grad = grad_matmul(pairs[-1], plain, (), waits)
                last_shards.append(scatter_fsdp(last_grad))
                waits = [last_grad]
            if line is not None and (own < experts_own - 1 or index == 0):
                line.step(waits)
                waits = [line.mark]
        if own < experts_own - 1:
            before, line = line, LineScatter(sum(pairs, []))
            line.parts = parts
            line.give(waits)
            d_hidden_sum, block_sum = back_matmul(
                [(inward, d_hidden_sum, jnp.float32), (outward, block_sum, jnp.float32)],
                [line.mark],
            )
            line.keep([block_sum])
            line.step()
            waits = [line.mark]
            if before is not None:
                spread.append([(peer_gather(before.finish(waits)), before.parts)])
                waits = [before.mark]
    d_hidden_pieces = token_pieces(d_hidden_sum)
    d_route_mat = lax.dot_general(
        d_route,
        hidden_wide,
        (((0,), (0,)), ((), ())),
        precision=highest,
        preferred_element_type=jnp.float32,
    )
    d_hidden = peer_scatter(d_hidden_pieces)
    grad_out = wide(cotangent)
    d_gain_two = jnp.sum(d_hidden * unit_two, axis=0)
    d_resid = grad_out + rms_back(d_hidden, unit_two, scale_two, gain_two)
    d_attn = low(d_resid)
    d_vec_own = back_matmul([([(d_attn, w_out_full, 0)], None, jnp.bfloat16)], waits)[0]
    d_vec_pieces = by_rank(
        [d_vec_own[:, k * att_cols : (k + 1) * att_cols] for k in range(ctx_size)]
    )
    d_vec = jnp.concatenate(
        d_vec_pieces[:1] + [to_peer(d_vec_pieces[bits], bits) for bits in range(1, ctx_size)],
        axis=0,
    )
    grad_w_out = grad_matmul([(attn_vec, d_attn)], plain, (), [d_vec_own])
    line.step([grad_w_out])
    block_sum = back_matmul([(outward, block_sum, jnp.bfloat16)], [line.mark])[0]
    grad_w_out = scatter_fsdp(grad_w_out)
    d_mixed = attend_back(
        split, places, log_total, d_vec, cos_table, sin_table, heads_own, [block_sum]
    )
    grad_w_in = grad_matmul([(normed_all, d_mixed)], plain)
    d_bias = jnp.sum(wide(d_mixed), axis=0)
    d_normed_part = back_matmul(
        [([(d_mixed, w_in_own, 0)], None, jnp.bfloat16)], [grad_w_in]
    )[0]
    grad_w_in = scatter_fsdp(grad_w_in)
    d_normed = peer_scatter(token_pieces(d_normed_part))
    spread.append([(peer_gather(line.finish([d_normed_part])), line.parts)])
    waits, totals = [line.mark], None
    spread.append([(peer_gather(shard), [part]) for shard, part in zip(last_shards, parts)])
    shared_totals = place_grads(spread[0], None, 1, None, waits)
    waits = [shared_totals[0]]
    for own in range(experts_own):
        totals = place_grads(spread[1 + own], own, experts_own, totals, waits)
        waits = ()
    block_out = low(residual + peer_scatter(token_pieces(block_sum)))
    wide_all = wide(tokens_all)
    d_gain_one = jnp.sum(wide(d_normed_part) * (wide_all * rms_scale(wide_all)), axis=0)
    d_tokens = d_resid + rms_back(d_normed, unit_one, scale_one, gain_one)

    bias_spread = lax.dynamic_update_slice(
        jnp.zeros((3, D), jnp.float32), d_bias.reshape(3, att_cols), (0, ctx_rank * att_cols)
    )
    early_grads = total_sum(jnp.concatenate([d_route_mat.reshape(-1), d_gain_two]))
    late_grads = total_sum(jnp.concatenate([bias_spread.reshape(-1), d_gain_one]))

    def own_part(vector):
        size = vector.shape[0] // fsdp_size
        return lax.dynamic_slice_in_dim(vector, fsdp_rank * size, size)

    route_total = early_grads[: (EXPERTS + 1) * D].reshape(EXPERTS + 1, D)
    route_part = lax.dynamic_slice_in_dim(route_total, fsdp_rank * rows, rows, axis=1)
    return (
        block_out,
        d_tokens,
        own_part(late_grads[3 * D :]),
        place_cols(peer_gather(grad_w_in), 3),
        own_part(late_grads[: 3 * D]),
        peer_sum(grad_w_out),
        own_part(early_grads[(EXPERTS + 1) * D :]),
        route_part[:EXPERTS].T,
        route_part[EXPERTS],
        *shared_totals,
        *totals,
    )


def solution(mesh):
    return jax.shard_map(
        per_device,
        mesh=mesh,
        in_specs=(
            P(("ctx", "fsdp"), None),
            P(("ctx", "fsdp"), None),
            P(),
            P("fsdp"),
            P("fsdp", None),
            P("fsdp"),
            P("fsdp", None),
            P("fsdp"),
            P("fsdp", None),
            P("fsdp"),
            P("fsdp", None),
            P("fsdp", None),
            P(None, "fsdp", None),
            P(None, "fsdp", None),
            P(("ctx", "fsdp"), None),
        ),
        out_specs=(
            P(("ctx", "fsdp"), None),
            P(("ctx", "fsdp"), None),
            P("fsdp"),
            P("fsdp", None),
            P("fsdp"),
            P("fsdp", None),
            P("fsdp"),
            P("fsdp", None),
            P("fsdp"),
            P("fsdp", None),
            P("fsdp", None),
            P(None, "fsdp", None),
            P(None, "fsdp", None),
        ),
        check_vma=False,
    )
```

```python
import functools

import jax
import jax.numpy as jnp
from jax import lax
from jax.experimental import pallas as pl
from jax.experimental.pallas import tpu as pltpu
from jax.sharding import PartitionSpec as P

D = 2048
HEADS = 16
HEAD_DIM = 128
FS = 5632
FE = 1408
EXPERTS = 8


norm_eps = 1e-06
rope_base = 1000000.0
highest = lax.Precision.HIGHEST


def rms_scale(values):
    return lax.rsqrt(jnp.mean(values * values, axis=1, keepdims=True) + norm_eps)


def rms_back(grad_rows, unit_rows, row_scale, gain_row):
    scaled = grad_rows * gain_row
    return row_scale * (scaled - unit_rows * jnp.mean(scaled * unit_rows, axis=1, keepdims=True))


def block_places(block_list, block_len):
    offsets = jnp.arange(block_len, dtype=jnp.int32)
    return (block_list[:, None] * block_len + offsets[None, :]).reshape(-1)


def rotary_tables(positions):
    half_dim = HEAD_DIM // 2
    inverse = rope_base ** (-2.0 * jnp.arange(half_dim, dtype=jnp.float32) / HEAD_DIM)
    angles = positions.astype(jnp.float32)[:, None] * inverse[None, :]
    cos_table = jnp.cos(angles)
    sin_table = jnp.sin(angles)
    return (
        jnp.concatenate([cos_table, cos_table], axis=1),
        jnp.concatenate([sin_table, sin_table], axis=1),
    )


def rotate(values, cos_table, sin_table):
    half_dim = HEAD_DIM // 2
    turned = jnp.concatenate([-values[..., half_dim:], values[..., :half_dim]], axis=-1)
    return values * cos_table[:, None, :] + turned * sin_table[:, None, :]


def unrotate(values, cos_table, sin_table):
    half_dim = HEAD_DIM // 2
    scaled = values * sin_table[:, None, :]
    turned = jnp.concatenate([scaled[..., half_dim:], -scaled[..., :half_dim]], axis=-1)
    return values * cos_table[:, None, :] + turned


def swiglu(activation, breadth):
    return jax.nn.silu(activation[:, :breadth]) * activation[:, breadth:]


def swiglu_back(grad_hidden, activation, breadth):
    gate_part = activation[:, :breadth]
    up_part = activation[:, breadth:]
    sig_gate = jax.nn.sigmoid(gate_part)
    d_gate = grad_hidden * up_part * sig_gate * (1.0 + gate_part * (1.0 - sig_gate))
    d_up = grad_hidden * gate_part * sig_gate
    return jnp.concatenate([d_gate, d_up], axis=1)


def outer_rows(left_ops, right_ops):
    pieces = []
    for left_op, right_op in zip(left_ops, right_ops):
        pieces.append(
            lax.dot_general(
                left_op, right_op, (((0,), (0,)), ((), ())), preferred_element_type=jnp.float32
            )
        )
    return jnp.concatenate(pieces, axis=1)


def right_product(left_op, right_op):
    return lax.dot_general(
        left_op, right_op, (((1,), (1,)), ((), ())), preferred_element_type=jnp.float32
    )


def to_peer(array, bits):
    size = lax.axis_size("ctx")
    return lax.ppermute(array, "ctx", [(rank, rank ^ bits) for rank in range(size)])


def peer_gather(array, direct=False):
    size = lax.axis_size("ctx")
    if size != 4 or direct:
        return [array] + [to_peer(array, bits) for bits in range(1, size)]
    half = array.shape[0] // 2
    one, two = to_peer(array, 1), to_peer(array, 2)
    three = jnp.concatenate([to_peer(one[:half], 2), to_peer(two[half:], 1)], axis=0)
    return [array, one, two, three]


def wide(array):
    return array.astype(jnp.float32)


def low(array):
    return array.astype(jnp.bfloat16)


def peer_scatter(pieces):
    size = lax.axis_size("ctx")
    pieces = [low(piece) for piece in pieces]
    if size != 4:
        total = wide(pieces[0])
        for bits in range(1, size):
            total = total + wide(to_peer(pieces[bits], bits))
        return total
    half = pieces[0].shape[0] // 2
    first = to_peer(jnp.concatenate([pieces[1][:half], pieces[3][:half]], axis=0), 1)
    second = to_peer(jnp.concatenate([pieces[2][half:], pieces[3][half:]], axis=0), 2)
    upper = to_peer(low(wide(pieces[2][:half]) + wide(first[half:])), 2)
    lower = to_peer(low(wide(pieces[1][half:]) + wide(second[half:])), 1)
    return wide(pieces[0]) + jnp.concatenate(
        [wide(first[:half]) + wide(upper), wide(second[:half]) + wide(lower)], axis=0
    )


def peer_sum(array):
    size, half = lax.axis_size("ctx"), array.shape[0] // 2
    upper, lower, bits = array[:half], array[half:], 1
    while bits < size:
        upper, lower = low(upper), low(lower)
        other = size // 2 // bits
        upper = wide(upper) + wide(to_peer(upper, bits))
        lower = wide(lower) + wide(to_peer(lower, other))
        bits *= 2
    return jnp.concatenate([upper, lower], axis=0)


def by_rank(pieces):
    rank, bits = lax.axis_index("ctx"), 1
    while bits < len(pieces):
        odd = (rank & bits) != 0
        pieces = [jnp.where(odd, pieces[k ^ bits], pieces[k]) for k in range(len(pieces))]
        bits *= 2
    return pieces


def to_mate(array, bits):
    size = lax.axis_size("fsdp")
    return lax.ppermute(array, "fsdp", [(rank, rank ^ bits) for rank in range(size)])


def total_sum(array):
    bits = 1
    while bits < lax.axis_size("fsdp"):
        array = array + to_mate(array, bits)
        bits *= 2
    bits = 1
    while bits < lax.axis_size("ctx"):
        array = array + to_peer(array, bits)
        bits *= 2
    return array


VMEM_BYTES = 56 * 1024 * 1024


def own_call(kernel, name, grid, ins, in_specs, outs, out_specs, flops, waits=(), order=None, with_order=False):
    lead = 0 if order is None else 1
    count = len(ins)

    def body(*refs):
        first = 0 if with_order else lead
        kernel(*refs[first : lead + count], *refs[lead + count + len(waits) :])

    moved = sum(array.size * array.dtype.itemsize for array in [*ins, *outs])
    return pl.pallas_call(
        body,
        out_shape=list(outs),
        grid_spec=pltpu.PrefetchScalarGridSpec(
            num_scalar_prefetch=lead,
            grid=grid,
            in_specs=list(in_specs) + [pl.BlockSpec(memory_space=pl.ANY)] * len(waits),
            out_specs=list(out_specs),
        ),
        compiler_params=pltpu.CompilerParams(vmem_limit_bytes=VMEM_BYTES),
        cost_estimate=pl.CostEstimate(flops=flops, transcendentals=0, bytes_accessed=moved),
        name=name,
    )(*([] if order is None else [order]), *ins, *waits)


def after(array, waits):
    waits = [wait for wait in waits if wait is not None]
    if not waits:
        return array
    return pl.pallas_call(
        lambda *refs: None,
        out_shape=jax.ShapeDtypeStruct(array.shape, array.dtype),
        in_specs=[pl.BlockSpec(memory_space=pl.ANY)] * (1 + len(waits)),
        out_specs=pl.BlockSpec(memory_space=pl.ANY),
        input_output_aliases={0: 0},
        name="after",
    )(array, *waits)


def unit_backward(rows_in, rows_grad, weight, factor, waits=()):
    rows, depth = rows_in.shape
    breadth = weight.shape[1] // 3
    if breadth % 128:
        act = jnp.dot(rows_in, weight[:, : 2 * breadth], preferred_element_type=jnp.float32)
        d_unit = jnp.dot(rows_grad, weight[:, 2 * breadth :], preferred_element_type=jnp.float32)
        units = swiglu(act, breadth)
        return (
            low(factor * units),
            low(swiglu_back(factor * d_unit, act, breadth)),
            jnp.sum(d_unit * units, axis=1, keepdims=True),
        )
    tall = min(rows, 256)

    def kernel(rows_ref, grad_ref, weight_ref, factor_ref, out_ref, d_act_ref, d_factor_ref):
        scale = factor_ref[...]
        total = jnp.zeros((tall, 1), jnp.float32)
        for start in range(0, breadth, 256):
            gate = slice(start, min(start + 256, breadth))
            up = slice(breadth + gate.start, breadth + gate.stop)
            down = slice(2 * breadth + gate.start, 2 * breadth + gate.stop)
            gate_part = jnp.dot(
                rows_ref[...], weight_ref[:, gate], preferred_element_type=jnp.float32
            )
            up_part = jnp.dot(rows_ref[...], weight_ref[:, up], preferred_element_type=jnp.float32)
            d_unit = jnp.dot(grad_ref[...], weight_ref[:, down], preferred_element_type=jnp.float32)
            sig_gate = jax.nn.sigmoid(gate_part)
            silu = gate_part * sig_gate
            units = silu * up_part
            total = total + jnp.sum(d_unit * units, axis=1, keepdims=True)
            out_ref[:, gate] = low(scale * units)
            scaled = scale * d_unit
            d_act_ref[:, gate] = low(scaled * up_part * (sig_gate + silu * (1.0 - sig_gate)))
            d_act_ref[:, up] = low(scaled * silu)
        d_factor_ref[...] = total

    return own_call(
        kernel,
        "unit_backward",
        (rows // tall,),
        [rows_in, rows_grad, weight, factor],
        [
            pl.BlockSpec((tall, depth), lambda i: (i, 0)),
            pl.BlockSpec((tall, depth), lambda i: (i, 0)),
            pl.BlockSpec((depth, 3 * breadth), lambda i: (0, 0)),
            pl.BlockSpec((tall, 1), lambda i: (i, 0)),
        ],
        [
            jax.ShapeDtypeStruct((rows, breadth), jnp.bfloat16),
            jax.ShapeDtypeStruct((rows, 2 * breadth), jnp.bfloat16),
            jax.ShapeDtypeStruct((rows, 1), jnp.float32),
        ],
        [
            pl.BlockSpec((tall, breadth), lambda i: (i, 0)),
            pl.BlockSpec((tall, 2 * breadth), lambda i: (i, 0)),
            pl.BlockSpec((tall, 1), lambda i: (i, 0)),
        ],
        6 * rows * depth * breadth,
        waits,
    )


def back_matmul(jobs, waits=()):
    rows, breadth = jobs[0][0][0][0].shape[0], jobs[0][0][0][1].shape[0]
    tile = 256
    ins, specs, flops = [], [], 0
    for products, total, dtype in jobs:
        for rows_in, weight, column in products:
            depth = rows_in.shape[1]
            if depth % 128 and weight.shape[1] != depth:
                weight = weight[:, column * depth : (column + 1) * depth]
                column = 0
            ins += [rows_in, weight]
            specs += [
                pl.BlockSpec((rows, depth), lambda j: (0, 0)),
                pl.BlockSpec((tile, depth), lambda j, column=column: (j, column)),
            ]
            flops += 2 * rows * depth * breadth
        if total is not None:
            ins.append(total)
            specs.append(pl.BlockSpec((rows, tile), lambda j: (0, j)))

    def kernel(*refs):
        used = 0
        for out, (products, total, dtype) in enumerate(jobs):
            value = None
            for _ in products:
                part = right_product(refs[used][...], refs[used + 1][...])
                value = part if value is None else value + part
                used += 2
            if total is not None:
                value = value + wide(refs[used][...])
                used += 1
            refs[len(ins) + out][...] = value.astype(dtype)

    return own_call(
        kernel,
        "back_matmul",
        (breadth // tile,),
        ins,
        specs,
        [jax.ShapeDtypeStruct((rows, breadth), dtype) for products, total, dtype in jobs],
        [pl.BlockSpec((rows, tile), lambda j: (0, j))] * len(jobs),
        flops,
        waits,
    )


def route_product(d_route, route_mat):
    coarse = low(d_route)
    fine = low(d_route - wide(coarse))
    both = low(jnp.concatenate([route_mat, route_mat], axis=1))
    return (jnp.concatenate([coarse, fine], axis=1), both, 0)


def grad_matmul(pairs, waits=()):
    blocks = lax.axis_size("fsdp")
    depth = pairs[0][0][0].shape[1]
    widths = [rights[0].shape[1] for lefts, rights in pairs]
    total, block = sum(widths), depth // blocks
    ins, specs, flops = [], [], 0
    for lefts, rights in pairs:
        for left, right in zip(lefts, rights):
            ins += [left, right]
            specs += [
                pl.BlockSpec((left.shape[0], block), lambda j: (0, j)),
                pl.BlockSpec(right.shape, lambda j: (0, 0)),
            ]
            flops += 2 * left.shape[0] * depth * right.shape[1]

    def kernel(*refs):
        start, used = 0, 0
        for (lefts, rights), width in zip(pairs, widths):
            value = None
            for _ in lefts:
                part = lax.dot_general(
                    refs[used][...],
                    refs[used + 1][...],
                    (((0,), (0,)), ((), ())),
                    preferred_element_type=jnp.float32,
                )
                value = part if value is None else value + part
                used += 2
            refs[-1][:, start : start + width] = low(value)
            start += width

    return own_call(
        kernel,
        "grad_matmul",
        (blocks,),
        ins,
        specs,
        [jax.ShapeDtypeStruct((depth, total), jnp.bfloat16)],
        [pl.BlockSpec((block, total), lambda j: (j, 0))],
        flops,
        waits,
    )[0]


def split_matmul(rows_in, gain, weight, bias, cos_table, sin_table, waits=()):
    rows, depth = rows_in.shape
    breadth = bias.shape[0]
    tile = 256
    turned = breadth * 2 // 3 // tile
    tall = min(rows, 256)

    def kernel(rows_ref, gain_ref, weight_ref, bias_ref, cos_ref, sin_ref, normed_ref, out_ref):
        @pl.when(pl.program_id(0) == 0)
        def _():
            for start in range(0, rows, tall):
                some = slice(start, start + tall)
                values = wide(rows_ref[some, :])
                normed_ref[some, :] = low(values * rms_scale(values) * gain_ref[...])

        value = jnp.dot(normed_ref[...], weight_ref[...], preferred_element_type=jnp.float32)
        value = value + bias_ref[...]

        @pl.when(pl.program_id(0) < turned)
        def _():
            for start in range(0, tile, HEAD_DIM):
                head = value[:, start : start + HEAD_DIM]
                head = head * cos_ref[...] + pltpu.roll(head, HEAD_DIM // 2, 1) * sin_ref[...]
                out_ref[:, start : start + HEAD_DIM] = low(head)

        @pl.when(pl.program_id(0) >= turned)
        def _():
            out_ref[...] = low(value)

    whole = pl.BlockSpec((rows, depth), lambda j: (0, 0))
    table = pl.BlockSpec((rows, HEAD_DIM), lambda j: (0, 0))
    return own_call(
        kernel,
        "split_matmul",
        (breadth // tile,),
        [rows_in, gain.reshape(1, depth), weight, bias.reshape(1, breadth), cos_table, sin_table],
        [
            whole,
            pl.BlockSpec((1, depth), lambda j: (0, 0)),
            pl.BlockSpec((depth, tile), lambda j: (0, j)),
            pl.BlockSpec((1, tile), lambda j: (0, j)),
            table,
            table,
        ],
        [
            jax.ShapeDtypeStruct((rows, depth), jnp.bfloat16),
            jax.ShapeDtypeStruct((rows, breadth), jnp.bfloat16),
        ],
        [whole, pl.BlockSpec((rows, tile), lambda j: (0, j))],
        2 * rows * depth * breadth,
        waits,
    )


def head_specs(rows, heads):
    return [
        pl.BlockSpec((rows, HEAD_DIM), lambda h, part=part: (0, part * heads + h))
        for part in range(3)
    ]


def attend(split, places, heads, waits=()):
    rows = split.shape[0]
    tall = min(rows, 256)
    scale = HEAD_DIM ** (-0.5)

    def kernel(query_ref, key_ref, value_ref, down_ref, across_ref, out_ref, log_ref):
        for start in range(0, rows, tall):
            some = slice(start, start + tall)
            scores = right_product(query_ref[some, :], key_ref[...]) * scale
            scores = jnp.where(across_ref[...] <= down_ref[some, :], scores, -1e30)
            top = jnp.max(scores, axis=1, keepdims=True)
            exponent = jnp.exp(scores - top)
            total = jnp.sum(exponent, axis=1, keepdims=True)
            prob = low(exponent * (1.0 / total))
            out_ref[some, :] = low(
                jnp.dot(prob, value_ref[...], preferred_element_type=jnp.float32)
            )
            log_ref[some, :] = top + jnp.log(total)

    return own_call(
        kernel,
        "attend",
        (heads,),
        [split, split, split, places.reshape(rows, 1), places.reshape(1, rows)],
        head_specs(rows, heads)
        + [
            pl.BlockSpec((rows, 1), lambda h: (0, 0)),
            pl.BlockSpec((1, rows), lambda h: (0, 0)),
        ],
        [
            jax.ShapeDtypeStruct((rows, heads * HEAD_DIM), jnp.bfloat16),
            jax.ShapeDtypeStruct((heads, rows, 1), jnp.float32),
        ],
        [
            pl.BlockSpec((rows, HEAD_DIM), lambda h: (0, h)),
            pl.BlockSpec((None, rows, 1), lambda h: (h, 0, 0)),
        ],
        4 * rows * rows * heads * HEAD_DIM,
        waits,
    )


def attend_back(split, places, log_total, d_vec, cos_table, sin_table, heads, waits=()):
    rows = split.shape[0]
    tall = min(rows, 256)
    scale = HEAD_DIM ** (-0.5)

    def kernel(query_ref, key_ref, value_ref, down_ref, across_ref, log_ref, grad_ref, cos_ref, sin_ref, out_ref):
        first = pl.multiple_of(pl.program_id(0) * HEAD_DIM, HEAD_DIM)
        d_key = jnp.zeros((rows, HEAD_DIM), jnp.float32)
        d_value = jnp.zeros((rows, HEAD_DIM), jnp.float32)

        def unturned(grad, some):
            return low(
                grad * cos_ref[some, :]
                - pltpu.roll(grad, HEAD_DIM // 2, 1) * sin_ref[some, :]
            )

        def columns(part):
            return pl.ds(first + part * heads * HEAD_DIM, HEAD_DIM)

        for start in range(0, rows, tall):
            some = slice(start, start + tall)
            query, grad = query_ref[some, :], grad_ref[some, :]
            scores = right_product(query, key_ref[...]) * scale
            prob = jnp.where(
                across_ref[...] <= down_ref[some, :], jnp.exp(scores - log_ref[some, :]), 0.0
            )
            d_prob = right_product(grad, value_ref[...])
            inner = jnp.sum(prob * d_prob, axis=1, keepdims=True)
            d_score = low(prob * (d_prob - inner) * scale)
            across = (((0,), (0,)), ((), ()))
            d_value = d_value + lax.dot_general(
                low(prob), grad, across, preferred_element_type=jnp.float32
            )
            d_key = d_key + lax.dot_general(
                d_score, query, across, preferred_element_type=jnp.float32
            )
            d_query = jnp.dot(d_score, key_ref[...], preferred_element_type=jnp.float32)
            out_ref[some, columns(0)] = unturned(d_query, some)
        out_ref[:, columns(1)] = unturned(d_key, slice(0, rows))
        out_ref[:, columns(2)] = low(d_value)

    table = pl.BlockSpec((rows, HEAD_DIM), lambda h: (0, 0))
    return own_call(
        kernel,
        "attend_back",
        (heads,),
        [split, split, split, places.reshape(rows, 1), places.reshape(1, rows), log_total, d_vec]
        + [cos_table, sin_table],
        head_specs(rows, heads)
        + [
            pl.BlockSpec((rows, 1), lambda h: (0, 0)),
            pl.BlockSpec((1, rows), lambda h: (0, 0)),
            pl.BlockSpec((None, rows, 1), lambda h: (h, 0, 0)),
            pl.BlockSpec((rows, HEAD_DIM), lambda h: (0, h)),
            table,
            table,
        ],
        [jax.ShapeDtypeStruct((rows, 3 * heads * HEAD_DIM), jnp.bfloat16)],
        [pl.BlockSpec((rows, 3 * heads * HEAD_DIM), lambda h: (0, 0))],
        10 * rows * rows * heads * HEAD_DIM,
        waits,
    )[0]


def place_shared(pieces, real, waits=()):
    size, rows, padded = len(pieces), pieces[0].shape[0] // 2, pieces[0].shape[1] // 3
    units = 2 * real
    side = (lax.axis_index("fsdp") >> 1) & 1
    if units % 128:
        into, out = ordered_sides(pieces, real)
        return wide(into.reshape(rows, 2 * size * units)), wide(out.reshape(rows, size * units))
    tall = min(rows, 64)
    steps = rows // tall
    base, shift = real // 128 * 128, real % 128

    def joined(first, second):
        first, second = wide(first), wide(second)
        if shift:
            second = pltpu.roll(second, shift, 1)
        overlap = first[:, base:padded] + second[:, : padded - base]
        return [first[:, :base], overlap, second[:, padded - base : units - base]]

    def kernel(order_ref, *refs):
        in_ref, out_ref = refs[-2:]
        mine = order_ref[1] == 0
        for k in range(size):

            @pl.when(pl.program_id(0) == k)
            def _():
                own, other = refs[2 * k], refs[2 * k + 1]

                def sides(start):
                    here = slice(start, start + padded)
                    first = jnp.where(mine, own[:, here], other[:, here])
                    second = jnp.where(mine, other[:, here], own[:, here])
                    return joined(first, second)

                def put(ref, values):
                    place = 0
                    for value in values:
                        ref[:, place : place + value.shape[1]] = value
                        place += value.shape[1]

                @pl.when(pl.program_id(2) == 0)
                def _():
                    put(in_ref, sides(0))
                    put(out_ref, sides(2 * padded))

                @pl.when(pl.program_id(2) == 1)
                def _():
                    put(in_ref, sides(padded))

    def piece_spec(k, first):
        def piece_map(step, row, part, order_ref):
            return (first + jnp.where(step == k, row, jnp.where(step < k, 0, steps - 1)), 0)

        return pl.BlockSpec((tall, 3 * padded), piece_map)

    return own_call(
        kernel,
        "place_shared",
        (size, steps, 2),
        [piece for piece in pieces for _ in range(2)],
        [piece_spec(k, first) for k in range(size) for first in (0, steps)],
        [
            jax.ShapeDtypeStruct((rows, 2 * size * units), jnp.float32),
            jax.ShapeDtypeStruct((rows, size * units), jnp.float32),
        ],
        [
            pl.BlockSpec(
                (tall, units), lambda k, row, part, order_ref: (row, part * size + (order_ref[0] ^ k))
            ),
            pl.BlockSpec((tall, units), lambda k, row, part, order_ref: (row, order_ref[0] ^ k)),
        ],
        0,
        waits,
        jnp.stack([lax.axis_index("ctx"), side]),
        with_order=True,
    )


def place_experts(pieces, waits=()):
    size, rows, breadth = len(pieces), pieces[0].shape[0] // 2, pieces[0].shape[1]
    side = (lax.axis_index("fsdp") >> 1) & 1
    tall = min(rows, 64)
    steps = rows // tall

    def kernel(*refs):
        for k, ref in enumerate(refs[:-1]):

            @pl.when(pl.program_id(0) == k)
            def _():
                refs[-1][...] = wide(ref[...])

    def piece_spec(k):
        def piece_map(step, row, order_ref):
            return (jnp.where(step == k, row, jnp.where(step < k, 0, 2 * steps - 1)), 0)

        return pl.BlockSpec((tall, breadth), piece_map)

    def out_map(k, row, order_ref):
        expert = 2 * (order_ref[0] ^ k) + (order_ref[1] ^ (row // steps))
        return (expert, row % steps, 0)

    return own_call(
        kernel,
        "place_experts",
        (size, 2 * steps),
        pieces,
        [piece_spec(k) for k in range(size)],
        [jax.ShapeDtypeStruct((2 * size, rows, breadth), jnp.float32)],
        [pl.BlockSpec((None, tall, breadth), out_map)],
        0,
        waits,
        jnp.stack([lax.axis_index("ctx"), side]),
    )[0]


def ordered_sides(pieces, real):
    rows, padded = pieces[0].shape[0] // 2, pieces[0].shape[1] // 3
    first = ((lax.axis_index("fsdp") >> 1) & 1) == 0
    joined = []
    for piece in by_rank(pieces):
        own, other = piece[:rows], piece[rows:]
        halves = [jnp.where(first, own, other), jnp.where(first, other, own)]
        joined.append(
            [
                jnp.concatenate([half[:, k * padded : k * padded + real] for half in halves], axis=1)
                for k in range(3)
            ]
        )
    into = jnp.stack([jnp.stack([sides[k] for sides in joined], axis=1) for k in range(2)], axis=1)
    return into, jnp.stack([sides[2] for sides in joined], axis=1)


def place_cols(pieces, parts, waits=()):
    size, rows = len(pieces), pieces[0].shape[0]
    breadth = pieces[0].shape[1] // parts
    if breadth % 128:
        ordered = [piece.reshape(rows, parts, breadth) for piece in by_rank(pieces)]
        return wide(jnp.stack(ordered, axis=2).reshape(rows, parts * size * breadth))

    def kernel(*refs):
        for k, ref in enumerate(refs[:-1]):

            @pl.when(pl.program_id(0) == k)
            def _():
                refs[-1][...] = wide(ref[...])

    def piece_spec(own):
        def piece_map(k, part, rank_ref):
            return (0, jnp.where(k == own, part, jnp.where(k < own, 0, parts - 1)))

        return pl.BlockSpec((rows, breadth), piece_map)

    return own_call(
        kernel,
        "place_cols",
        (size, parts),
        pieces,
        [piece_spec(own) for own in range(size)],
        [jax.ShapeDtypeStruct((rows, parts * size * breadth), jnp.float32)],
        [
            pl.BlockSpec(
                (rows, breadth), lambda k, part, rank_ref: (0, part * size + (rank_ref[0] ^ k))
            )
        ],
        0,
        waits,
        lax.axis_index("ctx").reshape(1),
    )[0]

def per_device(
    tokens,
    routes,
    block_ids,
    attn_gain,
    w_attn_in,
    b_qkv,
    w_attn_out,
    ffn_gain,
    router,
    shared_gate,
    w_sh_in,
    w_sh_out,
    w_exp_in,
    w_exp_out,
    cotangent,
):
    ctx_size = lax.axis_size("ctx")
    fsdp_size = lax.axis_size("fsdp")
    ctx_rank = lax.axis_index("ctx")
    fsdp_rank = lax.axis_index("fsdp")
    tok_rows = tokens.shape[0]
    block_len = tok_rows // 2
    seq_len = tok_rows * ctx_size
    heads_own = HEADS // ctx_size
    att_cols = heads_own * HEAD_DIM
    sh_cols = FS // ctx_size
    experts_own = EXPERTS // ctx_size

    def own_cols(array, start, breadth):
        return lax.dynamic_slice_in_dim(array, start + ctx_rank * breadth, breadth, axis=1)

    def gather_fsdp(array):
        return lax.all_gather(array, "fsdp", axis=0, tiled=True)

    def scatter_fsdp(array):
        return lax.psum_scatter(
            array.astype(jnp.bfloat16), "fsdp", scatter_dimension=0, tiled=True
        )

    def token_pieces(array):
        return [array[k * tok_rows : (k + 1) * tok_rows] for k in range(ctx_size)]

    tokens_all = jnp.concatenate(peer_gather(tokens), axis=0)
    quarter = D // ctx_size
    w_out_own = gather_fsdp(own_cols(w_attn_out, 0, quarter))
    w_out_pieces = peer_gather(w_out_own)
    rows = attn_gain.shape[0]
    smalls = jnp.concatenate(
        [jnp.stack([attn_gain, ffn_gain, shared_gate], axis=1), router, b_qkv.reshape(3, rows).T],
        axis=1,
    )
    smalls = jnp.pad(smalls, ((0, 0), (0, 128 - smalls.shape[1])))
    w_in_slab = jnp.concatenate(
        [own_cols(w_attn_in, part * D, att_cols) for part in range(3)] + [smalls], axis=1
    )
    w_in_own = gather_fsdp(after(w_in_slab, [w_out_own]))
    smalls_all = w_in_own[:, 3 * att_cols :]
    gain_one, gain_two, gate_vec = [wide(smalls_all[:, k]) for k in range(3)]
    router_wide = wide(smalls_all[:, 3 : 3 + EXPERTS])
    bias_full = smalls_all[:, 3 + EXPERTS : 6 + EXPERTS].reshape(fsdp_size, rows, 3)
    bias_full = jnp.transpose(bias_full, (0, 2, 1)).reshape(3, D)
    bias_own = wide(own_cols(bias_full, 0, att_cols)).reshape(3 * att_cols)

    side = (fsdp_rank >> 1) & 1
    groups = [[rank for rank in range(fsdp_size) if (rank >> 1) & 1 == spot] for spot in range(2)]

    def by_side(own, other):
        return [jnp.where(side == 0, own, other), jnp.where(side == 0, other, own)]

    def halves_of(sides):
        real = sides[0].shape[1] // 2
        pad = ((0, 0), (0, -real % 128))
        return by_side(
            *[
                jnp.concatenate(
                    [jnp.pad(part[:, k * real : (k + 1) * real], pad) for part in sides], axis=1
                )
                for k in range(2)
            ]
        )

    def expert_sides(expert):
        return [w_exp_in[expert, :, :FE], w_exp_in[expert, :, FE:], w_exp_out[expert]]

    shared_sides = [own_cols(w_sh_in, part * FS, sh_cols) for part in range(2)]
    slabs = [halves_of(shared_sides + [own_cols(w_sh_out, 0, sh_cols)])]
    if experts_own == 1:
        own_expert = ctx_rank
        slabs.append(halves_of(expert_sides(own_expert)))
    else:
        own_expert = experts_own * ctx_rank + side
        both = [expert_sides(own_expert), expert_sides(experts_own * ctx_rank + 1 - side)]
        slabs.append([jnp.concatenate(sides, axis=1) for sides in both])

    def gather_slab(own, other, waits):
        rows_both = after(jnp.concatenate(by_side(own, to_mate(other, 2)), axis=0), waits)
        return lax.all_gather(
            rows_both, "fsdp", axis=0, axis_index_groups=groups, tiled=True
        )

    summed = []

    def scatter_slab(grad):
        both = lax.psum_scatter(
            grad, "fsdp", scatter_dimension=0, axis_index_groups=groups, tiled=True
        )
        summed.append(both)
        own, other = by_side(both[:rows], both[rows:])
        return jnp.concatenate([own, to_mate(other, 2)], axis=0)

    def turn(array):
        size = array.shape[1] // fsdp_size
        spots = [spot & ~3 | (spot & 1) << 1 | (spot & 2) >> 1 for spot in range(fsdp_size)]
        return jnp.concatenate(
            [array[:, spot * size : (spot + 1) * size] for spot in spots], axis=1
        )

    inputs = wide(tokens)
    scale_one = rms_scale(inputs)
    unit_one = inputs * scale_one
    ranks = ctx_rank ^ jnp.arange(ctx_size, dtype=jnp.int32)
    places = block_places(block_ids.reshape(ctx_size, 2)[ranks].reshape(-1), block_len)
    cos_table, sin_table = rotary_tables(places)
    half = HEAD_DIM // 2
    sin_table = jnp.concatenate([-sin_table[:, :half], sin_table[:, half:]], axis=1)
    normed_all, split = split_matmul(
        tokens_all, gain_one, w_in_own, bias_own, cos_table, sin_table
    )
    attended, log_total = attend(split, places, heads_own, w_out_pieces)
    head_pieces = token_pieces(attended)
    head_pieces = head_pieces[:1] + [
        to_peer(head_pieces[bits], bits) for bits in range(1, ctx_size)
    ]
    attn_vec = jnp.concatenate(by_rank(head_pieces), axis=1)
    attn_out = [
        jnp.dot(attn_vec, piece, preferred_element_type=jnp.float32) for piece in w_out_pieces
    ]
    residual = inputs + jnp.concatenate(by_rank(attn_out), axis=1)

    scale_two = rms_scale(residual)
    unit_two = residual * scale_two
    cot_own = after(turn(cotangent), [split])
    hidden_own = turn(low(unit_two * gain_two))
    cots = [cot_own, after(to_mate(cot_own, 2), [hidden_own])]
    cots = [jnp.concatenate(peer_gather(array), axis=0) for array in cots]

    hidden = [hidden_own, to_mate(hidden_own, 2)]
    hidden = [jnp.concatenate(peer_gather(array), axis=0) for array in hidden]
    route_mat = jnp.concatenate([router_wide, gate_vec[:, None]], axis=1)
    route_mat = turn(route_mat.T).T
    expert_ids = jnp.arange(EXPERTS, dtype=jnp.int32)
    halves = range(2)
    route_probs, shared_prob, chosen = [], [], []
    for half, routes_half in zip(halves, (routes, to_mate(routes, 2))):
        logits = jnp.dot(
            wide(hidden[half]), route_mat, precision=highest, preferred_element_type=jnp.float32
        )
        route_probs.append(jax.nn.softmax(logits[:, :EXPERTS], axis=1))
        shared_prob.append(jax.nn.sigmoid(logits[:, EXPERTS:]))
        routes_all = jnp.concatenate(
            [routes_half] + [to_peer(routes_half, bits) for bits in range(1, ctx_size)], axis=0
        )
        chosen.append(
            wide(jnp.any(routes_all[:, :, None] == expert_ids[None, None, :], axis=1))
        )
    picked = (expert_ids == own_expert)[None, :]

    def units_of(weight, factors, held):
        results = []
        for half in halves:
            results.append(unit_backward(hidden[half], cots[half], weight, factors[half], held))
            held = [results[-1][0]]
        return [list(kind) for kind in zip(*results)]

    other = after(slabs[0][1], [tokens_all])
    shared_weight = gather_slab(slabs[0][0], other, [w_in_own])
    other = after(slabs[1][1], [w_in_own])
    expert_weight = gather_slab(slabs[1][0], other, [attended])

    outs_shared, acts_shared, d_shared = units_of(shared_weight, shared_prob, [])
    grad_shared = grad_matmul(
        [(hidden, acts_shared), (cots, outs_shared)], outs_shared[1:]
    )
    waits, sums = [grad_shared], []
    for half in halves:
        sums.append(
            back_matmul(
                [
                    ([(acts_shared[half], shared_weight, 0)], None, jnp.float32),
                    ([(outs_shared[half], shared_weight, 2)], None, jnp.float32),
                ],
                waits,
            )
        )
        waits = [sums[-1][0]]
    factors = [
        jnp.sum(jnp.where(picked, route_probs[half] * chosen[half], 0.0), axis=1, keepdims=True)
        for half in halves
    ]
    outs_expert, acts_expert, d_expert = units_of(expert_weight, factors, waits)
    shard_shared = scatter_slab(grad_shared)
    d_routes, d_hidden_sums, block_sums = [], [None, None], [None, None]
    for half in halves:
        d_probs = jnp.where(picked, chosen[half] * d_expert[half], 0.0)
        d_logits = route_probs[half] * (
            d_probs - jnp.sum(route_probs[half] * d_probs, axis=1, keepdims=True)
        )
        d_gate_logit = d_shared[half] * (shared_prob[half] * (1.0 - shared_prob[half]))
        d_routes.append(jnp.concatenate([d_logits, d_gate_logit], axis=1))
    grad_in = grad_matmul([(hidden, acts_expert)], outs_expert[1:])
    waits = [grad_in, summed[0]]
    for half in (1, 0):
        products = [
            (acts_expert[half], expert_weight, 0),
            route_product(d_routes[half], route_mat),
        ]
        d_hidden_sums[half] = back_matmul([(products, sums[half][0], jnp.bfloat16)], waits)[0]
        waits = [d_hidden_sums[half], shard_shared]
    grad_out = grad_matmul([(cots, outs_expert)], waits)
    shard_in = scatter_slab(grad_in)
    shard_out = scatter_slab(grad_out)
    spread_shared = peer_gather(after(shard_shared, d_hidden_sums[:1]))
    d_route_mat = sum(
        [
            lax.dot_general(
                d_routes[half],
                wide(hidden[half]),
                (((0,), (0,)), ((), ())),
                precision=highest,
                preferred_element_type=jnp.float32,
            )
            for half in halves
        ]
    )
    d_route_mat = turn(d_route_mat)

    def pair_scatter(sums):
        theirs = to_mate(low(peer_scatter(token_pieces(sums[1]))), 2)
        return turn(peer_scatter(token_pieces(sums[0])) + wide(theirs))

    waits = [grad_out]
    for half in (1, 0):
        block_sums[half] = back_matmul(
            [([(outs_expert[half], expert_weight, 2)], sums[half][1], jnp.bfloat16)], waits
        )[0]
        waits = [block_sums[half]]
    d_hidden = pair_scatter(d_hidden_sums)
    cot_wide = wide(cotangent)
    d_gain_two = jnp.sum(d_hidden * unit_two, axis=0)
    d_resid = cot_wide + rms_back(d_hidden, unit_two, scale_two, gain_two)
    d_attn = low(d_resid)
    d_attn_pieces = by_rank(
        [d_attn[:, k * quarter : (k + 1) * quarter] for k in range(ctx_size)]
    )
    products = [(piece, weight, 0) for piece, weight in zip(d_attn_pieces, w_out_pieces)]
    d_vec_own = back_matmul([(products, None, jnp.bfloat16)], waits + spread_shared)[0]
    d_vec_pieces = by_rank(
        [d_vec_own[:, k * att_cols : (k + 1) * att_cols] for k in range(ctx_size)]
    )
    d_vec = jnp.concatenate(
        d_vec_pieces[:1] + [to_peer(d_vec_pieces[bits], bits) for bits in range(1, ctx_size)],
        axis=0,
    )
    grad_w_out = grad_matmul([([attn_vec], [d_attn])], [d_vec_own])
    grad_w_out_sum = scatter_fsdp(after(grad_w_out, summed[2:]))
    d_mixed = attend_back(split, places, log_total, d_vec, cos_table, sin_table, heads_own)
    grad_w_in = grad_matmul([([normed_all], [d_mixed])])
    d_bias = jnp.sum(wide(d_mixed), axis=0)
    d_normed_part = back_matmul(
        [([(d_mixed, w_in_own, 0)], None, jnp.bfloat16)], [grad_w_in]
    )[0]
    spread_in = peer_gather(after(shard_in, [d_normed_part]))
    grad_w_in = scatter_fsdp(grad_w_in)
    both_sums = [
        jnp.concatenate(pieces, axis=1)
        for pieces in zip(*[token_pieces(total) for total in [d_normed_part] + block_sums])
    ]
    both_sums = peer_scatter(both_sums)
    d_normed, block_own = both_sums[:, :D], both_sums[:, D : 2 * D]
    block_own = block_own + wide(to_mate(low(both_sums[:, 2 * D :]), 2))
    block_out = low(residual + turn(block_own))
    shared_totals = place_shared(spread_shared, sh_cols // 2, [d_normed_part])
    spread_out = peer_gather(after(shard_out, [d_normed_part]))
    if experts_own == 1:
        both = [jnp.concatenate(sides, axis=1) for sides in zip(spread_in, spread_out)]
        totals = ordered_sides(both, FE // 2)
        totals = [
            wide(jnp.transpose(totals[0], (2, 0, 1, 3)).reshape(EXPERTS, rows, 2 * FE)),
            wide(jnp.transpose(totals[1], (1, 0, 2))),
        ]
    else:
        totals = [place_experts(spread_in, [shared_totals[0]])]
        totals.append(place_experts(spread_out, totals))
    wide_all = wide(tokens_all)
    d_gain_one = jnp.sum(wide(d_normed_part) * (wide_all * rms_scale(wide_all)), axis=0)
    d_tokens = d_resid + rms_back(d_normed, unit_one, scale_one, gain_one)

    bias_spread = lax.dynamic_update_slice(
        jnp.zeros((3, D), jnp.float32), d_bias.reshape(3, att_cols), (0, ctx_rank * att_cols)
    )
    early_grads = total_sum(jnp.concatenate([d_route_mat.reshape(-1), d_gain_two]))
    late_grads = total_sum(jnp.concatenate([bias_spread.reshape(-1), d_gain_one]))

    def own_part(vector):
        size = vector.shape[0] // fsdp_size
        return lax.dynamic_slice_in_dim(vector, fsdp_rank * size, size)

    route_total = early_grads[: (EXPERTS + 1) * D].reshape(EXPERTS + 1, D)
    route_part = lax.dynamic_slice_in_dim(route_total, fsdp_rank * rows, rows, axis=1)
    return (
        block_out,
        d_tokens,
        own_part(late_grads[3 * D :]),
        place_cols(peer_gather(grad_w_in), 3, [totals[1]]),
        own_part(late_grads[: 3 * D]),
        peer_sum(grad_w_out_sum),
        own_part(early_grads[(EXPERTS + 1) * D :]),
        route_part[:EXPERTS].T,
        route_part[EXPERTS],
        *shared_totals,
        *totals,
    )


def solution(mesh):
    return jax.shard_map(
        per_device,
        mesh=mesh,
        in_specs=(
            P(("ctx", "fsdp"), None),
            P(("ctx", "fsdp"), None),
            P(),
            P("fsdp"),
            P("fsdp", None),
            P("fsdp"),
            P("fsdp", None),
            P("fsdp"),
            P("fsdp", None),
            P("fsdp"),
            P("fsdp", None),
            P("fsdp", None),
            P(None, "fsdp", None),
            P(None, "fsdp", None),
            P(("ctx", "fsdp"), None),
        ),
        out_specs=(
            P(("ctx", "fsdp"), None),
            P(("ctx", "fsdp"), None),
            P("fsdp"),
            P("fsdp", None),
            P("fsdp"),
            P("fsdp", None),
            P("fsdp"),
            P("fsdp", None),
            P("fsdp"),
            P("fsdp", None),
            P("fsdp", None),
            P(None, "fsdp", None),
            P(None, "fsdp", None),
        ),
        check_vma=False,
    )
```

```python
import functools

import jax
import jax.numpy as jnp
from jax import lax
from jax.experimental import pallas as pl
from jax.experimental.pallas import tpu as pltpu
from jax.sharding import PartitionSpec as P

D = 2048
HEADS = 16
HEAD_DIM = 128
FS = 5632
FE = 1408
EXPERTS = 8


norm_eps = 1e-06
rope_base = 1000000.0
highest = lax.Precision.HIGHEST


def rms_scale(values):
    return lax.rsqrt(jnp.mean(values * values, axis=1, keepdims=True) + norm_eps)


def rms_back(grad_rows, unit_rows, row_scale, gain_row):
    scaled = grad_rows * gain_row
    return row_scale * (scaled - unit_rows * jnp.mean(scaled * unit_rows, axis=1, keepdims=True))


def block_places(block_list, block_len):
    offsets = jnp.arange(block_len, dtype=jnp.int32)
    return (block_list[:, None] * block_len + offsets[None, :]).reshape(-1)


def rotary_tables(positions):
    half_dim = HEAD_DIM // 2
    inverse = rope_base ** (-2.0 * jnp.arange(half_dim, dtype=jnp.float32) / HEAD_DIM)
    angles = positions.astype(jnp.float32)[:, None] * inverse[None, :]
    cos_table = jnp.cos(angles)
    sin_table = jnp.sin(angles)
    return (
        jnp.concatenate([cos_table, cos_table], axis=1),
        jnp.concatenate([sin_table, sin_table], axis=1),
    )


def rotate(values, cos_table, sin_table):
    half_dim = HEAD_DIM // 2
    turned = jnp.concatenate([-values[..., half_dim:], values[..., :half_dim]], axis=-1)
    return values * cos_table[:, None, :] + turned * sin_table[:, None, :]


def unrotate(values, cos_table, sin_table):
    half_dim = HEAD_DIM // 2
    scaled = values * sin_table[:, None, :]
    turned = jnp.concatenate([scaled[..., half_dim:], -scaled[..., :half_dim]], axis=-1)
    return values * cos_table[:, None, :] + turned


def swiglu(activation, breadth):
    return jax.nn.silu(activation[:, :breadth]) * activation[:, breadth:]


def swiglu_back(grad_hidden, activation, breadth):
    gate_part = activation[:, :breadth]
    up_part = activation[:, breadth:]
    sig_gate = jax.nn.sigmoid(gate_part)
    d_gate = grad_hidden * up_part * sig_gate * (1.0 + gate_part * (1.0 - sig_gate))
    d_up = grad_hidden * gate_part * sig_gate
    return jnp.concatenate([d_gate, d_up], axis=1)


def outer_rows(left_ops, right_ops):
    pieces = []
    for left_op, right_op in zip(left_ops, right_ops):
        pieces.append(
            lax.dot_general(
                left_op, right_op, (((0,), (0,)), ((), ())), preferred_element_type=jnp.float32
            )
        )
    return jnp.concatenate(pieces, axis=1)


def right_product(left_op, right_op):
    return lax.dot_general(
        left_op, right_op, (((1,), (1,)), ((), ())), preferred_element_type=jnp.float32
    )


def to_peer(array, bits):
    size = lax.axis_size("ctx")
    return lax.ppermute(array, "ctx", [(rank, rank ^ bits) for rank in range(size)])


def peer_gather(array, direct=False):
    size = lax.axis_size("ctx")
    if size != 4 or direct:
        return [array] + [to_peer(array, bits) for bits in range(1, size)]
    half = array.shape[0] // 2
    one, two = to_peer(array, 1), to_peer(array, 2)
    three = jnp.concatenate([to_peer(one[:half], 2), to_peer(two[half:], 1)], axis=0)
    return [array, one, two, three]


def wide(array):
    return array.astype(jnp.float32)


def low(array):
    return array.astype(jnp.bfloat16)


def peer_scatter(pieces):
    size = lax.axis_size("ctx")
    pieces = [low(piece) for piece in pieces]
    if size != 4:
        total = wide(pieces[0])
        for bits in range(1, size):
            total = total + wide(to_peer(pieces[bits], bits))
        return total
    half = pieces[0].shape[0] // 2
    first = to_peer(jnp.concatenate([pieces[1][:half], pieces[3][:half]], axis=0), 1)
    second = to_peer(jnp.concatenate([pieces[2][half:], pieces[3][half:]], axis=0), 2)
    upper = to_peer(low(wide(pieces[2][:half]) + wide(first[half:])), 2)
    lower = to_peer(low(wide(pieces[1][half:]) + wide(second[half:])), 1)
    return wide(pieces[0]) + jnp.concatenate(
        [wide(first[:half]) + wide(upper), wide(second[:half]) + wide(lower)], axis=0
    )


def peer_sum(array):
    size, half = lax.axis_size("ctx"), array.shape[0] // 2
    upper, lower, bits = array[:half], array[half:], 1
    while bits < size:
        upper, lower = low(upper), low(lower)
        other = size // 2 // bits
        upper = wide(upper) + wide(to_peer(upper, bits))
        lower = wide(lower) + wide(to_peer(lower, other))
        bits *= 2
    return jnp.concatenate([upper, lower], axis=0)


def by_rank(pieces):
    rank, bits = lax.axis_index("ctx"), 1
    while bits < len(pieces):
        odd = (rank & bits) != 0
        pieces = [jnp.where(odd, pieces[k ^ bits], pieces[k]) for k in range(len(pieces))]
        bits *= 2
    return pieces


def to_mate(array, bits):
    size = lax.axis_size("fsdp")
    return lax.ppermute(array, "fsdp", [(rank, rank ^ bits) for rank in range(size)])


def total_sum(array):
    bits = 1
    while bits < lax.axis_size("fsdp"):
        array = array + to_mate(array, bits)
        bits *= 2
    bits = 1
    while bits < lax.axis_size("ctx"):
        array = array + to_peer(array, bits)
        bits *= 2
    return array


VMEM_BYTES = 56 * 1024 * 1024


def own_call(kernel, name, grid, ins, in_specs, outs, out_specs, flops, waits=(), order=None, aliases=None):
    lead = 0 if order is None else 1
    count = len(ins)

    def body(*refs):
        kernel(*refs[lead : lead + count], *refs[lead + count + len(waits) :])

    moved = sum(array.size * array.dtype.itemsize for array in [*ins, *outs])
    return pl.pallas_call(
        body,
        out_shape=list(outs),
        grid_spec=pltpu.PrefetchScalarGridSpec(
            num_scalar_prefetch=lead,
            grid=grid,
            in_specs=list(in_specs) + [pl.BlockSpec(memory_space=pl.ANY)] * len(waits),
            out_specs=list(out_specs),
        ),
        compiler_params=pltpu.CompilerParams(vmem_limit_bytes=VMEM_BYTES),
        cost_estimate=pl.CostEstimate(flops=flops, transcendentals=0, bytes_accessed=moved),
        input_output_aliases=aliases or {},
        name=name,
    )(*([] if order is None else [order]), *ins, *waits)


def after(array, waits):
    waits = [wait for wait in waits if wait is not None]
    if not waits:
        return array
    return pl.pallas_call(
        lambda *refs: None,
        out_shape=jax.ShapeDtypeStruct(array.shape, array.dtype),
        in_specs=[pl.BlockSpec(memory_space=pl.ANY)] * (1 + len(waits)),
        out_specs=pl.BlockSpec(memory_space=pl.ANY),
        input_output_aliases={0: 0},
        name="after",
    )(array, *waits)


def unit_backward(rows_in, rows_grad, weight, factor, waits=()):
    rows, depth = rows_in.shape
    breadth = weight.shape[1] // 3
    if breadth % 128:
        act = jnp.dot(rows_in, weight[:, : 2 * breadth], preferred_element_type=jnp.float32)
        d_unit = jnp.dot(rows_grad, weight[:, 2 * breadth :], preferred_element_type=jnp.float32)
        units = swiglu(act, breadth)
        return (
            low(factor * units),
            low(swiglu_back(factor * d_unit, act, breadth)),
            jnp.sum(d_unit * units, axis=1, keepdims=True),
        )
    tall = min(rows, 256)

    def kernel(rows_ref, grad_ref, weight_ref, factor_ref, out_ref, d_act_ref, d_factor_ref):
        scale = factor_ref[...]
        total = jnp.zeros((tall, 1), jnp.float32)
        for start in range(0, breadth, 256):
            gate = slice(start, min(start + 256, breadth))
            up = slice(breadth + gate.start, breadth + gate.stop)
            down = slice(2 * breadth + gate.start, 2 * breadth + gate.stop)
            gate_part = jnp.dot(
                rows_ref[...], weight_ref[:, gate], preferred_element_type=jnp.float32
            )
            up_part = jnp.dot(rows_ref[...], weight_ref[:, up], preferred_element_type=jnp.float32)
            d_unit = jnp.dot(grad_ref[...], weight_ref[:, down], preferred_element_type=jnp.float32)
            sig_gate = jax.nn.sigmoid(gate_part)
            silu = gate_part * sig_gate
            units = silu * up_part
            total = total + jnp.sum(d_unit * units, axis=1, keepdims=True)
            out_ref[:, gate] = low(scale * units)
            scaled = scale * d_unit
            d_act_ref[:, gate] = low(scaled * up_part * (sig_gate + silu * (1.0 - sig_gate)))
            d_act_ref[:, up] = low(scaled * silu)
        d_factor_ref[...] = total

    return own_call(
        kernel,
        "unit_backward",
        (rows // tall,),
        [rows_in, rows_grad, weight, factor],
        [
            pl.BlockSpec((tall, depth), lambda i: (i, 0)),
            pl.BlockSpec((tall, depth), lambda i: (i, 0)),
            pl.BlockSpec((depth, 3 * breadth), lambda i: (0, 0)),
            pl.BlockSpec((tall, 1), lambda i: (i, 0)),
        ],
        [
            jax.ShapeDtypeStruct((rows, breadth), jnp.bfloat16),
            jax.ShapeDtypeStruct((rows, 2 * breadth), jnp.bfloat16),
            jax.ShapeDtypeStruct((rows, 1), jnp.float32),
        ],
        [
            pl.BlockSpec((tall, breadth), lambda i: (i, 0)),
            pl.BlockSpec((tall, 2 * breadth), lambda i: (i, 0)),
            pl.BlockSpec((tall, 1), lambda i: (i, 0)),
        ],
        6 * rows * depth * breadth,
        waits,
    )


def back_matmul(jobs, waits=()):
    rows, breadth = jobs[0][0][0][0].shape[0], jobs[0][0][0][1].shape[0]
    tile = 256
    ins, specs, flops = [], [], 0
    for products, total, dtype in jobs:
        for rows_in, weight, column in products:
            depth = rows_in.shape[1]
            if depth % 128 and weight.shape[1] != depth:
                weight = weight[:, column * depth : (column + 1) * depth]
                column = 0
            ins += [rows_in, weight]
            specs += [
                pl.BlockSpec((rows, depth), lambda j: (0, 0)),
                pl.BlockSpec((tile, depth), lambda j, column=column: (j, column)),
            ]
            flops += 2 * rows * depth * breadth
        if total is not None:
            ins.append(total)
            specs.append(pl.BlockSpec((rows, tile), lambda j: (0, j)))

    def kernel(*refs):
        used = 0
        for out, (products, total, dtype) in enumerate(jobs):
            value = None
            for _ in products:
                part = right_product(refs[used][...], refs[used + 1][...])
                value = part if value is None else value + part
                used += 2
            if total is not None:
                value = value + wide(refs[used][...])
                used += 1
            refs[len(ins) + out][...] = value.astype(dtype)

    return own_call(
        kernel,
        "back_matmul",
        (breadth // tile,),
        ins,
        specs,
        [jax.ShapeDtypeStruct((rows, breadth), dtype) for products, total, dtype in jobs],
        [pl.BlockSpec((rows, tile), lambda j: (0, j))] * len(jobs),
        flops,
        waits,
    )


def route_product(d_route, route_mat):
    coarse = low(d_route)
    fine = low(d_route - wide(coarse))
    both = low(jnp.concatenate([route_mat, route_mat], axis=1))
    return (jnp.concatenate([coarse, fine], axis=1), both, 0)


def grad_matmul(pairs, waits=()):
    blocks = lax.axis_size("fsdp")
    depth = pairs[0][0][0].shape[1]
    widths = [rights[0].shape[1] for lefts, rights in pairs]
    total, block = sum(widths), depth // blocks
    ins, specs, flops = [], [], 0
    for lefts, rights in pairs:
        for left, right in zip(lefts, rights):
            ins += [left, right]
            specs += [
                pl.BlockSpec((left.shape[0], block), lambda j: (0, j)),
                pl.BlockSpec(right.shape, lambda j: (0, 0)),
            ]
            flops += 2 * left.shape[0] * depth * right.shape[1]

    def kernel(*refs):
        start, used = 0, 0
        for (lefts, rights), width in zip(pairs, widths):
            value = None
            for _ in lefts:
                part = lax.dot_general(
                    refs[used][...],
                    refs[used + 1][...],
                    (((0,), (0,)), ((), ())),
                    preferred_element_type=jnp.float32,
                )
                value = part if value is None else value + part
                used += 2
            refs[-1][:, start : start + width] = low(value)
            start += width

    return own_call(
        kernel,
        "grad_matmul",
        (blocks,),
        ins,
        specs,
        [jax.ShapeDtypeStruct((depth, total), jnp.bfloat16)],
        [pl.BlockSpec((block, total), lambda j: (j, 0))],
        flops,
        waits,
    )[0]


def split_matmul(rows_in, gain, weight, bias, cos_table, sin_table, waits=()):
    rows, depth = rows_in.shape
    breadth = bias.shape[0]
    tile = 256
    turned = breadth * 2 // 3 // tile
    tall = min(rows, 256)

    def kernel(rows_ref, gain_ref, weight_ref, bias_ref, cos_ref, sin_ref, normed_ref, out_ref):
        @pl.when(pl.program_id(0) == 0)
        def _():
            for start in range(0, rows, tall):
                some = slice(start, start + tall)
                values = wide(rows_ref[some, :])
                normed_ref[some, :] = low(values * rms_scale(values) * gain_ref[...])

        value = jnp.dot(normed_ref[...], weight_ref[...], preferred_element_type=jnp.float32)
        value = value + bias_ref[...]

        @pl.when(pl.program_id(0) < turned)
        def _():
            for start in range(0, tile, HEAD_DIM):
                head = value[:, start : start + HEAD_DIM]
                head = head * cos_ref[...] + pltpu.roll(head, HEAD_DIM // 2, 1) * sin_ref[...]
                out_ref[:, start : start + HEAD_DIM] = low(head)

        @pl.when(pl.program_id(0) >= turned)
        def _():
            out_ref[...] = low(value)

    whole = pl.BlockSpec((rows, depth), lambda j: (0, 0))
    table = pl.BlockSpec((rows, HEAD_DIM), lambda j: (0, 0))
    return own_call(
        kernel,
        "split_matmul",
        (breadth // tile,),
        [rows_in, gain.reshape(1, depth), weight, bias.reshape(1, breadth), cos_table, sin_table],
        [
            whole,
            pl.BlockSpec((1, depth), lambda j: (0, 0)),
            pl.BlockSpec((depth, tile), lambda j: (0, j)),
            pl.BlockSpec((1, tile), lambda j: (0, j)),
            table,
            table,
        ],
        [
            jax.ShapeDtypeStruct((rows, depth), jnp.bfloat16),
            jax.ShapeDtypeStruct((rows, breadth), jnp.bfloat16),
        ],
        [whole, pl.BlockSpec((rows, tile), lambda j: (0, j))],
        2 * rows * depth * breadth,
        waits,
    )


def head_specs(rows, heads):
    return [
        pl.BlockSpec((rows, HEAD_DIM), lambda h, part=part: (0, part * heads + h))
        for part in range(3)
    ]


def attend(split, places, heads, waits=()):
    rows = split.shape[0]
    tall = min(rows, 256)
    scale = HEAD_DIM ** (-0.5)

    def kernel(query_ref, key_ref, value_ref, down_ref, across_ref, out_ref, log_ref):
        for start in range(0, rows, tall):
            some = slice(start, start + tall)
            scores = right_product(query_ref[some, :], key_ref[...]) * scale
            scores = jnp.where(across_ref[...] <= down_ref[some, :], scores, -1e30)
            top = jnp.max(scores, axis=1, keepdims=True)
            exponent = jnp.exp(scores - top)
            total = jnp.sum(exponent, axis=1, keepdims=True)
            prob = low(exponent * (1.0 / total))
            out_ref[some, :] = low(
                jnp.dot(prob, value_ref[...], preferred_element_type=jnp.float32)
            )
            log_ref[some, :] = top + jnp.log(total)

    return own_call(
        kernel,
        "attend",
        (heads,),
        [split, split, split, places.reshape(rows, 1), places.reshape(1, rows)],
        head_specs(rows, heads)
        + [
            pl.BlockSpec((rows, 1), lambda h: (0, 0)),
            pl.BlockSpec((1, rows), lambda h: (0, 0)),
        ],
        [
            jax.ShapeDtypeStruct((rows, heads * HEAD_DIM), jnp.bfloat16),
            jax.ShapeDtypeStruct((heads, rows, 1), jnp.float32),
        ],
        [
            pl.BlockSpec((rows, HEAD_DIM), lambda h: (0, h)),
            pl.BlockSpec((None, rows, 1), lambda h: (h, 0, 0)),
        ],
        4 * rows * rows * heads * HEAD_DIM,
        waits,
    )


def attend_back(split, places, log_total, d_vec, cos_table, sin_table, heads, waits=()):
    rows = split.shape[0]
    tall = min(rows, 256)
    scale = HEAD_DIM ** (-0.5)

    def kernel(query_ref, key_ref, value_ref, down_ref, across_ref, log_ref, grad_ref, cos_ref, sin_ref, out_ref):
        first = pl.multiple_of(pl.program_id(0) * HEAD_DIM, HEAD_DIM)
        d_key = jnp.zeros((rows, HEAD_DIM), jnp.float32)
        d_value = jnp.zeros((rows, HEAD_DIM), jnp.float32)

        def unturned(grad, some):
            return low(
                grad * cos_ref[some, :]
                - pltpu.roll(grad, HEAD_DIM // 2, 1) * sin_ref[some, :]
            )

        def columns(part):
            return pl.ds(first + part * heads * HEAD_DIM, HEAD_DIM)

        for start in range(0, rows, tall):
            some = slice(start, start + tall)
            query, grad = query_ref[some, :], grad_ref[some, :]
            scores = right_product(query, key_ref[...]) * scale
            prob = jnp.where(
                across_ref[...] <= down_ref[some, :], jnp.exp(scores - log_ref[some, :]), 0.0
            )
            d_prob = right_product(grad, value_ref[...])
            inner = jnp.sum(prob * d_prob, axis=1, keepdims=True)
            d_score = low(prob * (d_prob - inner) * scale)
            across = (((0,), (0,)), ((), ()))
            d_value = d_value + lax.dot_general(
                low(prob), grad, across, preferred_element_type=jnp.float32
            )
            d_key = d_key + lax.dot_general(
                d_score, query, across, preferred_element_type=jnp.float32
            )
            d_query = jnp.dot(d_score, key_ref[...], preferred_element_type=jnp.float32)
            out_ref[some, columns(0)] = unturned(d_query, some)
        out_ref[:, columns(1)] = unturned(d_key, slice(0, rows))
        out_ref[:, columns(2)] = low(d_value)

    table = pl.BlockSpec((rows, HEAD_DIM), lambda h: (0, 0))
    return own_call(
        kernel,
        "attend_back",
        (heads,),
        [split, split, split, places.reshape(rows, 1), places.reshape(1, rows), log_total, d_vec]
        + [cos_table, sin_table],
        head_specs(rows, heads)
        + [
            pl.BlockSpec((rows, 1), lambda h: (0, 0)),
            pl.BlockSpec((1, rows), lambda h: (0, 0)),
            pl.BlockSpec((None, rows, 1), lambda h: (h, 0, 0)),
            pl.BlockSpec((rows, HEAD_DIM), lambda h: (0, h)),
            table,
            table,
        ],
        [jax.ShapeDtypeStruct((rows, 3 * heads * HEAD_DIM), jnp.bfloat16)],
        [pl.BlockSpec((rows, 3 * heads * HEAD_DIM), lambda h: (0, 0))],
        10 * rows * rows * heads * HEAD_DIM,
        waits,
    )[0]


def place_grads(spread, slot, slots, totals, waits=()):
    size, rows = len(spread[0][0]), spread[0][0][0].shape[0]
    units = sum([sum(parts) for pieces, parts in spread])
    if units % 128:
        ordered = by_rank(spread[0][0])
        sides = [
            jnp.stack([piece[:, k * units : (k + 1) * units] for piece in ordered], axis=1)
            for k in range(3)
        ]
        into = jnp.stack(sides[:2], axis=1).reshape(rows, 2 * size * units)
        return wide(into), wide(sides[2].reshape(rows, size * units))
    tall = min(rows, 64)
    columns = 2 if slot is None else 1
    pieces = [held[k] for k in range(size) for held, parts in spread]
    onto = [] if totals is None else list(totals)
    rest = list(waits) + onto
    steps = rows // tall

    def kernel(*refs):
        in_ref, out_ref = refs[-2:]
        for k in range(size):

            @pl.when(pl.program_id(0) == k)
            def _():
                used = refs[k * len(spread) : (k + 1) * len(spread)]
                place = 0
                for (held, parts), ref in zip(spread, used):
                    start = 0
                    for part in parts:
                        gate = ref[:, start : start + part]
                        up = ref[:, start + part : start + 2 * part]
                        if slot is None:
                            here = pl.program_id(2) == 0
                            in_ref[:, place : place + part] = wide(jnp.where(here, gate, up))
                        else:
                            in_ref[:, place : place + part] = wide(gate)
                            in_ref[:, units + place : units + place + part] = wide(up)
                        out_ref[:, place : place + part] = wide(
                            ref[:, start + 2 * part : start + 3 * part]
                        )
                        place += part
                        start += 3 * part

    def piece_spec(k, parts):
        def piece_map(step, row, column, rank_ref):
            return (jnp.where(step == k, row, jnp.where(step < k, 0, steps - 1)), 0)

        return pl.BlockSpec((tall, 3 * sum(parts)), piece_map)

    if slot is None:
        shapes = [(rows, 2 * size * units), (rows, size * units)]
        out_specs = [
            pl.BlockSpec(
                (tall, units),
                lambda k, row, column, rank_ref: (row, column * size + (rank_ref[0] ^ k)),
            ),
            pl.BlockSpec((tall, units), lambda k, row, column, rank_ref: (row, rank_ref[0] ^ k)),
        ]
    else:
        shapes = [(size * slots, rows, 2 * units), (size * slots, rows, units)]
        out_specs = [
            pl.BlockSpec(
                (None, tall, shape[2]),
                lambda k, row, column, rank_ref: ((rank_ref[0] ^ k) * slots + slot, row, 0),
            )
            for shape in shapes
        ]
    first = 1 + len(pieces) + len(waits)
    return own_call(
        kernel,
        "place_grads",
        (size, steps, columns),
        pieces,
        [piece_spec(k, parts) for k in range(size) for held, parts in spread],
        [jax.ShapeDtypeStruct(shape, jnp.float32) for shape in shapes],
        out_specs,
        0,
        rest,
        lax.axis_index("ctx").reshape(1),
        aliases={first: 0, first + 1: 1} if onto else {},
    )


def place_cols(pieces, parts, waits=()):
    size, rows = len(pieces), pieces[0].shape[0]
    breadth = pieces[0].shape[1] // parts
    if breadth % 128:
        ordered = [piece.reshape(rows, parts, breadth) for piece in by_rank(pieces)]
        return wide(jnp.stack(ordered, axis=2).reshape(rows, parts * size * breadth))

    def kernel(*refs):
        for k, ref in enumerate(refs[:-1]):

            @pl.when(pl.program_id(0) == k)
            def _():
                refs[-1][...] = wide(ref[...])

    def piece_spec(own):
        def piece_map(k, part, rank_ref):
            return (0, jnp.where(k == own, part, jnp.where(k < own, 0, parts - 1)))

        return pl.BlockSpec((rows, breadth), piece_map)

    return own_call(
        kernel,
        "place_cols",
        (size, parts),
        pieces,
        [piece_spec(own) for own in range(size)],
        [jax.ShapeDtypeStruct((rows, parts * size * breadth), jnp.float32)],
        [
            pl.BlockSpec(
                (rows, breadth), lambda k, part, rank_ref: (0, part * size + (rank_ref[0] ^ k))
            )
        ],
        0,
        waits,
        lax.axis_index("ctx").reshape(1),
    )[0]

def per_device(
    tokens,
    routes,
    block_ids,
    attn_gain,
    w_attn_in,
    b_qkv,
    w_attn_out,
    ffn_gain,
    router,
    shared_gate,
    w_sh_in,
    w_sh_out,
    w_exp_in,
    w_exp_out,
    cotangent,
):
    ctx_size = lax.axis_size("ctx")
    fsdp_size = lax.axis_size("fsdp")
    ctx_rank = lax.axis_index("ctx")
    fsdp_rank = lax.axis_index("fsdp")
    tok_rows = tokens.shape[0]
    block_len = tok_rows // 2
    seq_len = tok_rows * ctx_size
    heads_own = HEADS // ctx_size
    att_cols = heads_own * HEAD_DIM
    sh_cols = FS // ctx_size
    experts_own = EXPERTS // ctx_size

    def own_cols(array, start, breadth):
        return lax.dynamic_slice_in_dim(array, start + ctx_rank * breadth, breadth, axis=1)

    def gather_fsdp(array):
        return lax.all_gather(array, "fsdp", axis=0, tiled=True)

    def scatter_fsdp(array):
        return lax.psum_scatter(
            array.astype(jnp.bfloat16), "fsdp", scatter_dimension=0, tiled=True
        )

    def token_pieces(array):
        return [array[k * tok_rows : (k + 1) * tok_rows] for k in range(ctx_size)]

    tokens_all = jnp.concatenate(peer_gather(tokens), axis=0)
    quarter = D // ctx_size
    w_out_own = gather_fsdp(own_cols(w_attn_out, 0, quarter))
    w_out_pieces = peer_gather(w_out_own)
    rows = attn_gain.shape[0]
    smalls = jnp.concatenate(
        [jnp.stack([attn_gain, ffn_gain, shared_gate], axis=1), router, b_qkv.reshape(3, rows).T],
        axis=1,
    )
    smalls = jnp.pad(smalls, ((0, 0), (0, 128 - smalls.shape[1])))
    w_in_slab = jnp.concatenate(
        [own_cols(w_attn_in, part * D, att_cols) for part in range(3)] + [smalls], axis=1
    )
    w_in_own = gather_fsdp(after(w_in_slab, [w_out_own]))
    smalls_all = w_in_own[:, 3 * att_cols :]
    gain_one, gain_two, gate_vec = [wide(smalls_all[:, k]) for k in range(3)]
    router_wide = wide(smalls_all[:, 3 : 3 + EXPERTS])
    bias_full = smalls_all[:, 3 + EXPERTS : 6 + EXPERTS].reshape(fsdp_size, rows, 3)
    bias_full = jnp.transpose(bias_full, (0, 2, 1)).reshape(3, D)
    bias_own = wide(own_cols(bias_full, 0, att_cols)).reshape(3 * att_cols)

    slabs = [
        [own_cols(w_sh_in, part * FS, sh_cols) for part in range(2)]
        + [own_cols(w_sh_out, 0, sh_cols)]
    ]
    for own in range(experts_own):
        expert = ctx_rank * experts_own + own
        slabs.append([w_exp_in[expert, :, :FE], w_exp_in[expert, :, FE:], w_exp_out[expert]])
    slabs = [jnp.concatenate(sides, axis=1) for sides in slabs]

    inputs = wide(tokens)
    scale_one = rms_scale(inputs)
    unit_one = inputs * scale_one
    ranks = ctx_rank ^ jnp.arange(ctx_size, dtype=jnp.int32)
    places = block_places(block_ids.reshape(ctx_size, 2)[ranks].reshape(-1), block_len)
    cos_table, sin_table = rotary_tables(places)
    half = HEAD_DIM // 2
    sin_table = jnp.concatenate([-sin_table[:, :half], sin_table[:, half:]], axis=1)
    normed_all, split = split_matmul(
        tokens_all, gain_one, w_in_own, bias_own, cos_table, sin_table
    )
    attended, log_total = attend(split, places, heads_own, w_out_pieces)
    head_pieces = token_pieces(attended)
    head_pieces = head_pieces[:1] + [
        to_peer(head_pieces[bits], bits) for bits in range(1, ctx_size)
    ]
    attn_vec = jnp.concatenate(by_rank(head_pieces), axis=1)
    attn_out = [
        jnp.dot(attn_vec, piece, preferred_element_type=jnp.float32) for piece in w_out_pieces
    ]
    residual = inputs + jnp.concatenate(by_rank(attn_out), axis=1)

    scale_two = rms_scale(residual)
    unit_two = residual * scale_two
    cots = [jnp.concatenate(peer_gather(after(cotangent, [split])), axis=0)]
    hidden_in = low(unit_two * gain_two)
    hidden = [jnp.concatenate(peer_gather(hidden_in), axis=0)]
    route_mat = jnp.concatenate([router_wide, gate_vec[:, None]], axis=1)
    expert_ids = jnp.arange(EXPERTS, dtype=jnp.int32)
    logits = jnp.dot(
        wide(hidden[0]), route_mat, precision=highest, preferred_element_type=jnp.float32
    )
    route_probs = jax.nn.softmax(logits[:, :EXPERTS], axis=1)
    shared_prob = jax.nn.sigmoid(logits[:, EXPERTS:])
    routes_all = jnp.concatenate(
        [routes] + [to_peer(routes, bits) for bits in range(1, ctx_size)], axis=0
    )
    chosen = wide(jnp.any(routes_all[:, :, None] == expert_ids[None, None, :], axis=1))

    weights = [
        gather_fsdp(after(slab, [wait]))
        for slab, wait in zip(slabs, (w_in_own, split, attended))
    ]
    d_probs = jnp.zeros((seq_len, EXPERTS), jnp.float32)
    sums, waits, grads = [None, None], [], []
    for index, weight in enumerate(weights):
        own = index - 1
        if own < 0:
            factor = shared_prob
        else:
            picked = (expert_ids == ctx_rank * experts_own + own)[None, :]
            factor = jnp.sum(
                jnp.where(picked, route_probs * chosen, 0.0), axis=1, keepdims=True
            )
        scaled_out, d_act, d_factor = unit_backward(hidden[0], cots[0], weight, factor, waits)
        if own < 0:
            d_gate_logit = d_factor * (shared_prob * (1.0 - shared_prob))
        else:
            d_probs = d_probs + jnp.where(picked, chosen * d_factor, 0.0)
        waits = [scaled_out]
        products, outward = [(d_act, weight, 0)], [(scaled_out, weight, 2)]
        if index == len(weights) - 1:
            d_logits = route_probs * (
                d_probs - jnp.sum(route_probs * d_probs, axis=1, keepdims=True)
            )
            d_route = jnp.concatenate([d_logits, d_gate_logit], axis=1)
            products.append(route_product(d_route, route_mat))
            d_hidden_sum = back_matmul([(products, sums[0], jnp.bfloat16)], waits)[0]
            waits = [d_hidden_sum]
        grads.append(grad_matmul([(hidden, [d_act]), (cots, [scaled_out])], waits))
        waits = [grads[-1]]
        if index < len(weights) - 1:
            sums = back_matmul(
                [(products, sums[0], jnp.float32), (outward, sums[1], jnp.float32)], waits
            )
            waits = [sums[0]]
    block_sum = back_matmul([(outward, sums[1], jnp.bfloat16)], waits)[0]
    waits = [block_sum]
    shards = [scatter_fsdp(grad) for grad in grads]
    d_route_mat = lax.dot_general(
        d_route,
        wide(hidden[0]),
        (((0,), (0,)), ((), ())),
        precision=highest,
        preferred_element_type=jnp.float32,
    )
    d_hidden = peer_scatter(token_pieces(d_hidden_sum))
    cot_wide = wide(cotangent)
    d_gain_two = jnp.sum(d_hidden * unit_two, axis=0)
    d_resid = cot_wide + rms_back(d_hidden, unit_two, scale_two, gain_two)
    d_attn = low(d_resid)
    d_attn_pieces = by_rank(
        [d_attn[:, k * quarter : (k + 1) * quarter] for k in range(ctx_size)]
    )
    products = [(piece, weight, 0) for piece, weight in zip(d_attn_pieces, w_out_pieces)]
    d_vec_own = back_matmul([(products, None, jnp.bfloat16)], waits)[0]
    d_vec_pieces = by_rank(
        [d_vec_own[:, k * att_cols : (k + 1) * att_cols] for k in range(ctx_size)]
    )
    d_vec = jnp.concatenate(
        d_vec_pieces[:1] + [to_peer(d_vec_pieces[bits], bits) for bits in range(1, ctx_size)],
        axis=0,
    )
    grad_w_out = grad_matmul(
        [([attn_vec], [jnp.concatenate(d_attn_pieces, axis=1)])], [d_vec_own]
    )
    grad_w_out = peer_scatter(
        [grad_w_out[:, k * quarter : (k + 1) * quarter] for k in range(ctx_size)]
    )
    grad_w_out = scatter_fsdp(grad_w_out)
    d_mixed = attend_back(split, places, log_total, d_vec, cos_table, sin_table, heads_own)
    grad_w_in = grad_matmul([([normed_all], [d_mixed])])
    d_bias = jnp.sum(wide(d_mixed), axis=0)
    d_normed_part = back_matmul(
        [([(d_mixed, w_in_own, 0)], None, jnp.bfloat16)], [grad_w_in]
    )[0]
    grad_w_in = scatter_fsdp(grad_w_in)
    d_normed = peer_scatter(token_pieces(d_normed_part))
    block_out = low(residual + peer_scatter(token_pieces(after(block_sum, [d_mixed]))))
    units, totals, waits = [sh_cols] + [FE] * experts_own, None, [d_normed_part]
    for own, shard in zip(range(-1, experts_own), shards):
        spread = [(peer_gather(after(shard, waits)), units[:1] if own < 0 else units[1:2])]
        if own < 0:
            shared_totals = place_grads(spread, None, 1, None, waits)
            waits = [shared_totals[0]]
        else:
            totals = place_grads(spread, own, experts_own, totals, waits)
    wide_all = wide(tokens_all)
    d_gain_one = jnp.sum(wide(d_normed_part) * (wide_all * rms_scale(wide_all)), axis=0)
    d_tokens = d_resid + rms_back(d_normed, unit_one, scale_one, gain_one)

    bias_spread = lax.dynamic_update_slice(
        jnp.zeros((3, D), jnp.float32), d_bias.reshape(3, att_cols), (0, ctx_rank * att_cols)
    )
    early_grads = total_sum(jnp.concatenate([d_route_mat.reshape(-1), d_gain_two]))
    late_grads = total_sum(jnp.concatenate([bias_spread.reshape(-1), d_gain_one]))

    def own_part(vector):
        size = vector.shape[0] // fsdp_size
        return lax.dynamic_slice_in_dim(vector, fsdp_rank * size, size)

    route_total = early_grads[: (EXPERTS + 1) * D].reshape(EXPERTS + 1, D)
    route_part = lax.dynamic_slice_in_dim(route_total, fsdp_rank * rows, rows, axis=1)
    return (
        block_out,
        d_tokens,
        own_part(late_grads[3 * D :]),
        place_cols(peer_gather(grad_w_in), 3, [totals[1]]),
        own_part(late_grads[: 3 * D]),
        wide(jnp.concatenate(by_rank(peer_gather(after(grad_w_out, totals[:1]))), axis=1)),
        own_part(early_grads[(EXPERTS + 1) * D :]),
        route_part[:EXPERTS].T,
        route_part[EXPERTS],
        *shared_totals,
        *totals,
    )


def solution(mesh):
    return jax.shard_map(
        per_device,
        mesh=mesh,
        in_specs=(
            P(("ctx", "fsdp"), None),
            P(("ctx", "fsdp"), None),
            P(),
            P("fsdp"),
            P("fsdp", None),
            P("fsdp"),
            P("fsdp", None),
            P("fsdp"),
            P("fsdp", None),
            P("fsdp"),
            P("fsdp", None),
            P("fsdp", None),
            P(None, "fsdp", None),
            P(None, "fsdp", None),
            P(("ctx", "fsdp"), None),
        ),
        out_specs=(
            P(("ctx", "fsdp"), None),
            P(("ctx", "fsdp"), None),
            P("fsdp"),
            P("fsdp", None),
            P("fsdp"),
            P("fsdp", None),
            P("fsdp"),
            P("fsdp", None),
            P("fsdp"),
            P("fsdp", None),
            P("fsdp", None),
            P(None, "fsdp", None),
            P(None, "fsdp", None),
        ),
        check_vma=False,
    )
```

```python
import functools

import jax
import jax.numpy as jnp
from jax import lax
from jax.experimental import pallas as pl
from jax.experimental.pallas import tpu as pltpu
from jax.sharding import PartitionSpec as P

D = 2048
HEADS = 16
HEAD_DIM = 128
FS = 5632
FE = 1408
EXPERTS = 8


norm_eps = 1e-06
rope_base = 1000000.0
highest = lax.Precision.HIGHEST


def rms_scale(values):
    return lax.rsqrt(jnp.mean(values * values, axis=1, keepdims=True) + norm_eps)


def rms_back(grad_rows, unit_rows, row_scale, gain_row):
    scaled = grad_rows * gain_row
    return row_scale * (scaled - unit_rows * jnp.mean(scaled * unit_rows, axis=1, keepdims=True))


def block_places(block_list, block_len):
    offsets = jnp.arange(block_len, dtype=jnp.int32)
    return (block_list[:, None] * block_len + offsets[None, :]).reshape(-1)


def rotary_tables(positions):
    half_dim = HEAD_DIM // 2
    inverse = rope_base ** (-2.0 * jnp.arange(half_dim, dtype=jnp.float32) / HEAD_DIM)
    angles = positions.astype(jnp.float32)[:, None] * inverse[None, :]
    cos_table = jnp.cos(angles)
    sin_table = jnp.sin(angles)
    return (
        jnp.concatenate([cos_table, cos_table], axis=1),
        jnp.concatenate([sin_table, sin_table], axis=1),
    )


def rotate(values, cos_table, sin_table):
    half_dim = HEAD_DIM // 2
    turned = jnp.concatenate([-values[..., half_dim:], values[..., :half_dim]], axis=-1)
    return values * cos_table[:, None, :] + turned * sin_table[:, None, :]


def unrotate(values, cos_table, sin_table):
    half_dim = HEAD_DIM // 2
    scaled = values * sin_table[:, None, :]
    turned = jnp.concatenate([scaled[..., half_dim:], -scaled[..., :half_dim]], axis=-1)
    return values * cos_table[:, None, :] + turned


def swiglu(activation, breadth):
    return jax.nn.silu(activation[:, :breadth]) * activation[:, breadth:]


def swiglu_back(grad_hidden, activation, breadth):
    gate_part = activation[:, :breadth]
    up_part = activation[:, breadth:]
    sig_gate = jax.nn.sigmoid(gate_part)
    d_gate = grad_hidden * up_part * sig_gate * (1.0 + gate_part * (1.0 - sig_gate))
    d_up = grad_hidden * gate_part * sig_gate
    return jnp.concatenate([d_gate, d_up], axis=1)


def outer_rows(left_ops, right_ops):
    pieces = []
    for left_op, right_op in zip(left_ops, right_ops):
        pieces.append(
            lax.dot_general(
                left_op, right_op, (((0,), (0,)), ((), ())), preferred_element_type=jnp.float32
            )
        )
    return jnp.concatenate(pieces, axis=1)


def right_product(left_op, right_op):
    return lax.dot_general(
        left_op, right_op, (((1,), (1,)), ((), ())), preferred_element_type=jnp.float32
    )


def to_peer(array, bits):
    size = lax.axis_size("ctx")
    return lax.ppermute(array, "ctx", [(rank, rank ^ bits) for rank in range(size)])


def peer_gather(array, direct=False):
    size = lax.axis_size("ctx")
    if size != 4 or direct:
        return [array] + [to_peer(array, bits) for bits in range(1, size)]
    half = array.shape[0] // 2
    one, two = to_peer(array, 1), to_peer(array, 2)
    three = jnp.concatenate([to_peer(one[:half], 2), to_peer(two[half:], 1)], axis=0)
    return [array, one, two, three]


def wide(array):
    return array.astype(jnp.float32)


def low(array):
    return array.astype(jnp.bfloat16)


def peer_scatter(pieces):
    size = lax.axis_size("ctx")
    pieces = [low(piece) for piece in pieces]
    if size != 4:
        total = wide(pieces[0])
        for bits in range(1, size):
            total = total + wide(to_peer(pieces[bits], bits))
        return total
    half = pieces[0].shape[0] // 2
    first = to_peer(jnp.concatenate([pieces[1][:half], pieces[3][:half]], axis=0), 1)
    second = to_peer(jnp.concatenate([pieces[2][half:], pieces[3][half:]], axis=0), 2)
    upper = to_peer(low(wide(pieces[2][:half]) + wide(first[half:])), 2)
    lower = to_peer(low(wide(pieces[1][half:]) + wide(second[half:])), 1)
    return wide(pieces[0]) + jnp.concatenate(
        [wide(first[:half]) + wide(upper), wide(second[:half]) + wide(lower)], axis=0
    )


def peer_sum(array):
    size, half = lax.axis_size("ctx"), array.shape[0] // 2
    upper, lower, bits = array[:half], array[half:], 1
    while bits < size:
        upper, lower = low(upper), low(lower)
        other = size // 2 // bits
        upper = wide(upper) + wide(to_peer(upper, bits))
        lower = wide(lower) + wide(to_peer(lower, other))
        bits *= 2
    return jnp.concatenate([upper, lower], axis=0)


def by_rank(pieces):
    rank, bits = lax.axis_index("ctx"), 1
    while bits < len(pieces):
        odd = (rank & bits) != 0
        pieces = [jnp.where(odd, pieces[k ^ bits], pieces[k]) for k in range(len(pieces))]
        bits *= 2
    return pieces


def to_mate(array, bits):
    size = lax.axis_size("fsdp")
    return lax.ppermute(array, "fsdp", [(rank, rank ^ bits) for rank in range(size)])


def total_sum(array):
    bits = 1
    while bits < lax.axis_size("fsdp"):
        array = array + to_mate(array, bits)
        bits *= 2
    bits = 1
    while bits < lax.axis_size("ctx"):
        array = array + to_peer(array, bits)
        bits *= 2
    return array


VMEM_BYTES = 56 * 1024 * 1024


def own_call(kernel, name, grid, ins, in_specs, outs, out_specs, flops, waits=(), order=None, aliases=None):
    lead = 0 if order is None else 1
    count = len(ins)

    def body(*refs):
        kernel(*refs[lead : lead + count], *refs[lead + count + len(waits) :])

    moved = sum(array.size * array.dtype.itemsize for array in [*ins, *outs])
    return pl.pallas_call(
        body,
        out_shape=list(outs),
        grid_spec=pltpu.PrefetchScalarGridSpec(
            num_scalar_prefetch=lead,
            grid=grid,
            in_specs=list(in_specs) + [pl.BlockSpec(memory_space=pl.ANY)] * len(waits),
            out_specs=list(out_specs),
        ),
        compiler_params=pltpu.CompilerParams(vmem_limit_bytes=VMEM_BYTES),
        cost_estimate=pl.CostEstimate(flops=flops, transcendentals=0, bytes_accessed=moved),
        input_output_aliases=aliases or {},
        name=name,
    )(*([] if order is None else [order]), *ins, *waits)


def after(array, waits):
    waits = [wait for wait in waits if wait is not None]
    if not waits:
        return array
    return pl.pallas_call(
        lambda *refs: None,
        out_shape=jax.ShapeDtypeStruct(array.shape, array.dtype),
        in_specs=[pl.BlockSpec(memory_space=pl.ANY)] * (1 + len(waits)),
        out_specs=pl.BlockSpec(memory_space=pl.ANY),
        input_output_aliases={0: 0},
        name="after",
    )(array, *waits)


def unit_backward(rows_in, rows_grad, weight, factor, waits=()):
    rows, depth = rows_in.shape
    breadth = weight.shape[1] // 3
    if breadth % 128:
        act = jnp.dot(rows_in, weight[:, : 2 * breadth], preferred_element_type=jnp.float32)
        d_unit = jnp.dot(rows_grad, weight[:, 2 * breadth :], preferred_element_type=jnp.float32)
        units = swiglu(act, breadth)
        return (
            low(factor * units),
            low(swiglu_back(factor * d_unit, act, breadth)),
            jnp.sum(d_unit * units, axis=1, keepdims=True),
        )
    tall = min(rows, 256)

    def kernel(rows_ref, grad_ref, weight_ref, factor_ref, out_ref, d_act_ref, d_factor_ref):
        scale = factor_ref[...]
        total = jnp.zeros((tall, 1), jnp.float32)
        for start in range(0, breadth, 256):
            gate = slice(start, min(start + 256, breadth))
            up = slice(breadth + gate.start, breadth + gate.stop)
            down = slice(2 * breadth + gate.start, 2 * breadth + gate.stop)
            gate_part = jnp.dot(
                rows_ref[...], weight_ref[:, gate], preferred_element_type=jnp.float32
            )
            up_part = jnp.dot(rows_ref[...], weight_ref[:, up], preferred_element_type=jnp.float32)
            d_unit = jnp.dot(grad_ref[...], weight_ref[:, down], preferred_element_type=jnp.float32)
            sig_gate = jax.nn.sigmoid(gate_part)
            silu = gate_part * sig_gate
            units = silu * up_part
            total = total + jnp.sum(d_unit * units, axis=1, keepdims=True)
            out_ref[:, gate] = low(scale * units)
            scaled = scale * d_unit
            d_act_ref[:, gate] = low(scaled * up_part * (sig_gate + silu * (1.0 - sig_gate)))
            d_act_ref[:, up] = low(scaled * silu)
        d_factor_ref[...] = total

    return own_call(
        kernel,
        "unit_backward",
        (rows // tall,),
        [rows_in, rows_grad, weight, factor],
        [
            pl.BlockSpec((tall, depth), lambda i: (i, 0)),
            pl.BlockSpec((tall, depth), lambda i: (i, 0)),
            pl.BlockSpec((depth, 3 * breadth), lambda i: (0, 0)),
            pl.BlockSpec((tall, 1), lambda i: (i, 0)),
        ],
        [
            jax.ShapeDtypeStruct((rows, breadth), jnp.bfloat16),
            jax.ShapeDtypeStruct((rows, 2 * breadth), jnp.bfloat16),
            jax.ShapeDtypeStruct((rows, 1), jnp.float32),
        ],
        [
            pl.BlockSpec((tall, breadth), lambda i: (i, 0)),
            pl.BlockSpec((tall, 2 * breadth), lambda i: (i, 0)),
            pl.BlockSpec((tall, 1), lambda i: (i, 0)),
        ],
        6 * rows * depth * breadth,
        waits,
    )


def back_matmul(jobs, waits=()):
    rows, breadth = jobs[0][0][0][0].shape[0], jobs[0][0][0][1].shape[0]
    tile = 256
    ins, specs, flops = [], [], 0
    for products, total, dtype in jobs:
        for rows_in, weight, column in products:
            depth = rows_in.shape[1]
            if depth % 128 and weight.shape[1] != depth:
                weight = weight[:, column * depth : (column + 1) * depth]
                column = 0
            ins += [rows_in, weight]
            specs += [
                pl.BlockSpec((rows, depth), lambda j: (0, 0)),
                pl.BlockSpec((tile, depth), lambda j, column=column: (j, column)),
            ]
            flops += 2 * rows * depth * breadth
        if total is not None:
            ins.append(total)
            specs.append(pl.BlockSpec((rows, tile), lambda j: (0, j)))

    def kernel(*refs):
        used = 0
        for out, (products, total, dtype) in enumerate(jobs):
            value = None
            for _ in products:
                part = right_product(refs[used][...], refs[used + 1][...])
                value = part if value is None else value + part
                used += 2
            if total is not None:
                value = value + wide(refs[used][...])
                used += 1
            refs[len(ins) + out][...] = value.astype(dtype)

    return own_call(
        kernel,
        "back_matmul",
        (breadth // tile,),
        ins,
        specs,
        [jax.ShapeDtypeStruct((rows, breadth), dtype) for products, total, dtype in jobs],
        [pl.BlockSpec((rows, tile), lambda j: (0, j))] * len(jobs),
        flops,
        waits,
    )


def route_product(d_route, route_mat):
    coarse = low(d_route)
    fine = low(d_route - wide(coarse))
    both = low(jnp.concatenate([route_mat, route_mat], axis=1))
    return (jnp.concatenate([coarse, fine], axis=1), both, 0)


def grad_matmul(pairs, waits=(), core=None, add=None):
    blocks = lax.axis_size("fsdp")
    depth = pairs[0][0][0].shape[1]
    widths = [rights[0].shape[1] for lefts, rights in pairs]
    total, block = sum(widths), depth // blocks
    step, first = (1, 0) if core is None else (2, core)
    blocks //= step
    ins, specs, flops = [], [], 0
    for lefts, rights in pairs:
        for left, right in zip(lefts, rights):
            ins += [left, right]
            specs += [
                pl.BlockSpec((left.shape[0], block), lambda j, first_ref: (0, step * j + first_ref[0])),
                pl.BlockSpec(right.shape, lambda j, first_ref: (0, 0)),
            ]
            flops += 2 * left.shape[0] * depth // step * right.shape[1]
    if add is not None:
        ins.append(add)
        specs.append(pl.BlockSpec((block, total), lambda j, first_ref: (j, 0)))

    def kernel(*refs):
        start, used = 0, 0
        for (lefts, rights), width in zip(pairs, widths):
            value = None
            for _ in lefts:
                part = lax.dot_general(
                    refs[used][...],
                    refs[used + 1][...],
                    (((0,), (0,)), ((), ())),
                    preferred_element_type=jnp.float32,
                )
                value = part if value is None else value + part
                used += 2
            if add is not None:
                value = value + wide(refs[-2][:, start : start + width])
            refs[-1][:, start : start + width] = low(value)
            start += width

    return own_call(
        kernel,
        "grad_matmul",
        (blocks,),
        ins,
        specs,
        [jax.ShapeDtypeStruct((blocks * block, total), jnp.bfloat16)],
        [pl.BlockSpec((block, total), lambda j, first_ref: (j, 0))],
        flops,
        waits,
        jnp.asarray(first, jnp.int32).reshape(1),
    )[0]


def split_matmul(rows_in, gain, weight, bias, cos_table, sin_table, waits=()):
    rows, depth = rows_in.shape
    breadth = bias.shape[0]
    tile = 256
    turned = breadth * 2 // 3 // tile
    tall = min(rows, 256)

    def kernel(rows_ref, gain_ref, weight_ref, bias_ref, cos_ref, sin_ref, normed_ref, out_ref):
        @pl.when(pl.program_id(0) == 0)
        def _():
            for start in range(0, rows, tall):
                some = slice(start, start + tall)
                values = wide(rows_ref[some, :])
                normed_ref[some, :] = low(values * rms_scale(values) * gain_ref[...])

        value = jnp.dot(normed_ref[...], weight_ref[...], preferred_element_type=jnp.float32)
        value = value + bias_ref[...]

        @pl.when(pl.program_id(0) < turned)
        def _():
            for start in range(0, tile, HEAD_DIM):
                head = value[:, start : start + HEAD_DIM]
                head = head * cos_ref[...] + pltpu.roll(head, HEAD_DIM // 2, 1) * sin_ref[...]
                out_ref[:, start : start + HEAD_DIM] = low(head)

        @pl.when(pl.program_id(0) >= turned)
        def _():
            out_ref[...] = low(value)

    whole = pl.BlockSpec((rows, depth), lambda j: (0, 0))
    table = pl.BlockSpec((rows, HEAD_DIM), lambda j: (0, 0))
    return own_call(
        kernel,
        "split_matmul",
        (breadth // tile,),
        [rows_in, gain.reshape(1, depth), weight, bias.reshape(1, breadth), cos_table, sin_table],
        [
            whole,
            pl.BlockSpec((1, depth), lambda j: (0, 0)),
            pl.BlockSpec((depth, tile), lambda j: (0, j)),
            pl.BlockSpec((1, tile), lambda j: (0, j)),
            table,
            table,
        ],
        [
            jax.ShapeDtypeStruct((rows, depth), jnp.bfloat16),
            jax.ShapeDtypeStruct((rows, breadth), jnp.bfloat16),
        ],
        [whole, pl.BlockSpec((rows, tile), lambda j: (0, j))],
        2 * rows * depth * breadth,
        waits,
    )


def head_specs(rows, heads):
    return [
        pl.BlockSpec((rows, HEAD_DIM), lambda h, part=part: (0, part * heads + h))
        for part in range(3)
    ]


def attend(split, places, heads, waits=()):
    rows = split.shape[0]
    tall = min(rows, 256)
    scale = HEAD_DIM ** (-0.5)

    def kernel(query_ref, key_ref, value_ref, down_ref, across_ref, out_ref, log_ref):
        for start in range(0, rows, tall):
            some = slice(start, start + tall)
            scores = right_product(query_ref[some, :], key_ref[...]) * scale
            scores = jnp.where(across_ref[...] <= down_ref[some, :], scores, -1e30)
            top = jnp.max(scores, axis=1, keepdims=True)
            exponent = jnp.exp(scores - top)
            total = jnp.sum(exponent, axis=1, keepdims=True)
            prob = low(exponent * (1.0 / total))
            out_ref[some, :] = low(
                jnp.dot(prob, value_ref[...], preferred_element_type=jnp.float32)
            )
            log_ref[some, :] = top + jnp.log(total)

    return own_call(
        kernel,
        "attend",
        (heads,),
        [split, split, split, places.reshape(rows, 1), places.reshape(1, rows)],
        head_specs(rows, heads)
        + [
            pl.BlockSpec((rows, 1), lambda h: (0, 0)),
            pl.BlockSpec((1, rows), lambda h: (0, 0)),
        ],
        [
            jax.ShapeDtypeStruct((rows, heads * HEAD_DIM), jnp.bfloat16),
            jax.ShapeDtypeStruct((heads, rows, 1), jnp.float32),
        ],
        [
            pl.BlockSpec((rows, HEAD_DIM), lambda h: (0, h)),
            pl.BlockSpec((None, rows, 1), lambda h: (h, 0, 0)),
        ],
        4 * rows * rows * heads * HEAD_DIM,
        waits,
    )


def attend_back(split, places, log_total, d_vec, cos_table, sin_table, heads, waits=()):
    rows = split.shape[0]
    tall = min(rows, 256)
    scale = HEAD_DIM ** (-0.5)

    def kernel(query_ref, key_ref, value_ref, down_ref, across_ref, log_ref, grad_ref, cos_ref, sin_ref, out_ref):
        first = pl.multiple_of(pl.program_id(0) * HEAD_DIM, HEAD_DIM)
        d_key = jnp.zeros((rows, HEAD_DIM), jnp.float32)
        d_value = jnp.zeros((rows, HEAD_DIM), jnp.float32)

        def unturned(grad, some):
            return low(
                grad * cos_ref[some, :]
                - pltpu.roll(grad, HEAD_DIM // 2, 1) * sin_ref[some, :]
            )

        def columns(part):
            return pl.ds(first + part * heads * HEAD_DIM, HEAD_DIM)

        for start in range(0, rows, tall):
            some = slice(start, start + tall)
            query, grad = query_ref[some, :], grad_ref[some, :]
            scores = right_product(query, key_ref[...]) * scale
            prob = jnp.where(
                across_ref[...] <= down_ref[some, :], jnp.exp(scores - log_ref[some, :]), 0.0
            )
            d_prob = right_product(grad, value_ref[...])
            inner = jnp.sum(prob * d_prob, axis=1, keepdims=True)
            d_score = low(prob * (d_prob - inner) * scale)
            across = (((0,), (0,)), ((), ()))
            d_value = d_value + lax.dot_general(
                low(prob), grad, across, preferred_element_type=jnp.float32
            )
            d_key = d_key + lax.dot_general(
                d_score, query, across, preferred_element_type=jnp.float32
            )
            d_query = jnp.dot(d_score, key_ref[...], preferred_element_type=jnp.float32)
            out_ref[some, columns(0)] = unturned(d_query, some)
        out_ref[:, columns(1)] = unturned(d_key, slice(0, rows))
        out_ref[:, columns(2)] = low(d_value)

    table = pl.BlockSpec((rows, HEAD_DIM), lambda h: (0, 0))
    return own_call(
        kernel,
        "attend_back",
        (heads,),
        [split, split, split, places.reshape(rows, 1), places.reshape(1, rows), log_total, d_vec]
        + [cos_table, sin_table],
        head_specs(rows, heads)
        + [
            pl.BlockSpec((rows, 1), lambda h: (0, 0)),
            pl.BlockSpec((1, rows), lambda h: (0, 0)),
            pl.BlockSpec((None, rows, 1), lambda h: (h, 0, 0)),
            pl.BlockSpec((rows, HEAD_DIM), lambda h: (0, h)),
            table,
            table,
        ],
        [jax.ShapeDtypeStruct((rows, 3 * heads * HEAD_DIM), jnp.bfloat16)],
        [pl.BlockSpec((rows, 3 * heads * HEAD_DIM), lambda h: (0, 0))],
        10 * rows * rows * heads * HEAD_DIM,
        waits,
    )[0]


def place_grads(spread, slot, slots, totals, waits=()):
    size, rows = len(spread[0][0]), spread[0][0][0].shape[0]
    units = sum([sum(parts) for pieces, parts in spread])
    if units % 128:
        ordered = by_rank(spread[0][0])
        sides = [
            jnp.stack([piece[:, k * units : (k + 1) * units] for piece in ordered], axis=1)
            for k in range(3)
        ]
        into = jnp.stack(sides[:2], axis=1).reshape(rows, 2 * size * units)
        return wide(into), wide(sides[2].reshape(rows, size * units)), spread[0][0][0]
    tall = min(rows, 64)
    columns = 2 if slot is None else 1
    pieces = [held[k] for k in range(size) for held, parts in spread]
    onto = [] if totals is None else list(totals[:2])
    rest = list(waits) + onto
    steps = rows // tall

    def kernel(*refs):
        in_ref, out_ref, mark_ref = refs[-3:]
        mark_ref[...] = jnp.zeros_like(mark_ref)
        for k in range(size):

            @pl.when(pl.program_id(0) == k)
            def _():
                used = refs[k * len(spread) : (k + 1) * len(spread)]
                place = 0
                for (held, parts), ref in zip(spread, used):
                    start = 0
                    for part in parts:
                        gate = ref[:, start : start + part]
                        up = ref[:, start + part : start + 2 * part]
                        if slot is None:
                            here = pl.program_id(2) == 0
                            in_ref[:, place : place + part] = wide(jnp.where(here, gate, up))
                        else:
                            in_ref[:, place : place + part] = wide(gate)
                            in_ref[:, units + place : units + place + part] = wide(up)
                        out_ref[:, place : place + part] = wide(
                            ref[:, start + 2 * part : start + 3 * part]
                        )
                        place += part
                        start += 3 * part

    def piece_spec(k, parts):
        def piece_map(step, row, column, rank_ref):
            return (jnp.where(step == k, row, jnp.where(step < k, 0, steps - 1)), 0)

        return pl.BlockSpec((tall, 3 * sum(parts)), piece_map)

    if slot is None:
        shapes = [(rows, 2 * size * units), (rows, size * units)]
        out_specs = [
            pl.BlockSpec(
                (tall, units),
                lambda k, row, column, rank_ref: (row, column * size + (rank_ref[0] ^ k)),
            ),
            pl.BlockSpec((tall, units), lambda k, row, column, rank_ref: (row, rank_ref[0] ^ k)),
        ]
    else:
        shapes = [(size * slots, rows, 2 * units), (size * slots, rows, units)]
        out_specs = [
            pl.BlockSpec(
                (None, tall, shape[2]),
                lambda k, row, column, rank_ref: ((rank_ref[0] ^ k) * slots + slot, row, 0),
            )
            for shape in shapes
        ]
    first = 1 + len(pieces) + len(waits)
    return own_call(
        kernel,
        "place_grads",
        (size, steps, columns),
        pieces,
        [piece_spec(k, parts) for k in range(size) for held, parts in spread],
        [jax.ShapeDtypeStruct(shape, jnp.float32) for shape in [*shapes, (8, 128)]],
        out_specs + [pl.BlockSpec((8, 128), lambda k, row, column, rank_ref: (0, 0))],
        0,
        rest,
        lax.axis_index("ctx").reshape(1),
        aliases={first: 0, first + 1: 1} if onto else {},
    )


def place_cols(pieces, parts, waits=()):
    size, rows = len(pieces), pieces[0].shape[0]
    breadth = pieces[0].shape[1] // parts
    if breadth % 128:
        ordered = [piece.reshape(rows, parts, breadth) for piece in by_rank(pieces)]
        return wide(jnp.stack(ordered, axis=2).reshape(rows, parts * size * breadth))

    def kernel(*refs):
        for k, ref in enumerate(refs[:-1]):

            @pl.when(pl.program_id(0) == k)
            def _():
                refs[-1][...] = wide(ref[...])

    def piece_spec(own):
        def piece_map(k, part, rank_ref):
            return (0, jnp.where(k == own, part, jnp.where(k < own, 0, parts - 1)))

        return pl.BlockSpec((rows, breadth), piece_map)

    return own_call(
        kernel,
        "place_cols",
        (size, parts),
        pieces,
        [piece_spec(own) for own in range(size)],
        [jax.ShapeDtypeStruct((rows, parts * size * breadth), jnp.float32)],
        [
            pl.BlockSpec(
                (rows, breadth), lambda k, part, rank_ref: (0, part * size + (rank_ref[0] ^ k))
            )
        ],
        0,
        waits,
        lax.axis_index("ctx").reshape(1),
    )[0]

def per_device(
    tokens,
    routes,
    block_ids,
    attn_gain,
    w_attn_in,
    b_qkv,
    w_attn_out,
    ffn_gain,
    router,
    shared_gate,
    w_sh_in,
    w_sh_out,
    w_exp_in,
    w_exp_out,
    cotangent,
):
    ctx_size = lax.axis_size("ctx")
    fsdp_size = lax.axis_size("fsdp")
    ctx_rank = lax.axis_index("ctx")
    fsdp_rank = lax.axis_index("fsdp")
    tok_rows = tokens.shape[0]
    block_len = tok_rows // 2
    seq_len = tok_rows * ctx_size
    heads_own = HEADS // ctx_size
    att_cols = heads_own * HEAD_DIM
    sh_cols = FS // ctx_size
    experts_own = EXPERTS // ctx_size

    def own_cols(array, start, breadth):
        return lax.dynamic_slice_in_dim(array, start + ctx_rank * breadth, breadth, axis=1)

    def gather_fsdp(array):
        return lax.all_gather(array, "fsdp", axis=0, tiled=True)

    def scatter_fsdp(array):
        return lax.psum_scatter(
            array.astype(jnp.bfloat16), "fsdp", scatter_dimension=0, tiled=True
        )

    def token_pieces(array):
        return [array[k * tok_rows : (k + 1) * tok_rows] for k in range(ctx_size)]

    tokens_all = jnp.concatenate(peer_gather(tokens), axis=0)
    quarter = D // ctx_size
    w_out_own = gather_fsdp(own_cols(w_attn_out, 0, quarter))
    w_out_pieces = peer_gather(w_out_own)
    rows = attn_gain.shape[0]
    smalls = jnp.concatenate(
        [jnp.stack([attn_gain, ffn_gain, shared_gate], axis=1), router, b_qkv.reshape(3, rows).T],
        axis=1,
    )
    smalls = jnp.pad(smalls, ((0, 0), (0, 128 - smalls.shape[1])))
    w_in_slab = jnp.concatenate(
        [own_cols(w_attn_in, part * D, att_cols) for part in range(3)] + [smalls], axis=1
    )
    w_in_own = gather_fsdp(after(w_in_slab, [w_out_own]))
    smalls_all = w_in_own[:, 3 * att_cols :]
    gain_one, gain_two, gate_vec = [wide(smalls_all[:, k]) for k in range(3)]
    router_wide = wide(smalls_all[:, 3 : 3 + EXPERTS])
    bias_full = smalls_all[:, 3 + EXPERTS : 6 + EXPERTS].reshape(fsdp_size, rows, 3)
    bias_full = jnp.transpose(bias_full, (0, 2, 1)).reshape(3, D)
    bias_own = wide(own_cols(bias_full, 0, att_cols)).reshape(3 * att_cols)

    core = fsdp_rank % 2
    lines = [[rank for rank in range(fsdp_size) if rank % 2 == spot] for spot in range(2)]

    def scatter_line(grad):
        return lax.psum_scatter(
            grad, "fsdp", scatter_dimension=0, axis_index_groups=lines, tiled=True
        )

    slabs = [
        [own_cols(w_sh_in, part * FS, sh_cols) for part in range(2)]
        + [own_cols(w_sh_out, 0, sh_cols)]
    ]
    for own in range(experts_own):
        expert = ctx_rank * experts_own + own
        slabs.append([w_exp_in[expert, :, :FE], w_exp_in[expert, :, FE:], w_exp_out[expert]])
    slabs = [jnp.concatenate(sides, axis=1) for sides in slabs]

    inputs = wide(tokens)
    scale_one = rms_scale(inputs)
    unit_one = inputs * scale_one
    ranks = ctx_rank ^ jnp.arange(ctx_size, dtype=jnp.int32)
    places = block_places(block_ids.reshape(ctx_size, 2)[ranks].reshape(-1), block_len)
    cos_table, sin_table = rotary_tables(places)
    half = HEAD_DIM // 2
    sin_table = jnp.concatenate([-sin_table[:, :half], sin_table[:, half:]], axis=1)
    normed_all, split = split_matmul(
        tokens_all, gain_one, w_in_own, bias_own, cos_table, sin_table
    )
    attended, log_total = attend(split, places, heads_own, w_out_pieces)
    head_pieces = token_pieces(attended)
    head_pieces = head_pieces[:1] + [
        to_peer(head_pieces[bits], bits) for bits in range(1, ctx_size)
    ]
    attn_vec = jnp.concatenate(by_rank(head_pieces), axis=1)
    attn_out = [
        jnp.dot(attn_vec, piece, preferred_element_type=jnp.float32) for piece in w_out_pieces
    ]
    residual = inputs + jnp.concatenate(by_rank(attn_out), axis=1)

    scale_two = rms_scale(residual)
    unit_two = residual * scale_two
    cots = [jnp.concatenate(peer_gather(after(cotangent, [split])), axis=0)]
    hidden_in = low(unit_two * gain_two)
    hidden = [jnp.concatenate(peer_gather(hidden_in), axis=0)]
    route_mat = jnp.concatenate([router_wide, gate_vec[:, None]], axis=1)
    expert_ids = jnp.arange(EXPERTS, dtype=jnp.int32)
    logits = jnp.dot(
        wide(hidden[0]), route_mat, precision=highest, preferred_element_type=jnp.float32
    )
    route_probs = jax.nn.softmax(logits[:, :EXPERTS], axis=1)
    shared_prob = jax.nn.sigmoid(logits[:, EXPERTS:])
    routes_all = jnp.concatenate(
        [routes] + [to_peer(routes, bits) for bits in range(1, ctx_size)], axis=0
    )
    chosen = wide(jnp.any(routes_all[:, :, None] == expert_ids[None, None, :], axis=1))

    weights = [
        gather_fsdp(after(slab, [wait]))
        for slab, wait in zip(slabs, (w_in_own, split, attended))
    ]
    d_probs = jnp.zeros((seq_len, EXPERTS), jnp.float32)
    sums, waits, grads = [None, None], [], []
    for index, weight in enumerate(weights):
        own = index - 1
        if own < 0:
            factor = shared_prob
        else:
            picked = (expert_ids == ctx_rank * experts_own + own)[None, :]
            factor = jnp.sum(
                jnp.where(picked, route_probs * chosen, 0.0), axis=1, keepdims=True
            )
        scaled_out, d_act, d_factor = unit_backward(hidden[0], cots[0], weight, factor, waits)
        if own < 0:
            d_gate_logit = d_factor * (shared_prob * (1.0 - shared_prob))
        else:
            d_probs = d_probs + jnp.where(picked, chosen * d_factor, 0.0)
        waits = [scaled_out]
        products, outward = [(d_act, weight, 0)], [(scaled_out, weight, 2)]
        if index == len(weights) - 1:
            d_logits = route_probs * (
                d_probs - jnp.sum(route_probs * d_probs, axis=1, keepdims=True)
            )
            d_route = jnp.concatenate([d_logits, d_gate_logit], axis=1)
            products.append(route_product(d_route, route_mat))
            d_hidden_sum = back_matmul([(products, sums[0], jnp.bfloat16)], waits)[0]
            waits = [d_hidden_sum]
        pairs = [(hidden, [d_act]), (cots, [scaled_out])]
        given = grad_matmul(pairs, waits, 1 - core)
        waits = [given]
        if index < len(weights) - 1:
            sums = back_matmul(
                [(products, sums[0], jnp.float32), (outward, sums[1], jnp.float32)], waits
            )
            waits = [sums[0]]
        else:
            block_sum = back_matmul([(outward, sums[1], jnp.bfloat16)], waits)[0]
            waits = [block_sum]
        grads.append(grad_matmul(pairs, waits, core, to_mate(given, 1)))
        waits = [grads[-1]]
    shards = [scatter_line(grad) for grad in grads]
    d_route_mat = lax.dot_general(
        d_route,
        wide(hidden[0]),
        (((0,), (0,)), ((), ())),
        precision=highest,
        preferred_element_type=jnp.float32,
    )
    d_hidden = peer_scatter(token_pieces(d_hidden_sum))
    cot_wide = wide(cotangent)
    d_gain_two = jnp.sum(d_hidden * unit_two, axis=0)
    d_resid = cot_wide + rms_back(d_hidden, unit_two, scale_two, gain_two)
    d_attn = low(d_resid)
    d_attn_pieces = by_rank(
        [d_attn[:, k * quarter : (k + 1) * quarter] for k in range(ctx_size)]
    )
    products = [(piece, weight, 0) for piece, weight in zip(d_attn_pieces, w_out_pieces)]
    d_vec_own = back_matmul([(products, None, jnp.bfloat16)], waits)[0]
    d_vec_pieces = by_rank(
        [d_vec_own[:, k * att_cols : (k + 1) * att_cols] for k in range(ctx_size)]
    )
    d_vec = jnp.concatenate(
        d_vec_pieces[:1] + [to_peer(d_vec_pieces[bits], bits) for bits in range(1, ctx_size)],
        axis=0,
    )
    grad_w_out = grad_matmul(
        [([attn_vec], [jnp.concatenate(d_attn_pieces, axis=1)])], [d_vec_own]
    )
    grad_w_out = peer_scatter(
        [grad_w_out[:, k * quarter : (k + 1) * quarter] for k in range(ctx_size)]
    )
    grad_w_out = scatter_fsdp(grad_w_out)
    d_mixed = attend_back(split, places, log_total, d_vec, cos_table, sin_table, heads_own)
    given = grad_matmul([([normed_all], [d_mixed])], (), 1 - core)
    d_bias = jnp.sum(wide(d_mixed), axis=0)
    d_normed_part = back_matmul(
        [([(d_mixed, w_in_own, 0)], None, jnp.bfloat16)], [given]
    )[0]
    grad_w_in = scatter_line(
        grad_matmul([([normed_all], [d_mixed])], [d_normed_part], core, to_mate(given, 1))
    )
    d_normed = peer_scatter(token_pieces(d_normed_part))
    block_out = low(residual + peer_scatter(token_pieces(after(block_sum, [d_mixed]))))
    units, totals, waits = [sh_cols] + [FE] * experts_own, None, [d_normed_part]
    for own, shard in zip(range(-1, experts_own), shards):
        spread = [(peer_gather(after(shard, waits)), units[:1] if own < 0 else units[1:2])]
        if own < 0:
            shared_totals = place_grads(spread, None, 1, None, waits)
            waits = [shared_totals[2]]
        else:
            totals = place_grads(spread, own, experts_own, totals, waits)
            waits = [totals[2]]
    wide_all = wide(tokens_all)
    d_gain_one = jnp.sum(wide(d_normed_part) * (wide_all * rms_scale(wide_all)), axis=0)
    d_tokens = d_resid + rms_back(d_normed, unit_one, scale_one, gain_one)

    bias_spread = lax.dynamic_update_slice(
        jnp.zeros((3, D), jnp.float32), d_bias.reshape(3, att_cols), (0, ctx_rank * att_cols)
    )
    early_grads = total_sum(jnp.concatenate([d_route_mat.reshape(-1), d_gain_two]))
    late_grads = total_sum(jnp.concatenate([bias_spread.reshape(-1), d_gain_one]))

    def own_part(vector):
        size = vector.shape[0] // fsdp_size
        return lax.dynamic_slice_in_dim(vector, fsdp_rank * size, size)

    route_total = early_grads[: (EXPERTS + 1) * D].reshape(EXPERTS + 1, D)
    route_part = lax.dynamic_slice_in_dim(route_total, fsdp_rank * rows, rows, axis=1)
    return (
        block_out,
        d_tokens,
        own_part(late_grads[3 * D :]),
        place_cols(peer_gather(grad_w_in), 3, [totals[1]]),
        own_part(late_grads[: 3 * D]),
        wide(jnp.concatenate(by_rank(peer_gather(grad_w_out)), axis=1)),
        own_part(early_grads[(EXPERTS + 1) * D :]),
        route_part[:EXPERTS].T,
        route_part[EXPERTS],
        *shared_totals[:2],
        *totals[:2],
    )


def solution(mesh):
    return jax.shard_map(
        per_device,
        mesh=mesh,
        in_specs=(
            P(("ctx", "fsdp"), None),
            P(("ctx", "fsdp"), None),
            P(),
            P("fsdp"),
            P("fsdp", None),
            P("fsdp"),
            P("fsdp", None),
            P("fsdp"),
            P("fsdp", None),
            P("fsdp"),
            P("fsdp", None),
            P("fsdp", None),
            P(None, "fsdp", None),
            P(None, "fsdp", None),
            P(("ctx", "fsdp"), None),
        ),
        out_specs=(
            P(("ctx", "fsdp"), None),
            P(("ctx", "fsdp"), None),
            P("fsdp"),
            P("fsdp", None),
            P("fsdp"),
            P("fsdp", None),
            P("fsdp"),
            P("fsdp", None),
            P("fsdp"),
            P("fsdp", None),
            P("fsdp", None),
            P(None, "fsdp", None),
            P(None, "fsdp", None),
        ),
        check_vma=False,
    )
```

```python
import functools

import jax
import jax.numpy as jnp
from jax import lax
from jax.experimental import pallas as pl
from jax.experimental.pallas import tpu as pltpu
from jax.sharding import PartitionSpec as P

D = 2048
HEADS = 16
HEAD_DIM = 128
FS = 5632
FE = 1408
EXPERTS = 8


norm_eps = 1e-06
rope_base = 1000000.0
highest = lax.Precision.HIGHEST


def rms_scale(values):
    return lax.rsqrt(jnp.mean(values * values, axis=1, keepdims=True) + norm_eps)


def rms_back(grad_rows, unit_rows, row_scale, gain_row):
    scaled = grad_rows * gain_row
    return row_scale * (scaled - unit_rows * jnp.mean(scaled * unit_rows, axis=1, keepdims=True))


def block_places(block_list, block_len):
    offsets = jnp.arange(block_len, dtype=jnp.int32)
    return (block_list[:, None] * block_len + offsets[None, :]).reshape(-1)


def rotary_tables(positions):
    half_dim = HEAD_DIM // 2
    inverse = rope_base ** (-2.0 * jnp.arange(half_dim, dtype=jnp.float32) / HEAD_DIM)
    angles = positions.astype(jnp.float32)[:, None] * inverse[None, :]
    cos_table = jnp.cos(angles)
    sin_table = jnp.sin(angles)
    return (
        jnp.concatenate([cos_table, cos_table], axis=1),
        jnp.concatenate([sin_table, sin_table], axis=1),
    )


def rotate(values, cos_table, sin_table):
    half_dim = HEAD_DIM // 2
    turned = jnp.concatenate([-values[..., half_dim:], values[..., :half_dim]], axis=-1)
    return values * cos_table[:, None, :] + turned * sin_table[:, None, :]


def unrotate(values, cos_table, sin_table):
    half_dim = HEAD_DIM // 2
    scaled = values * sin_table[:, None, :]
    turned = jnp.concatenate([scaled[..., half_dim:], -scaled[..., :half_dim]], axis=-1)
    return values * cos_table[:, None, :] + turned


def swiglu(activation, breadth):
    return jax.nn.silu(activation[:, :breadth]) * activation[:, breadth:]


def swiglu_back(grad_hidden, activation, breadth):
    gate_part = activation[:, :breadth]
    up_part = activation[:, breadth:]
    sig_gate = jax.nn.sigmoid(gate_part)
    d_gate = grad_hidden * up_part * sig_gate * (1.0 + gate_part * (1.0 - sig_gate))
    d_up = grad_hidden * gate_part * sig_gate
    return jnp.concatenate([d_gate, d_up], axis=1)


def outer_rows(left_ops, right_ops):
    pieces = []
    for left_op, right_op in zip(left_ops, right_ops):
        pieces.append(
            lax.dot_general(
                left_op, right_op, (((0,), (0,)), ((), ())), preferred_element_type=jnp.float32
            )
        )
    return jnp.concatenate(pieces, axis=1)


def right_product(left_op, right_op):
    return lax.dot_general(
        left_op, right_op, (((1,), (1,)), ((), ())), preferred_element_type=jnp.float32
    )


def to_peer(array, bits):
    size = lax.axis_size("ctx")
    return lax.ppermute(array, "ctx", [(rank, rank ^ bits) for rank in range(size)])


def peer_gather(array, direct=False):
    size = lax.axis_size("ctx")
    if size != 4 or direct:
        return [array] + [to_peer(array, bits) for bits in range(1, size)]
    half = array.shape[0] // 2
    one, two = to_peer(array, 1), to_peer(array, 2)
    three = jnp.concatenate([to_peer(one[:half], 2), to_peer(two[half:], 1)], axis=0)
    return [array, one, two, three]


def wide(array):
    return array.astype(jnp.float32)


def low(array):
    return array.astype(jnp.bfloat16)


def peer_scatter(pieces):
    size = lax.axis_size("ctx")
    pieces = [low(piece) for piece in pieces]
    if size != 4:
        total = wide(pieces[0])
        for bits in range(1, size):
            total = total + wide(to_peer(pieces[bits], bits))
        return total
    half = pieces[0].shape[0] // 2
    first = to_peer(jnp.concatenate([pieces[1][:half], pieces[3][:half]], axis=0), 1)
    second = to_peer(jnp.concatenate([pieces[2][half:], pieces[3][half:]], axis=0), 2)
    upper = to_peer(low(wide(pieces[2][:half]) + wide(first[half:])), 2)
    lower = to_peer(low(wide(pieces[1][half:]) + wide(second[half:])), 1)
    return wide(pieces[0]) + jnp.concatenate(
        [wide(first[:half]) + wide(upper), wide(second[:half]) + wide(lower)], axis=0
    )


def peer_sum(array):
    size, half = lax.axis_size("ctx"), array.shape[0] // 2
    upper, lower, bits = array[:half], array[half:], 1
    while bits < size:
        upper, lower = low(upper), low(lower)
        other = size // 2 // bits
        upper = wide(upper) + wide(to_peer(upper, bits))
        lower = wide(lower) + wide(to_peer(lower, other))
        bits *= 2
    return jnp.concatenate([upper, lower], axis=0)


def by_rank(pieces):
    rank, bits = lax.axis_index("ctx"), 1
    while bits < len(pieces):
        odd = (rank & bits) != 0
        pieces = [jnp.where(odd, pieces[k ^ bits], pieces[k]) for k in range(len(pieces))]
        bits *= 2
    return pieces


def to_mate(array, bits):
    size = lax.axis_size("fsdp")
    return lax.ppermute(array, "fsdp", [(rank, rank ^ bits) for rank in range(size)])


def total_sum(array):
    bits = 1
    while bits < lax.axis_size("fsdp"):
        array = array + to_mate(array, bits)
        bits *= 2
    bits = 1
    while bits < lax.axis_size("ctx"):
        array = array + to_peer(array, bits)
        bits *= 2
    return array


VMEM_BYTES = 56 * 1024 * 1024


def own_call(kernel, name, grid, ins, in_specs, outs, out_specs, flops, waits=(), order=None, aliases=None):
    lead = 0 if order is None else 1
    count = len(ins)

    def body(*refs):
        kernel(*refs[lead : lead + count], *refs[lead + count + len(waits) :])

    moved = sum(array.size * array.dtype.itemsize for array in [*ins, *outs])
    return pl.pallas_call(
        body,
        out_shape=list(outs),
        grid_spec=pltpu.PrefetchScalarGridSpec(
            num_scalar_prefetch=lead,
            grid=grid,
            in_specs=list(in_specs) + [pl.BlockSpec(memory_space=pl.ANY)] * len(waits),
            out_specs=list(out_specs),
        ),
        compiler_params=pltpu.CompilerParams(vmem_limit_bytes=VMEM_BYTES),
        cost_estimate=pl.CostEstimate(flops=flops, transcendentals=0, bytes_accessed=moved),
        input_output_aliases=aliases or {},
        name=name,
    )(*([] if order is None else [order]), *ins, *waits)


def after(array, waits):
    waits = [wait for wait in waits if wait is not None]
    if not waits:
        return array
    return pl.pallas_call(
        lambda *refs: None,
        out_shape=jax.ShapeDtypeStruct(array.shape, array.dtype),
        in_specs=[pl.BlockSpec(memory_space=pl.ANY)] * (1 + len(waits)),
        out_specs=pl.BlockSpec(memory_space=pl.ANY),
        input_output_aliases={0: 0},
        name="after",
    )(array, *waits)


def unit_backward(rows_in, rows_grad, weight, factor, waits=()):
    rows, depth = rows_in.shape
    breadth = weight.shape[1] // 3
    if breadth % 128:
        act = jnp.dot(rows_in, weight[:, : 2 * breadth], preferred_element_type=jnp.float32)
        d_unit = jnp.dot(rows_grad, weight[:, 2 * breadth :], preferred_element_type=jnp.float32)
        units = swiglu(act, breadth)
        return (
            low(factor * units),
            low(swiglu_back(factor * d_unit, act, breadth)),
            jnp.sum(d_unit * units, axis=1, keepdims=True),
        )
    tall = min(rows, 256)

    def kernel(rows_ref, grad_ref, weight_ref, factor_ref, out_ref, d_act_ref, d_factor_ref):
        scale = factor_ref[...]
        total = jnp.zeros((tall, 1), jnp.float32)
        for start in range(0, breadth, 256):
            gate = slice(start, min(start + 256, breadth))
            up = slice(breadth + gate.start, breadth + gate.stop)
            down = slice(2 * breadth + gate.start, 2 * breadth + gate.stop)
            gate_part = jnp.dot(
                rows_ref[...], weight_ref[:, gate], preferred_element_type=jnp.float32
            )
            up_part = jnp.dot(rows_ref[...], weight_ref[:, up], preferred_element_type=jnp.float32)
            d_unit = jnp.dot(grad_ref[...], weight_ref[:, down], preferred_element_type=jnp.float32)
            sig_gate = jax.nn.sigmoid(gate_part)
            silu = gate_part * sig_gate
            units = silu * up_part
            total = total + jnp.sum(d_unit * units, axis=1, keepdims=True)
            out_ref[:, gate] = low(scale * units)
            scaled = scale * d_unit
            d_act_ref[:, gate] = low(scaled * up_part * (sig_gate + silu * (1.0 - sig_gate)))
            d_act_ref[:, up] = low(scaled * silu)
        d_factor_ref[...] = total

    return own_call(
        kernel,
        "unit_backward",
        (rows // tall,),
        [rows_in, rows_grad, weight, factor],
        [
            pl.BlockSpec((tall, depth), lambda i: (i, 0)),
            pl.BlockSpec((tall, depth), lambda i: (i, 0)),
            pl.BlockSpec((depth, 3 * breadth), lambda i: (0, 0)),
            pl.BlockSpec((tall, 1), lambda i: (i, 0)),
        ],
        [
            jax.ShapeDtypeStruct((rows, breadth), jnp.bfloat16),
            jax.ShapeDtypeStruct((rows, 2 * breadth), jnp.bfloat16),
            jax.ShapeDtypeStruct((rows, 1), jnp.float32),
        ],
        [
            pl.BlockSpec((tall, breadth), lambda i: (i, 0)),
            pl.BlockSpec((tall, 2 * breadth), lambda i: (i, 0)),
            pl.BlockSpec((tall, 1), lambda i: (i, 0)),
        ],
        6 * rows * depth * breadth,
        waits,
    )


def back_matmul(jobs, waits=()):
    rows, breadth = jobs[0][0][0][0].shape[0], jobs[0][0][0][1].shape[0]
    tile = 256
    ins, specs, flops = [], [], 0
    for products, total, dtype in jobs:
        for rows_in, weight, column in products:
            depth = rows_in.shape[1]
            if depth % 128 and weight.shape[1] != depth:
                weight = weight[:, column * depth : (column + 1) * depth]
                column = 0
            ins += [rows_in, weight]
            specs += [
                pl.BlockSpec((rows, depth), lambda j: (0, 0)),
                pl.BlockSpec((tile, depth), lambda j, column=column: (j, column)),
            ]
            flops += 2 * rows * depth * breadth
        if total is not None:
            ins.append(total)
            specs.append(pl.BlockSpec((rows, tile), lambda j: (0, j)))

    def kernel(*refs):
        used = 0
        for out, (products, total, dtype) in enumerate(jobs):
            value = None
            for _ in products:
                part = right_product(refs[used][...], refs[used + 1][...])
                value = part if value is None else value + part
                used += 2
            if total is not None:
                value = value + wide(refs[used][...])
                used += 1
            refs[len(ins) + out][...] = value.astype(dtype)

    return own_call(
        kernel,
        "back_matmul",
        (breadth // tile,),
        ins,
        specs,
        [jax.ShapeDtypeStruct((rows, breadth), dtype) for products, total, dtype in jobs],
        [pl.BlockSpec((rows, tile), lambda j: (0, j))] * len(jobs),
        flops,
        waits,
    )


def route_product(d_route, route_mat):
    coarse = low(d_route)
    fine = low(d_route - wide(coarse))
    both = low(jnp.concatenate([route_mat, route_mat], axis=1))
    return (jnp.concatenate([coarse, fine], axis=1), both, 0)


def grad_matmul(pairs, waits=(), core=None, add=None):
    blocks = lax.axis_size("fsdp")
    depth = pairs[0][0][0].shape[1]
    widths = [rights[0].shape[1] for lefts, rights in pairs]
    total, block = sum(widths), depth // blocks
    step, first = (1, 0) if core is None else (2, core)
    blocks //= step
    ins, specs, flops = [], [], 0
    for lefts, rights in pairs:
        for left, right in zip(lefts, rights):
            ins += [left, right]
            specs += [
                pl.BlockSpec((left.shape[0], block), lambda j, first_ref: (0, step * j + first_ref[0])),
                pl.BlockSpec(right.shape, lambda j, first_ref: (0, 0)),
            ]
            flops += 2 * left.shape[0] * depth // step * right.shape[1]
    if add is not None:
        ins.append(add)
        specs.append(pl.BlockSpec((block, total), lambda j, first_ref: (j, 0)))

    def kernel(*refs):
        start, used = 0, 0
        for (lefts, rights), width in zip(pairs, widths):
            value = None
            for _ in lefts:
                part = lax.dot_general(
                    refs[used][...],
                    refs[used + 1][...],
                    (((0,), (0,)), ((), ())),
                    preferred_element_type=jnp.float32,
                )
                value = part if value is None else value + part
                used += 2
            if add is not None:
                value = value + wide(refs[-2][:, start : start + width])
            refs[-1][:, start : start + width] = low(value)
            start += width

    return own_call(
        kernel,
        "grad_matmul",
        (blocks,),
        ins,
        specs,
        [jax.ShapeDtypeStruct((blocks * block, total), jnp.bfloat16)],
        [pl.BlockSpec((block, total), lambda j, first_ref: (j, 0))],
        flops,
        waits,
        jnp.asarray(first, jnp.int32).reshape(1),
    )[0]


def split_matmul(rows_in, gain, weight, bias, cos_table, sin_table, waits=()):
    rows, depth = rows_in.shape
    breadth = bias.shape[0]
    tile = 256
    turned = breadth * 2 // 3 // tile
    tall = min(rows, 256)

    def kernel(rows_ref, gain_ref, weight_ref, bias_ref, cos_ref, sin_ref, normed_ref, out_ref):
        @pl.when(pl.program_id(0) == 0)
        def _():
            for start in range(0, rows, tall):
                some = slice(start, start + tall)
                values = wide(rows_ref[some, :])
                normed_ref[some, :] = low(values * rms_scale(values) * gain_ref[...])

        value = jnp.dot(normed_ref[...], weight_ref[...], preferred_element_type=jnp.float32)
        value = value + bias_ref[...]

        @pl.when(pl.program_id(0) < turned)
        def _():
            for start in range(0, tile, HEAD_DIM):
                head = value[:, start : start + HEAD_DIM]
                head = head * cos_ref[...] + pltpu.roll(head, HEAD_DIM // 2, 1) * sin_ref[...]
                out_ref[:, start : start + HEAD_DIM] = low(head)

        @pl.when(pl.program_id(0) >= turned)
        def _():
            out_ref[...] = low(value)

    whole = pl.BlockSpec((rows, depth), lambda j: (0, 0))
    table = pl.BlockSpec((rows, HEAD_DIM), lambda j: (0, 0))
    return own_call(
        kernel,
        "split_matmul",
        (breadth // tile,),
        [rows_in, gain.reshape(1, depth), weight, bias.reshape(1, breadth), cos_table, sin_table],
        [
            whole,
            pl.BlockSpec((1, depth), lambda j: (0, 0)),
            pl.BlockSpec((depth, tile), lambda j: (0, j)),
            pl.BlockSpec((1, tile), lambda j: (0, j)),
            table,
            table,
        ],
        [
            jax.ShapeDtypeStruct((rows, depth), jnp.bfloat16),
            jax.ShapeDtypeStruct((rows, breadth), jnp.bfloat16),
        ],
        [whole, pl.BlockSpec((rows, tile), lambda j: (0, j))],
        2 * rows * depth * breadth,
        waits,
    )


def head_specs(rows, heads):
    return [
        pl.BlockSpec((rows, HEAD_DIM), lambda h, part=part: (0, part * heads + h))
        for part in range(3)
    ]


def attend(split, places, heads, waits=()):
    rows = split.shape[0]
    tall = min(rows, 256)
    scale = HEAD_DIM ** (-0.5)

    def kernel(query_ref, key_ref, value_ref, down_ref, across_ref, out_ref, log_ref):
        for start in range(0, rows, tall):
            some = slice(start, start + tall)
            scores = right_product(query_ref[some, :], key_ref[...]) * scale
            scores = jnp.where(across_ref[...] <= down_ref[some, :], scores, -1e30)
            top = jnp.max(scores, axis=1, keepdims=True)
            exponent = jnp.exp(scores - top)
            total = jnp.sum(exponent, axis=1, keepdims=True)
            prob = low(exponent * (1.0 / total))
            out_ref[some, :] = low(
                jnp.dot(prob, value_ref[...], preferred_element_type=jnp.float32)
            )
            log_ref[some, :] = top + jnp.log(total)

    return own_call(
        kernel,
        "attend",
        (heads,),
        [split, split, split, places.reshape(rows, 1), places.reshape(1, rows)],
        head_specs(rows, heads)
        + [
            pl.BlockSpec((rows, 1), lambda h: (0, 0)),
            pl.BlockSpec((1, rows), lambda h: (0, 0)),
        ],
        [
            jax.ShapeDtypeStruct((rows, heads * HEAD_DIM), jnp.bfloat16),
            jax.ShapeDtypeStruct((heads, rows, 1), jnp.float32),
        ],
        [
            pl.BlockSpec((rows, HEAD_DIM), lambda h: (0, h)),
            pl.BlockSpec((None, rows, 1), lambda h: (h, 0, 0)),
        ],
        4 * rows * rows * heads * HEAD_DIM,
        waits,
    )


def attend_back(split, places, log_total, d_vec, cos_table, sin_table, heads, waits=()):
    rows = split.shape[0]
    tall = min(rows, 256)
    scale = HEAD_DIM ** (-0.5)

    def kernel(query_ref, key_ref, value_ref, down_ref, across_ref, log_ref, grad_ref, cos_ref, sin_ref, out_ref):
        first = pl.multiple_of(pl.program_id(0) * HEAD_DIM, HEAD_DIM)
        d_key = jnp.zeros((rows, HEAD_DIM), jnp.float32)
        d_value = jnp.zeros((rows, HEAD_DIM), jnp.float32)

        def unturned(grad, some):
            return low(
                grad * cos_ref[some, :]
                - pltpu.roll(grad, HEAD_DIM // 2, 1) * sin_ref[some, :]
            )

        def columns(part):
            return pl.ds(first + part * heads * HEAD_DIM, HEAD_DIM)

        for start in range(0, rows, tall):
            some = slice(start, start + tall)
            query, grad = query_ref[some, :], grad_ref[some, :]
            scores = right_product(query, key_ref[...]) * scale
            prob = jnp.where(
                across_ref[...] <= down_ref[some, :], jnp.exp(scores - log_ref[some, :]), 0.0
            )
            d_prob = right_product(grad, value_ref[...])
            inner = jnp.sum(prob * d_prob, axis=1, keepdims=True)
            d_score = low(prob * (d_prob - inner) * scale)
            across = (((0,), (0,)), ((), ()))
            d_value = d_value + lax.dot_general(
                low(prob), grad, across, preferred_element_type=jnp.float32
            )
            d_key = d_key + lax.dot_general(
                d_score, query, across, preferred_element_type=jnp.float32
            )
            d_query = jnp.dot(d_score, key_ref[...], preferred_element_type=jnp.float32)
            out_ref[some, columns(0)] = unturned(d_query, some)
        out_ref[:, columns(1)] = unturned(d_key, slice(0, rows))
        out_ref[:, columns(2)] = low(d_value)

    table = pl.BlockSpec((rows, HEAD_DIM), lambda h: (0, 0))
    return own_call(
        kernel,
        "attend_back",
        (heads,),
        [split, split, split, places.reshape(rows, 1), places.reshape(1, rows), log_total, d_vec]
        + [cos_table, sin_table],
        head_specs(rows, heads)
        + [
            pl.BlockSpec((rows, 1), lambda h: (0, 0)),
            pl.BlockSpec((1, rows), lambda h: (0, 0)),
            pl.BlockSpec((None, rows, 1), lambda h: (h, 0, 0)),
            pl.BlockSpec((rows, HEAD_DIM), lambda h: (0, h)),
            table,
            table,
        ],
        [jax.ShapeDtypeStruct((rows, 3 * heads * HEAD_DIM), jnp.bfloat16)],
        [pl.BlockSpec((rows, 3 * heads * HEAD_DIM), lambda h: (0, 0))],
        10 * rows * rows * heads * HEAD_DIM,
        waits,
    )[0]


def place_grads(spread, slot, slots, totals, waits=()):
    size, rows = len(spread[0][0]), spread[0][0][0].shape[0]
    units = sum([sum(parts) for pieces, parts in spread])
    if units % 128:
        ordered = by_rank(spread[0][0])
        sides = [
            jnp.stack([piece[:, k * units : (k + 1) * units] for piece in ordered], axis=1)
            for k in range(3)
        ]
        into = jnp.stack(sides[:2], axis=1).reshape(rows, 2 * size * units)
        return wide(into), wide(sides[2].reshape(rows, size * units)), spread[0][0][0]
    tall = min(rows, 64)
    columns = 2 if slot is None else 1
    pieces = [held[k] for k in range(size) for held, parts in spread]
    onto = [] if totals is None else list(totals[:2])
    rest = list(waits) + onto
    steps = rows // tall

    def kernel(*refs):
        in_ref, out_ref, mark_ref = refs[-3:]
        mark_ref[...] = jnp.zeros_like(mark_ref)
        for k in range(size):

            @pl.when(pl.program_id(0) == k)
            def _():
                used = refs[k * len(spread) : (k + 1) * len(spread)]
                place = 0
                for (held, parts), ref in zip(spread, used):
                    start = 0
                    for part in parts:
                        gate = ref[:, start : start + part]
                        up = ref[:, start + part : start + 2 * part]
                        if slot is None:
                            here = pl.program_id(2) == 0
                            in_ref[:, place : place + part] = wide(jnp.where(here, gate, up))
                        else:
                            in_ref[:, place : place + part] = wide(gate)
                            in_ref[:, units + place : units + place + part] = wide(up)
                        out_ref[:, place : place + part] = wide(
                            ref[:, start + 2 * part : start + 3 * part]
                        )
                        place += part
                        start += 3 * part

    def piece_spec(k, parts):
        def piece_map(step, row, column, rank_ref):
            return (jnp.where(step == k, row, jnp.where(step < k, 0, steps - 1)), 0)

        return pl.BlockSpec((tall, 3 * sum(parts)), piece_map)

    if slot is None:
        shapes = [(rows, 2 * size * units), (rows, size * units)]
        out_specs = [
            pl.BlockSpec(
                (tall, units),
                lambda k, row, column, rank_ref: (row, column * size + (rank_ref[0] ^ k)),
            ),
            pl.BlockSpec((tall, units), lambda k, row, column, rank_ref: (row, rank_ref[0] ^ k)),
        ]
    else:
        shapes = [(size * slots, rows, 2 * units), (size * slots, rows, units)]
        out_specs = [
            pl.BlockSpec(
                (None, tall, shape[2]),
                lambda k, row, column, rank_ref: ((rank_ref[0] ^ k) * slots + slot, row, 0),
            )
            for shape in shapes
        ]
    first = 1 + len(pieces) + len(waits)
    return own_call(
        kernel,
        "place_grads",
        (size, steps, columns),
        pieces,
        [piece_spec(k, parts) for k in range(size) for held, parts in spread],
        [jax.ShapeDtypeStruct(shape, jnp.float32) for shape in [*shapes, (8, 128)]],
        out_specs + [pl.BlockSpec((8, 128), lambda k, row, column, rank_ref: (0, 0))],
        0,
        rest,
        lax.axis_index("ctx").reshape(1),
        aliases={first: 0, first + 1: 1} if onto else {},
    )


def place_cols(pieces, parts, waits=()):
    size, rows = len(pieces), pieces[0].shape[0]
    breadth = pieces[0].shape[1] // parts
    if breadth % 128:
        ordered = [piece.reshape(rows, parts, breadth) for piece in by_rank(pieces)]
        return wide(jnp.stack(ordered, axis=2).reshape(rows, parts * size * breadth))

    def kernel(*refs):
        for k, ref in enumerate(refs[:-1]):

            @pl.when(pl.program_id(0) == k)
            def _():
                refs[-1][...] = wide(ref[...])

    def piece_spec(own):
        def piece_map(k, part, rank_ref):
            return (0, jnp.where(k == own, part, jnp.where(k < own, 0, parts - 1)))

        return pl.BlockSpec((rows, breadth), piece_map)

    return own_call(
        kernel,
        "place_cols",
        (size, parts),
        pieces,
        [piece_spec(own) for own in range(size)],
        [jax.ShapeDtypeStruct((rows, parts * size * breadth), jnp.float32)],
        [
            pl.BlockSpec(
                (rows, breadth), lambda k, part, rank_ref: (0, part * size + (rank_ref[0] ^ k))
            )
        ],
        0,
        waits,
        lax.axis_index("ctx").reshape(1),
    )[0]

def per_device(
    tokens,
    routes,
    block_ids,
    attn_gain,
    w_attn_in,
    b_qkv,
    w_attn_out,
    ffn_gain,
    router,
    shared_gate,
    w_sh_in,
    w_sh_out,
    w_exp_in,
    w_exp_out,
    cotangent,
):
    ctx_size = lax.axis_size("ctx")
    fsdp_size = lax.axis_size("fsdp")
    ctx_rank = lax.axis_index("ctx")
    fsdp_rank = lax.axis_index("fsdp")
    tok_rows = tokens.shape[0]
    block_len = tok_rows // 2
    seq_len = tok_rows * ctx_size
    heads_own = HEADS // ctx_size
    att_cols = heads_own * HEAD_DIM
    sh_cols = FS // ctx_size
    experts_own = EXPERTS // ctx_size

    def own_cols(array, start, breadth):
        return lax.dynamic_slice_in_dim(array, start + ctx_rank * breadth, breadth, axis=1)

    def gather_fsdp(array):
        return lax.all_gather(array, "fsdp", axis=0, tiled=True)

    def scatter_fsdp(array):
        return lax.psum_scatter(
            array.astype(jnp.bfloat16), "fsdp", scatter_dimension=0, tiled=True
        )

    def token_pieces(array):
        return [array[k * tok_rows : (k + 1) * tok_rows] for k in range(ctx_size)]

    tokens_all = jnp.concatenate(peer_gather(tokens), axis=0)
    quarter = D // ctx_size
    w_out_own = gather_fsdp(own_cols(w_attn_out, 0, quarter))
    w_out_pieces = peer_gather(w_out_own)
    rows = attn_gain.shape[0]
    smalls = jnp.concatenate(
        [jnp.stack([attn_gain, ffn_gain, shared_gate], axis=1), router, b_qkv.reshape(3, rows).T],
        axis=1,
    )
    smalls = jnp.pad(smalls, ((0, 0), (0, 128 - smalls.shape[1])))
    w_in_slab = jnp.concatenate(
        [own_cols(w_attn_in, part * D, att_cols) for part in range(3)] + [smalls], axis=1
    )
    w_in_own = gather_fsdp(after(w_in_slab, [w_out_own]))
    smalls_all = w_in_own[:, 3 * att_cols :]
    gain_one, gain_two, gate_vec = [wide(smalls_all[:, k]) for k in range(3)]
    router_wide = wide(smalls_all[:, 3 : 3 + EXPERTS])
    bias_full = smalls_all[:, 3 + EXPERTS : 6 + EXPERTS].reshape(fsdp_size, rows, 3)
    bias_full = jnp.transpose(bias_full, (0, 2, 1)).reshape(3, D)
    bias_own = wide(own_cols(bias_full, 0, att_cols)).reshape(3 * att_cols)

    core = fsdp_rank % 2
    lines = [[rank for rank in range(fsdp_size) if rank % 2 == spot] for spot in range(2)]

    def scatter_line(grad):
        return lax.psum_scatter(
            grad, "fsdp", scatter_dimension=0, axis_index_groups=lines, tiled=True
        )

    slabs = [
        [own_cols(w_sh_in, part * FS, sh_cols) for part in range(2)]
        + [own_cols(w_sh_out, 0, sh_cols)]
    ]
    for own in range(experts_own):
        expert = ctx_rank * experts_own + own
        slabs.append([w_exp_in[expert, :, :FE], w_exp_in[expert, :, FE:], w_exp_out[expert]])
    slabs = [jnp.concatenate(sides, axis=1) for sides in slabs]

    inputs = wide(tokens)
    scale_one = rms_scale(inputs)
    unit_one = inputs * scale_one
    ranks = ctx_rank ^ jnp.arange(ctx_size, dtype=jnp.int32)
    places = block_places(block_ids.reshape(ctx_size, 2)[ranks].reshape(-1), block_len)
    cos_table, sin_table = rotary_tables(places)
    half = HEAD_DIM // 2
    sin_table = jnp.concatenate([-sin_table[:, :half], sin_table[:, half:]], axis=1)
    normed_all, split = split_matmul(
        tokens_all, gain_one, w_in_own, bias_own, cos_table, sin_table
    )
    attended, log_total = attend(split, places, heads_own, w_out_pieces)
    head_pieces = token_pieces(attended)
    head_pieces = head_pieces[:1] + [
        to_peer(head_pieces[bits], bits) for bits in range(1, ctx_size)
    ]
    attn_vec = jnp.concatenate(by_rank(head_pieces), axis=1)
    attn_out = [
        jnp.dot(attn_vec, piece, preferred_element_type=jnp.float32) for piece in w_out_pieces
    ]
    residual = inputs + jnp.concatenate(by_rank(attn_out), axis=1)

    scale_two = rms_scale(residual)
    unit_two = residual * scale_two
    cots = [jnp.concatenate(peer_gather(after(cotangent, [split])), axis=0)]
    hidden_in = low(unit_two * gain_two)
    hidden = [jnp.concatenate(peer_gather(hidden_in), axis=0)]
    route_mat = jnp.concatenate([router_wide, gate_vec[:, None]], axis=1)
    expert_ids = jnp.arange(EXPERTS, dtype=jnp.int32)
    logits = jnp.dot(
        wide(hidden[0]), route_mat, precision=highest, preferred_element_type=jnp.float32
    )
    route_probs = jax.nn.softmax(logits[:, :EXPERTS], axis=1)
    shared_prob = jax.nn.sigmoid(logits[:, EXPERTS:])
    routes_all = jnp.concatenate(
        [routes] + [to_peer(routes, bits) for bits in range(1, ctx_size)], axis=0
    )
    chosen = wide(jnp.any(routes_all[:, :, None] == expert_ids[None, None, :], axis=1))

    weights = [
        gather_fsdp(after(slab, [wait]))
        for slab, wait in zip(slabs, (w_in_own, split, attended))
    ]
    d_probs = jnp.zeros((seq_len, EXPERTS), jnp.float32)
    sums, waits, grads = [None, None], [], []
    for index, weight in enumerate(weights):
        own = index - 1
        if own < 0:
            factor = shared_prob
        else:
            picked = (expert_ids == ctx_rank * experts_own + own)[None, :]
            factor = jnp.sum(
                jnp.where(picked, route_probs * chosen, 0.0), axis=1, keepdims=True
            )
        scaled_out, d_act, d_factor = unit_backward(hidden[0], cots[0], weight, factor, waits)
        if own < 0:
            d_gate_logit = d_factor * (shared_prob * (1.0 - shared_prob))
        else:
            d_probs = d_probs + jnp.where(picked, chosen * d_factor, 0.0)
        waits = [scaled_out]
        products, outward = [(d_act, weight, 0)], [(scaled_out, weight, 2)]
        if index == len(weights) - 1:
            d_logits = route_probs * (
                d_probs - jnp.sum(route_probs * d_probs, axis=1, keepdims=True)
            )
            d_route = jnp.concatenate([d_logits, d_gate_logit], axis=1)
            products.append(route_product(d_route, route_mat))
            d_hidden_sum = back_matmul([(products, sums[0], jnp.bfloat16)], waits)[0]
            waits = [d_hidden_sum]
        pairs = [(hidden, [d_act]), (cots, [scaled_out])]
        given = grad_matmul(pairs, waits, 1 - core)
        waits = [given]
        if index < len(weights) - 1:
            sums = back_matmul(
                [(products, sums[0], jnp.float32), (outward, sums[1], jnp.float32)], waits
            )
            waits = [sums[0]]
        else:
            block_sum = back_matmul([(outward, sums[1], jnp.bfloat16)], waits)[0]
            waits = [block_sum]
        grads.append(grad_matmul(pairs, waits, core, to_mate(given, 1)))
        waits = [grads[-1]]
    shards = [scatter_line(grad) for grad in grads]
    d_route_mat = lax.dot_general(
        d_route,
        wide(hidden[0]),
        (((0,), (0,)), ((), ())),
        precision=highest,
        preferred_element_type=jnp.float32,
    )
    d_hidden = peer_scatter(token_pieces(d_hidden_sum))
    cot_wide = wide(cotangent)
    d_gain_two = jnp.sum(d_hidden * unit_two, axis=0)
    d_resid = cot_wide + rms_back(d_hidden, unit_two, scale_two, gain_two)
    d_attn = low(d_resid)
    d_attn_pieces = by_rank(
        [d_attn[:, k * quarter : (k + 1) * quarter] for k in range(ctx_size)]
    )
    products = [(piece, weight, 0) for piece, weight in zip(d_attn_pieces, w_out_pieces)]
    d_vec_own = back_matmul([(products, None, jnp.bfloat16)], waits)[0]
    d_vec_pieces = by_rank(
        [d_vec_own[:, k * att_cols : (k + 1) * att_cols] for k in range(ctx_size)]
    )
    d_vec = jnp.concatenate(
        d_vec_pieces[:1] + [to_peer(d_vec_pieces[bits], bits) for bits in range(1, ctx_size)],
        axis=0,
    )
    grad_w_out = grad_matmul(
        [([attn_vec], [jnp.concatenate(d_attn_pieces, axis=1)])], [d_vec_own]
    )
    grad_w_out = peer_scatter(
        [grad_w_out[:, k * quarter : (k + 1) * quarter] for k in range(ctx_size)]
    )
    grad_w_out = scatter_fsdp(grad_w_out)
    d_mixed = attend_back(split, places, log_total, d_vec, cos_table, sin_table, heads_own)
    given = grad_matmul([([normed_all], [d_mixed])], (), 1 - core)
    d_bias = jnp.sum(wide(d_mixed), axis=0)
    d_normed_part = back_matmul(
        [([(d_mixed, w_in_own, 0)], None, jnp.bfloat16)], [given]
    )[0]
    grad_w_in = scatter_line(
        grad_matmul([([normed_all], [d_mixed])], [d_normed_part], core, to_mate(given, 1))
    )
    d_normed = peer_scatter(token_pieces(d_normed_part))
    block_out = low(residual + peer_scatter(token_pieces(after(block_sum, [d_mixed]))))
    units, totals, waits = [sh_cols] + [FE] * experts_own, None, [d_normed_part]
    for own, shard in zip(range(-1, experts_own), shards):
        spread = [(peer_gather(after(shard, waits)), units[:1] if own < 0 else units[1:2])]
        if own < 0:
            shared_totals = place_grads(spread, None, 1, None, waits)
            waits = [shared_totals[2]]
        else:
            totals = place_grads(spread, own, experts_own, totals, waits)
    wide_all = wide(tokens_all)
    d_gain_one = jnp.sum(wide(d_normed_part) * (wide_all * rms_scale(wide_all)), axis=0)
    d_tokens = d_resid + rms_back(d_normed, unit_one, scale_one, gain_one)

    bias_spread = lax.dynamic_update_slice(
        jnp.zeros((3, D), jnp.float32), d_bias.reshape(3, att_cols), (0, ctx_rank * att_cols)
    )
    early_grads = total_sum(jnp.concatenate([d_route_mat.reshape(-1), d_gain_two]))
    late_grads = total_sum(jnp.concatenate([bias_spread.reshape(-1), d_gain_one]))

    def own_part(vector):
        size = vector.shape[0] // fsdp_size
        return lax.dynamic_slice_in_dim(vector, fsdp_rank * size, size)

    route_total = early_grads[: (EXPERTS + 1) * D].reshape(EXPERTS + 1, D)
    route_part = lax.dynamic_slice_in_dim(route_total, fsdp_rank * rows, rows, axis=1)
    return (
        block_out,
        d_tokens,
        own_part(late_grads[3 * D :]),
        place_cols(peer_gather(after(grad_w_in, [late_grads, early_grads])), 3, [totals[1]]),
        own_part(late_grads[: 3 * D]),
        wide(jnp.concatenate(by_rank(peer_gather(grad_w_out)), axis=1)),
        own_part(early_grads[(EXPERTS + 1) * D :]),
        route_part[:EXPERTS].T,
        route_part[EXPERTS],
        *shared_totals[:2],
        *totals[:2],
    )


def solution(mesh):
    return jax.shard_map(
        per_device,
        mesh=mesh,
        in_specs=(
            P(("ctx", "fsdp"), None),
            P(("ctx", "fsdp"), None),
            P(),
            P("fsdp"),
            P("fsdp", None),
            P("fsdp"),
            P("fsdp", None),
            P("fsdp"),
            P("fsdp", None),
            P("fsdp"),
            P("fsdp", None),
            P("fsdp", None),
            P(None, "fsdp", None),
            P(None, "fsdp", None),
            P(("ctx", "fsdp"), None),
        ),
        out_specs=(
            P(("ctx", "fsdp"), None),
            P(("ctx", "fsdp"), None),
            P("fsdp"),
            P("fsdp", None),
            P("fsdp"),
            P("fsdp", None),
            P("fsdp"),
            P("fsdp", None),
            P("fsdp"),
            P("fsdp", None),
            P("fsdp", None),
            P(None, "fsdp", None),
            P(None, "fsdp", None),
        ),
        check_vma=False,
    )
```
